32 devices in a mesh: dp: 2 (over x), fsdp: 16 (over z, y, core).
Axes of the slice: x: 2, y: 2, z: 4, core: 2. Of those that a mesh axis runs over, the one named last changes fastest.
Arguments:
- embeddings: bfloat16 [32768, 512], P(('dp', 'fsdp')), may hold values from -6 to 6
- conv_weight: bfloat16 [2, 2359296], P(None, ('dp', 'fsdp')), may hold values from -0.09375 to 0.09375
- inner_weight: bfloat16 [2, 1048576], P(None, ('dp', 'fsdp')), may hold values from -0.25 to 0.25
- outer_weight: bfloat16 [2, 1048576], P(None, ('dp', 'fsdp')), may hold values from -0.125 to 0.125
- vectors: bfloat16 [2, 3584], P(None, ('dp', 'fsdp')), may hold values from -2 to 3
- cotangent: bfloat16 [32768, 512], P(('dp', 'fsdp')), may hold values from -6 to 6
- row_mask: int32 [32768], P(('dp', 'fsdp')), may hold values 0 or 1
Outputs:
- output: bfloat16 [32768, 512], P(('dp', 'fsdp'))
- grad_embeddings: bfloat16 [32768, 512], P(('dp', 'fsdp'))
- grad_conv: float32 [2, 2359296], P(None, ('dp', 'fsdp'))
- grad_inner: float32 [2, 1048576], P(None, ('dp', 'fsdp'))
- grad_outer: float32 [2, 1048576], P(None, ('dp', 'fsdp'))
- grad_vectors: float32 [2, 3584], P(None, ('dp', 'fsdp'))
The draws below stay inside these ranges and needn't reach their ends.
All inputs are finite; a program needn't handle non-finite values. No bound on the sum of `row_mask` on one device may be relied on, other than what follows from the above.
Results may differ from the reference program's by a relative error of at most 0.013.
Values may be sent and summed in bfloat16 or wider, within the bound.
A program may use at most 192 MiB of HBM per device.

```python
import jax
import jax.numpy as jnp
from jax import lax

D = 512
FF = 2048
KS = 9
L = 512
WIN_DEV = 2
TOKENS = 32768


def draw_vectors(key, part):
    key = jax.random.fold_in(key, 7)
    length = 3 * D + FF
    columns = jnp.arange(length)
    is_gain = (columns >= D) & (columns < 3 * D)
    noise = jnp.clip(0.5 * jax.random.normal(key, (2, length), jnp.float32), -1.9, 1.9)
    values = jnp.where(is_gain[None, :], 1.0 + noise, noise)
    return values.astype(jnp.bfloat16)


def plant(values, stream_key, least, largest):
    index_at = [jax.random.randint(jax.random.fold_in(stream_key, axis), (), 0, length) for axis, length in enumerate(values.shape)]
    main_axis = values.shape.index(max(values.shape))
    beside = index_at[:main_axis] + [(index_at[main_axis] + 1) % values.shape[main_axis]] + index_at[main_axis + 1:]
    return values.at[tuple(index_at)].set(least).at[tuple(beside)].set(largest)


def levels(rng, shape, split, smallest, top_value):
    gain, own = 1.0, jax.random.fold_in(rng, 6)
    for dim, parts in split:
        heights = jnp.exp(jax.random.uniform(jax.random.fold_in(own, dim), (parts,), jnp.float32, smallest / len(split), top_value / len(split)))
        gain = gain * jnp.repeat(heights, shape[dim] // parts).reshape([-1 if axis == dim else 1 for axis in range(len(shape))])
    return gain


def scatter_about(key, shape, deviation, bound, cuts=(), dtype=jnp.bfloat16):
    values = deviation * jax.random.normal(key, shape, jnp.float32)
    if cuts:
        values = values * levels(key, shape, cuts, -0.22, 0.18)
    return jnp.clip(values, -bound, bound).astype(dtype)


def setup_inputs(seed: int = 0) -> dict:
    seeds = jax.random.split(jax.random.key(seed), 8)
    embeddings = scatter_about(seeds[0], (TOKENS, D), 1.0, 6.0, ((0, 32),))
    conv_weight = scatter_about(seeds[1], (2, KS * D * D), (KS * D) ** -0.5, 0.09375, ((1, 32),))
    inner_weight = scatter_about(seeds[2], (2, D * FF), D ** -0.5, 0.25, ((1, 32),))
    outer_weight = scatter_about(seeds[3], (2, FF * D), FF ** -0.5, 0.125, ((1, 32),))
    vectors = draw_vectors(jax.random.fold_in(seeds[7], 71), 0)
    cotangent = scatter_about(seeds[5], (TOKENS, D), 1.0, 6.0, ((0, 32),))
    row_mask = plant((jax.random.randint(seeds[6], (TOKENS,), 0, 100) < 15).astype(jnp.int32), jax.random.fold_in(seeds[6], 1), 0, 1)
    return dict(embeddings=embeddings, conv_weight=conv_weight, inner_weight=inner_weight, outer_weight=outer_weight, vectors=vectors, cotangent=cotangent, row_mask=row_mask)


@jax.custom_vjp
def low(v):
    return lax.optimization_barrier(v.astype(jnp.bfloat16)).astype(jnp.float32)

@jax.custom_vjp
def low_back(v):
    return v

def low_keep(v):
    return (low(v), None)

def low_pass(kept, grad):
    return (grad,)

def back_keep(v):
    return (v, None)

def back_low(kept, grad):
    return (low(grad),)
low.defvjp(low_keep, low_pass)
low_back.defvjp(back_keep, back_low)

def normalize(values):
    centered = values - lax.optimization_barrier(jnp.mean(values, axis=-1, keepdims=True))
    return centered * lax.rsqrt(lax.optimization_barrier(jnp.mean(centered * centered, axis=-1, keepdims=True)) + 1e-05)

def convolve(framed, kernel, dilation):
    margin = KS // 2 * dilation
    padded = jnp.pad(framed, ((0, 0), (margin, margin), (0, 0)))
    total = jnp.zeros(framed.shape, jnp.float32)
    for tap_id in range(KS):
        shifted = padded[:, tap_id * dilation:tap_id * dilation + L]
        total = total + jnp.einsum('wld,de->wle', shifted, kernel[tap_id], precision=lax.Precision.HIGHEST)
    return total

def block(stream, conv_flat, inner_flat, outer_flat, vector, dilation):
    kernel = conv_flat.reshape(KS, D, D)
    inner = inner_flat.reshape(D, FF)
    outer = outer_flat.reshape(FF, D)
    conv_bias = vector[:D]
    gain_conv = vector[D:2 * D]
    gain_ffn = vector[2 * D:3 * D]
    bias_ffn = vector[3 * D:]
    stream_low = low(stream)
    pre_conv = low_back(convolve(stream_low, kernel, dilation) + conv_bias)
    mixed = stream + gain_conv * normalize(jax.nn.gelu(pre_conv))
    mixed_low = low(mixed)
    pre_ffn = low_back(jnp.einsum('wld,df->wlf', mixed_low, inner, precision=lax.Precision.HIGHEST) + bias_ffn)
    hidden_low = low(jax.nn.gelu(pre_ffn))
    branch = low_back(jnp.einsum('wlf,fd->wld', hidden_low, outer, precision=lax.Precision.HIGHEST))
    return mixed + gain_ffn * normalize(branch)

def forward(framed, conv_all, inner_all, outer_all, vector_all):
    stream = framed
    for block_id, dilation in ((0, 2), (1, 16)):
        stream = block(stream, conv_all[block_id], inner_all[block_id], outer_all[block_id], vector_all[block_id], dilation)
    return stream

def reference(embeddings, conv_weight, inner_weight, outer_weight, vectors, cotangent, row_mask):
    params = tuple((weight.astype(jnp.float32) for weight in (conv_weight, inner_weight, outer_weight, vectors)))
    groups = TOKENS // (WIN_DEV * L)
    framed = embeddings.astype(jnp.float32).reshape(groups, WIN_DEV, L, D)
    weighted = (cotangent.astype(jnp.float32) * row_mask.astype(jnp.float32)[:, None]).reshape(groups, WIN_DEV, L, D)

    def one_group(totals, member):
        group_in, group_cot = member
        result, pullback = jax.vjp(forward, group_in, *params)
        gradients = pullback(group_cot)
        totals = tuple((total + update for total, update in zip(totals, gradients[1:])))
        return (totals, (result, gradients[0]))
    zeros = tuple((jnp.zeros_like(weight) for weight in params))
    totals, (results, input_grads) = lax.scan(one_group, zeros, (framed, weighted))
    output = results.reshape(TOKENS, D).astype(jnp.bfloat16)
    grad_embeddings = input_grads.reshape(TOKENS, D).astype(jnp.bfloat16)
    return (output, grad_embeddings, totals[0], totals[1], totals[2], totals[3])
```

```python
import functools

import jax
import jax.numpy as jnp
from jax import lax
from jax.experimental import pallas as pl
from jax.experimental.pallas import tpu as pltpu
from jax.sharding import PartitionSpec as P

D = 512
FF = 2048
KS = 9
L = 512
NV = 3 * D + FF
DILATIONS = (2, 16)
MESH = pl.DeviceIdType.MESH
BF = jnp.bfloat16
F32 = jnp.float32
NX, NZ, NY = 2, 4, 2
NDEV = 32


def normalize(values):
    centered = values - jnp.mean(values, axis=-1, keepdims=True)
    return centered * lax.rsqrt(jnp.mean(centered * centered, axis=-1, keepdims=True) + 1e-05)


def conv_branch(values):
    return normalize(jax.nn.gelu(values))


def contract_rows(left, right):
    return lax.dot_general(left, right, (((0,), (0,)), ((), ())), preferred_element_type=F32)


def contract_cols(left, right):
    return lax.dot_general(left, right, (((1,), (1,)), ((), ())), preferred_element_type=F32)


def columns(stream_low, dilation):
    windows = stream_low.shape[0] // L
    framed = stream_low.reshape(windows, L, D)
    margin = KS // 2 * dilation
    padded = jnp.pad(framed, ((0, 0), (margin, margin), (0, 0)))
    stacked = jnp.concatenate(
        [padded[:, tap_id * dilation : tap_id * dilation + L] for tap_id in range(KS)], axis=2
    )
    return stacked.reshape(windows * L, KS * D)


def fold_back(grad_cols, dilation):
    windows = grad_cols.shape[0] // L
    framed = grad_cols.reshape(windows, L, KS, D)
    margin = KS // 2 * dilation
    total = jnp.zeros((windows, L + 2 * margin, D), F32)
    for tap_id in range(KS):
        before = tap_id * dilation
        total = total + jnp.pad(
            framed[:, :, tap_id], ((0, 0), (before, 2 * margin - before), (0, 0))
        )
    return total[:, margin : margin + L].reshape(windows * L, D)


def block_forward(stream, weights, dilation):
    conv_mat, inner_mat, outer_mat, vector = weights
    conv_bias = vector[:D]
    gain_conv = vector[D : 2 * D]
    gain_ffn = vector[2 * D : 3 * D]
    bias_ffn = vector[3 * D :]
    stream_low = stream.astype(BF)
    pre_conv = (
        jnp.dot(columns(stream_low, dilation), conv_mat, preferred_element_type=F32) + conv_bias
    )
    mixed = stream + gain_conv * conv_branch(pre_conv)
    mixed_low = mixed.astype(BF)
    pre_ffn = jnp.dot(mixed_low, inner_mat, preferred_element_type=F32) + bias_ffn
    hidden_low = jax.nn.gelu(pre_ffn).astype(BF)
    branch = jnp.dot(hidden_low, outer_mat, preferred_element_type=F32)
    result = mixed + gain_ffn * normalize(branch)
    return (result, (stream_low, pre_conv, mixed_low, pre_ffn, hidden_low, branch))


def block_backward(grad_out, saved, weights, dilation):
    conv_mat, inner_mat, outer_mat, vector = weights
    gain_conv = vector[D : 2 * D]
    gain_ffn = vector[2 * D : 3 * D]
    stream_low, pre_conv, mixed_low, pre_ffn, hidden_low, branch = saved
    normed_branch, branch_back = jax.vjp(normalize, branch)
    grad_gain_ffn = jnp.sum(grad_out * normed_branch, axis=0)
    grad_branch = branch_back(grad_out * gain_ffn)[0].astype(BF)
    grad_outer = contract_rows(hidden_low, grad_branch)
    grad_hidden = contract_cols(grad_branch, outer_mat)
    _, gelu_back = jax.vjp(jax.nn.gelu, pre_ffn)
    grad_pre_ffn = gelu_back(grad_hidden)[0].astype(BF)
    grad_bias_ffn = jnp.sum(grad_pre_ffn.astype(F32), axis=0)
    grad_inner = contract_rows(mixed_low, grad_pre_ffn)
    grad_mixed = grad_out + contract_cols(grad_pre_ffn, inner_mat)
    normed_conv, conv_back = jax.vjp(conv_branch, pre_conv)
    grad_gain_conv = jnp.sum(grad_mixed * normed_conv, axis=0)
    grad_pre_conv = conv_back(grad_mixed * gain_conv)[0].astype(BF)
    grad_conv_bias = jnp.sum(grad_pre_conv.astype(F32), axis=0)
    grad_kernel = contract_rows(columns(stream_low, dilation), grad_pre_conv)
    grad_stream = grad_mixed + fold_back(contract_cols(grad_pre_conv, conv_mat), dilation)
    vector_grad = jnp.concatenate([grad_conv_bias, grad_gain_conv, grad_gain_ffn, grad_bias_ffn])
    return (grad_stream, (grad_kernel, grad_inner, grad_outer, vector_grad))


def place():
    across = lax.axis_index("dp")
    index = lax.axis_index("fsdp")
    return across, index // (2 * NY), (index // 2) % NY, index % 2


def device(x, z, y, c):
    return (x, (z * NY + y) * 2 + c)


def shard(x, z, y, c):
    return x * (NZ * NY * 2) + (z * NY + y) * 2 + c


def meet(peers):
    barrier = pltpu.get_barrier_semaphore()
    for peer in peers:
        pl.semaphore_signal(barrier, inc=1, device_id=peer, device_id_type=MESH)
    pl.semaphore_wait(barrier, len(peers))


def neighbours(x, z, y, c):
    return [
        device(1 - x, z, y, c),
        device(x, z, 1 - y, c),
        device(x, z, y, 1 - c),
        device(x, (z + 1) % NZ, y, c),
        device(x, (z + 2) % NZ, y, c),
        device(x, (z + 3) % NZ, y, c),
    ]


def cut(rows, cols):
    if rows >= 32:
        first = (rows // 2 + 15) // 16 * 16
        return (0, first, 0, cols), (first, rows - first, 0, cols)
    if cols >= 256:
        return (0, rows, 0, cols // 2), (0, rows, cols // 2, cols // 2)
    return (0, rows, 0, cols), None


def gather_kernel(shapes, *refs):
    count = len(shapes)
    own_refs = refs[:count]
    full_refs = refs[count : 2 * count]
    own_sem, send_sem, recv_sem, half_sem = refs[2 * count :]
    x, z, y, c = place()
    meet(neighbours(x, z, y, c))
    to_x, to_y, to_c = device(1 - x, z, y, c), device(x, z, 1 - y, c), device(x, z, y, 1 - c)

    def rows_of(t, index, half=None):
        rows, cols = shapes[t]
        base = pl.multiple_of(index * rows, 16)
        if half is None:
            return full_refs[t].at[pl.ds(base, rows)]
        at, height, left, width = half
        base = pl.multiple_of(base + at, 16)
        if width == cols:
            return full_refs[t].at[pl.ds(base, height)]
        return full_refs[t].at[pl.ds(base, height), pl.ds(left, width)]

    def copy(t, index, kind, target, half=None, sem=None):
        part = rows_of(t, index, half)
        return pltpu.make_async_remote_copy(
            src_ref=part,
            dst_ref=part,
            send_sem=send_sem.at[t, kind],
            recv_sem=recv_sem.at[t, index] if sem is None else sem,
            device_id=target,
            device_id_type=MESH,
        )

    def arrive(t, index, half=None, sem=None):
        part = rows_of(t, index, half)
        pltpu.make_async_copy(part, part, recv_sem.at[t, index] if sem is None else sem).wait()

    def own(t):
        mine = shard(x, z, y, c)
        move = pltpu.make_async_copy(own_refs[t], rows_of(t, mine), own_sem.at[t])
        move.start()
        return move

    def along_z(t):
        mine = shard(x, z, y, c)
        for step in (1, 2, 3):
            copy(t, mine, 0, device(x, (z + step) % NZ, y, c)).start()
        spread(t, mine)

    def spread(t, index):
        copy(t, index, 1, to_x).start()
        copy(t, index, 2, to_y).start()
        copy(t, index, 3, to_c).start()

    def across(t):
        for step in (1, 2, 3):
            index = shard(x, (z + step) % NZ, y, c)
            arrive(t, index)
            spread(t, index)

    def corner(t):
        first, second = cut(*shapes[t])
        for step in range(NZ):
            level = (z + step) % NZ
            from_x = shard(1 - x, level, y, c)
            arrive(t, from_x)
            copy(t, from_x, 2, to_y, first).start()
            copy(t, from_x, 3, to_c).start()
            from_y = shard(x, level, 1 - y, c)
            arrive(t, from_y)
            if second is not None:
                copy(t, from_y, 1, to_x, second, half_sem.at[t, level]).start()
            copy(t, from_y, 3, to_c).start()

    def finish(t):
        first, second = cut(*shapes[t])
        for step in range(NZ):
            level = (z + step) % NZ
            far = shard(1 - x, level, 1 - y, c)
            arrive(t, far, first)
            if second is not None:
                arrive(t, far, second, half_sem.at[t, level])
            copy(t, far, 3, to_c).start()

    def settle(t):
        for ax in range(NX):
            for az in range(NZ):
                for ay in range(NY):
                    arrive(t, shard(ax, az, ay, 1 - c))

    def sent(t):
        rows, cols = shapes[t]
        first, second = cut(rows, cols)
        halves = [0 if half is None else half[1] * half[3] * NZ // cols for half in (second, first)]
        for kind, total in enumerate(
            (3 * rows, NZ * rows + halves[0], NZ * rows + halves[1], 16 * rows)
        ):
            part = full_refs[t].at[pl.ds(0, total)]
            pltpu.make_async_copy(part, part, send_sem.at[t, kind]).wait()

    moves = [own(t) for t in range(count)]
    moves[0].wait()
    along_z(0)
    for t in range(count):
        across(t)
        if t + 1 < count:
            moves[t + 1].wait()
            along_z(t + 1)
        corner(t)
        finish(t)
    for t in range(count):
        settle(t)
        sent(t)


def gather(shards):
    shapes = tuple(member.shape for member in shards)
    count = len(shapes)
    return pl.pallas_call(
        functools.partial(gather_kernel, shapes),
        out_shape=[jax.ShapeDtypeStruct((NDEV * r, w), BF) for r, w in shapes],
        in_specs=[pl.BlockSpec(memory_space=pl.ANY)] * count,
        out_specs=[pl.BlockSpec(memory_space=pl.ANY)] * count,
        scratch_shapes=[
            pltpu.SemaphoreType.DMA((count,)),
            pltpu.SemaphoreType.DMA((count, 4)),
            pltpu.SemaphoreType.DMA((count, NDEV)),
            pltpu.SemaphoreType.DMA((count, NZ)),
        ],
        compiler_params=pltpu.CompilerParams(collective_id=0, has_side_effects=True),
        name="gather",
    )(*shards)


def reduce_kernel(shapes, *refs):
    count = len(shapes)
    part_refs = refs[:count]
    out_refs = refs[count : 2 * count]
    scratch = refs[2 * count :]
    held, swap, first_in, second_in, from_x, from_y, total, from_z, result = (
        scratch[i * count : (i + 1) * count] for i in range(9)
    )
    local_sem, send_sem, recv_sem, out_sem = scratch[9 * count :]
    x, z, y, c = place()
    meet(neighbours(x, z, y, c))
    to_x, to_y, to_c = device(1 - x, z, y, c), device(x, z, 1 - y, c), device(x, z, y, 1 - c)

    def send(t, kind, src, dst, target):
        move = pltpu.make_async_remote_copy(
            src_ref=src,
            dst_ref=dst,
            send_sem=send_sem.at[t, kind],
            recv_sem=recv_sem.at[t, kind],
            device_id=target,
            device_id_type=MESH,
        )
        move.start()
        moves.append(move)
        return move

    moves = []
    live = {}

    def half_of(ref, half):
        at, height, left, width = half
        return ref.at[:, pl.ds(at, height), pl.ds(left, width)]

    def begin(t):
        live[t, "own"] = pltpu.make_async_copy(part_refs[t].at[:, c], held[t], local_sem.at[t])
        live[t, "own"].start()
        live[t, 0] = send(t, 0, part_refs[t].at[:, 1 - c], swap[t], to_c)

    def column(t, ax, ay):
        rows, cols = shapes[t]
        return held[t].reshape(NX, NZ, NY, rows, cols).at[ax, :, ay]

    def pair(t):
        live[t, "own"].wait()
        live[t, 0].wait_recv()

        @pl.loop(0, 16)
        def _(i):
            held[t][i] = (held[t][i].astype(F32) + swap[t][i].astype(F32)).astype(BF)

        first, second = cut(*shapes[t])
        far = column(t, 1 - x, 1 - y)
        live[t, 1] = send(t, 1, half_of(far, first), first_in[t], to_x)
        if second is not None:
            live[t, 2] = send(t, 2, half_of(far, second), second_in[t], to_y)
            live[t, 4] = send(
                t, 4, half_of(column(t, x, 1 - y), second), half_of(from_y[t], second), to_y
            )
        live[t, 3] = send(
            t, 3, half_of(column(t, 1 - x, y), first), half_of(from_x[t], first), to_x
        )

    def corner(t):
        first, second = cut(*shapes[t])
        rows, cols = shapes[t]
        live[t, 1].wait_recv()
        at, height, left, width = first

        @pl.loop(0, NZ)
        def _(i):
            j = (x * NZ + i) * NY + 1 - y
            spot = (j, pl.ds(at, height), pl.ds(left, width))
            held[t][spot] = (held[t][spot].astype(F32) + first_in[t][i].astype(F32)).astype(BF)

        live[t, 5] = send(
            t, 5, half_of(column(t, x, 1 - y), first), half_of(from_y[t], first), to_y
        )
        if second is not None:
            live[t, 2].wait_recv()
            low, tall, off, wide = second

            @pl.loop(0, NZ)
            def _(i):
                j = ((1 - x) * NZ + i) * NY + y
                spot = (j, pl.ds(low, tall), pl.ds(off, wide))
                held[t][spot] = (
                    held[t][spot].astype(F32) + second_in[t][i].astype(F32)
                ).astype(BF)

            live[t, 6] = send(
                t, 6, half_of(column(t, 1 - x, y), second), half_of(from_x[t], second), to_x
            )

    def line(t):
        for kind in (3, 4, 5, 6):
            if (t, kind) in live:
                live[t, kind].wait_recv()

        def summed(i):
            j = (x * NZ + i) * NY + y
            return (
                held[t][j].astype(F32) + from_x[t][i].astype(F32) + from_y[t][i].astype(F32)
            )

        for step in (1, 2, 3):
            level = (z + step) % NZ
            total[t][step - 1] = summed(level).astype(BF)
            live[t, 6 + step] = send(
                t, 6 + step, total[t].at[step - 1], from_z[t].at[step - 1], device(x, level, y, c)
            )
        result[t][...] = summed(z)

    def end(t):
        for step in (1, 2, 3):
            live[t, 6 + step].wait_recv()
        acc = result[t][...]
        for step in range(3):
            acc = acc + from_z[t][step].astype(F32)
        result[t][...] = acc
        live[t, "out"] = pltpu.make_async_copy(result[t], out_refs[t], out_sem.at[t])
        live[t, "out"].start()

    stages = (begin, pair, corner, line, end)
    for tick in range(count + len(stages) - 1):
        for lag, stage in enumerate(stages):
            if 0 <= tick - lag < count:
                stage(tick - lag)
    for move in moves:
        move.wait_send()
    for t in range(count):
        live[t, "out"].wait()


def reduce_shards(parts, shapes):
    count = len(shapes)

    def halves(which, dtype=BF):
        spaces = []
        for rows, cols in shapes:
            half = cut(rows, cols)[which]
            half = (0, 16, 0, 128) if half is None else half
            spaces.append(pltpu.VMEM((NZ, half[1], half[3]), dtype))
        return spaces

    def space(lead, dtype=BF):
        return [pltpu.VMEM(lead + shape, dtype) for shape in shapes]

    return pl.pallas_call(
        functools.partial(reduce_kernel, shapes),
        out_shape=[jax.ShapeDtypeStruct(shape, F32) for shape in shapes],
        in_specs=[pl.BlockSpec(memory_space=pl.ANY)] * count,
        out_specs=[pl.BlockSpec(memory_space=pl.ANY)] * count,
        scratch_shapes=[
            *space((16,)),
            *space((16,)),
            *halves(0),
            *halves(1),
            *space((NZ,)),
            *space((NZ,)),
            *space((3,)),
            *space((3,)),
            *space((), F32),
            pltpu.SemaphoreType.DMA((count,)),
            pltpu.SemaphoreType.DMA((count, 10)),
            pltpu.SemaphoreType.DMA((count, 10)),
            pltpu.SemaphoreType.DMA((count,)),
        ],
        compiler_params=pltpu.CompilerParams(
            collective_id=1, has_side_effects=True, vmem_limit_bytes=60 * 2**20
        ),
        name="reduce",
    )(*parts)


def gather_all(conv_weight, inner_weight, outer_weight, vectors):
    width = vectors.shape[1]
    padded = jnp.pad(vectors, ((0, 14), (0, 128 - width)))
    shards = []
    for b in range(2):
        shards += [
            conv_weight[b].reshape(-1, D),
            inner_weight[b].reshape(-1, FF),
            outer_weight[b].reshape(-1, D),
        ]
    full = gather([padded] + shards)
    flat = full[0].reshape(NDEV, 16, 128)[:, :2, :width]
    flat = flat.transpose(1, 0, 2).reshape(2, NV).astype(F32)
    return [tuple(full[1 + 3 * b : 4 + 3 * b]) + (flat[b],) for b in range(2)]


def reduce_all(grads, width):
    members, shapes = [], []
    for b in (1, 0):
        conv, inner, outer, _ = grads[b]
        for member in (outer, inner, conv):
            rows, cols = member.shape[0] // NDEV, member.shape[1]
            members.append(member.astype(BF).reshape(16, 2, rows, cols))
            shapes.append((rows, cols))
    vector = jnp.stack([grads[0][3], grads[1][3]]).reshape(2, NDEV, width).transpose(1, 0, 2)
    vector = jnp.pad(vector, ((0, 0), (0, 14), (0, 128 - width))).astype(BF)
    members.append(vector.reshape(16, 2, 16, 128))
    shapes.append((16, 128))
    outer1, inner1, conv1, outer0, inner0, conv0, vec = reduce_shards(members, tuple(shapes))

    def both(first, second):
        return jnp.stack([first.reshape(-1), second.reshape(-1)])

    return both(conv0, conv1), both(inner0, inner1), both(outer0, outer1), vec[:2, :width]


def gather_any(conv_weight, inner_weight, outer_weight, vectors):
    def whole(member):
        return lax.all_gather(member, ("dp", "fsdp"), axis=1, tiled=True)

    conv, inner, outer, vector = (
        whole(member) for member in (conv_weight, inner_weight, outer_weight, vectors)
    )
    return [
        (
            conv[b].reshape(KS * D, D),
            inner[b].reshape(D, FF),
            outer[b].reshape(FF, D),
            vector[b].astype(F32),
        )
        for b in range(2)
    ]


def reduce_any(grads, width):
    count_dp = lax.axis_size("dp")
    count_fsdp = lax.axis_size("fsdp")

    def settle(first, second):
        member = jnp.stack([first.reshape(-1), second.reshape(-1)]).astype(BF)
        member = member.reshape(2, count_dp, count_fsdp, -1)
        spread = lax.all_to_all(member, "fsdp", split_axis=2, concat_axis=2, tiled=True)
        partial = jnp.sum(spread.astype(F32), axis=2, keepdims=True).astype(BF)
        settled = lax.all_to_all(partial, "dp", split_axis=1, concat_axis=1, tiled=True)
        return jnp.sum(settled.astype(F32), axis=(1, 2))

    return tuple(settle(first, second) for first, second in zip(*grads))


def body(fast, embeddings, conv_weight, inner_weight, outer_weight, vectors, cotangent, row_mask):
    collect = gather_all if fast else gather_any
    weights = collect(conv_weight, inner_weight, outer_weight, vectors)
    stream = embeddings.astype(F32)
    saved = []
    for b in range(2):
        stream, kept = block_forward(stream, weights[b], DILATIONS[b])
        saved.append(kept)
    output = stream.astype(BF)
    grad_stream = cotangent.astype(F32) * row_mask.astype(F32)[:, None]
    grads = [None, None]
    for b in (1, 0):
        grad_stream, grads[b] = block_backward(grad_stream, saved[b], weights[b], DILATIONS[b])
    settle = reduce_all if fast else reduce_any
    conv, inner, outer, vector = settle(grads, vectors.shape[1])
    return output, grad_stream.astype(BF), conv, inner, outer, vector


def solution(mesh):
    rows = P(("dp", "fsdp"), None)
    flat = P(None, ("dp", "fsdp"))
    fast = mesh.shape["dp"] == NX and mesh.shape["fsdp"] == NZ * NY * 2
    return jax.shard_map(
        functools.partial(body, fast),
        mesh=mesh,
        in_specs=(rows, flat, flat, flat, flat, rows, P(("dp", "fsdp"))),
        out_specs=(rows, rows, flat, flat, flat, flat),
        check_vma=False,
    )
```

```python
import functools

import jax
import jax.numpy as jnp
import numpy as np
from jax import lax
from jax.experimental import pallas as pl
from jax.experimental.pallas import tpu as pltpu
from jax.sharding import PartitionSpec as P

MESH = pl.DeviceIdType.MESH
BF = jnp.bfloat16
NX, NZ, NY = 2, 4, 2
NDEV = 32


def place():
    across = lax.axis_index("dp")
    index = lax.axis_index("fsdp")
    return across, index // (2 * NY), (index // 2) % NY, index % 2


def device(x, z, y, c):
    return (x, (z * NY + y) * 2 + c)


def shard(x, z, y, c):
    return x * (NZ * NY * 2) + (z * NY + y) * 2 + c


def meet(peers):
    barrier = pltpu.get_barrier_semaphore()
    for peer in peers:
        pl.semaphore_signal(barrier, inc=1, device_id=peer, device_id_type=MESH)
    pl.semaphore_wait(barrier, len(peers))


def neighbours(x, z, y, c):
    return [
        device(1 - x, z, y, c),
        device(x, z, 1 - y, c),
        device(x, z, y, 1 - c),
        device(x, (z + 1) % NZ, y, c),
        device(x, (z + 2) % NZ, y, c),
        device(x, (z + 3) % NZ, y, c),
    ]

def halves_of(rect):
    at, rows, left, cols = rect
    if rows >= 32:
        first = (rows // 2 + 15) // 16 * 16
        return (at, first, left, cols), (at + first, rows - first, left, cols)
    if cols >= 256:
        return (at, rows, left, cols // 2), (at, rows, left + cols // 2, cols // 2)
    return rect, None


class Gather:
    def __init__(self, shapes, pieces, own_refs, full_refs, own_sem, send_sem, recv_sem, half_sem):
        self.shapes, self.pieces = shapes, pieces
        self.own_refs, self.full_refs = own_refs, full_refs
        self.own_sem, self.send_sem, self.recv_sem, self.half_sem = own_sem, send_sem, recv_sem, half_sem
        self.place = x, z, y, c = place()
        self.to_x, self.to_y, self.to_c = device(1 - x, z, y, c), device(x, z, 1 - y, c), device(x, z, y, 1 - c)
        self.moves = {}
        self.totals = {}

    def start(self):
        meet(neighbours(*self.place))

    def part(self, p, index, rect=None):
        t, whole, _ = self.pieces[p]
        at, height, left, width = whole if rect is None else rect
        rows, cols = self.shapes[t]
        base = pl.multiple_of(index * rows + at, 16)
        if width == cols:
            return self.full_refs[t].at[pl.ds(base, height)]
        return self.full_refs[t].at[pl.ds(base, height), pl.ds(left, width)]

    def send(self, p, index, kind, target, rect=None, sem=None):
        part = self.part(p, index, rect)
        r = self.pieces[p][1] if rect is None else rect
        self.totals[p, kind] = self.totals.get((p, kind), 0) + r[1] * r[3]
        pltpu.make_async_remote_copy(
            src_ref=part, dst_ref=part, send_sem=self.send_sem.at[p, kind],
            recv_sem=self.recv_sem.at[p, index] if sem is None else sem,
            device_id=target, device_id_type=MESH).start()

    def arrive(self, p, index, rect=None, sem=None):
        part = self.part(p, index, rect)
        pltpu.make_async_copy(part, part, self.recv_sem.at[p, index] if sem is None else sem).wait()

    def own(self, t):
        x, z, y, c = self.place
        rows, cols = self.shapes[t]
        base = pl.multiple_of(shard(x, z, y, c) * rows, 16)
        self.moves[t] = pltpu.make_async_copy(self.own_refs[t], self.full_refs[t].at[pl.ds(base, rows)], self.own_sem.at[t])
        self.moves[t].start()

    def ready(self, p):
        t = self.pieces[p][0]
        if t in self.moves:
            self.moves.pop(t).wait()

    def along(self, p, index):
        x, z, y, c = self.place
        for step in (1, 2, 3):
            self.send(p, index, 0, device(x, (z + step) % NZ, y, c))

    def spread(self, p, index):
        self.send(p, index, 1, self.to_x)
        self.send(p, index, 2, self.to_y)
        self.send(p, index, 3, self.to_c)

    def Z(self, p):
        x, z, y, c = self.place
        self.ready(p)
        mine = shard(x, z, y, c)
        if self.pieces[p][2] == "A":
            self.along(p, mine)
            self.spread(p, mine)
        else:
            self.spread(p, mine)
            self.along(p, mine)

    def A(self, p, ks=(1, 2, 3)):
        x, z, y, c = self.place
        for step in ks:
            index = shard(x, (z + step) % NZ, y, c)
            self.arrive(p, index)
            if self.pieces[p][2] == "A":
                self.spread(p, index)
            else:
                self.send(p, index, 3, self.to_c)

    def C(self, p, ks=(0, 1, 2, 3)):
        x, z, y, c = self.place
        first, second = halves_of(self.pieces[p][1])
        if self.pieces[p][2] == "B":
            ks = (0,) if 0 in ks else ()
        for step in ks:
            level = (z + step) % NZ
            from_x = shard(1 - x, level, y, c)
            from_y = shard(x, level, 1 - y, c)
            self.arrive(p, from_x)
            self.send(p, from_x, 2, self.to_y, first)
            self.send(p, from_x, 3, self.to_c)
            self.arrive(p, from_y)
            if second is not None:
                self.send(p, from_y, 1, self.to_x, second, self.half_sem.at[p, level])
            self.send(p, from_y, 3, self.to_c)
            if self.pieces[p][2] == "B":
                self.along(p, from_x)
                self.along(p, from_y)

    def F(self, p, ks=(0, 1, 2, 3)):
        x, z, y, c = self.place
        first, second = halves_of(self.pieces[p][1])
        if self.pieces[p][2] == "B":
            ks = (0,) if 0 in ks else ()
        for step in ks:
            level = (z + step) % NZ
            far = shard(1 - x, level, 1 - y, c)
            self.arrive(p, far, first)
            if second is not None:
                self.arrive(p, far, second, self.half_sem.at[p, level])
            self.send(p, far, 3, self.to_c)
            if self.pieces[p][2] == "B":
                self.along(p, far)

    def E(self, p, ks=(1, 2, 3), which=(0, 1, 2)):
        x, z, y, c = self.place
        for step in ks:
            level = (z + step) % NZ
            for w in which:
                ax, ay = ((1 - x, y), (x, 1 - y), (1 - x, 1 - y))[w]
                index = shard(ax, level, ay, c)
                self.arrive(p, index)
                self.send(p, index, 3, self.to_c)

    def settle(self, p):
        x, z, y, c = self.place
        for ax in range(NX):
            for az in range(NZ):
                for ay in range(NY):
                    self.arrive(p, shard(ax, az, ay, 1 - c))

    def sent(self, p):
        t, rect, _ = self.pieces[p]
        for kind in range(4):
            total = self.totals[p, kind]
            at, rows, left, cols = rect
            assert total % cols == 0
            part = self.full_refs[t].at[pl.ds(0, total // cols), pl.ds(left, cols)]
            pltpu.make_async_copy(part, part, self.send_sem.at[p, kind]).wait()


D = 512
FF = 2048
KS = 9
L = 512
NV = 3 * D + FF
DILATIONS = (2, 16)
F32 = jnp.float32
EDGE = 64
WINDOWS = 2
ROWS = WINDOWS * L
SHARE = NV // NDEV
SHAPES = ((16, 128),) + ((KS * D // NDEV, D), (D // NDEV, FF), (FF // NDEV, D)) * 2
VEC, CONV, INNER, OUTER = 0, (1, 4), (2, 5), (3, 6)


def selectors():
    column = lax.broadcasted_iota(jnp.int32, (NDEV, NV), 1)
    first = lax.broadcasted_iota(jnp.int32, (NDEV, NV), 0) * SHARE
    inside = (column >= first) & (column < first + SHARE)
    pick = jnp.where(inside, 1.0, 0.0).astype(F32)
    offset = jnp.sum(jnp.where(inside, column - first, 0), axis=0, keepdims=True)
    lane = lax.broadcasted_iota(jnp.int32, (128, NV), 0)
    return jnp.where(lane == offset, 1.0, 0.0).astype(BF), pick


def dot(left, right):
    return jnp.dot(left, right, preferred_element_type=F32)


def gelu_both(v):
    square = v * v
    t = jnp.tanh(0.7978845608028654 * (v + 0.044715 * (square * v)))
    half = 0.5 * (1.0 + t)
    slope = half + (0.5 * v) * ((1.0 - t * t) * (0.7978845608028654 + 0.10703222440890037 * square))
    return v * half, slope


def norm_parts(v):
    centered = v - jnp.mean(v, axis=-1, keepdims=True)
    r = lax.rsqrt(jnp.mean(centered * centered, axis=-1, keepdims=True) + 1e-05)
    return centered * r, r


def whole(t):
    rows, cols = SHAPES[t]
    return (0, rows, 0, cols)


PIECES = tuple((t, whole(t), "A") for t in range(len(SHAPES)))


FORWARD = (
    ("Z", 1), ("Z", 0), ("C", 1, 0), ("Z", 2), ("F", 1, 0), ("Z", 3), ("C", 2, 0), ("Z", 5),
    ("A", 1, 3), ("C", 3, 0), ("A", 1, 2), ("C", 1, 3), ("A", 0, 2), ("A", 1, 1), ("A", 0, 1, 3),
    ("Z", 4), ("C", 0, 2), ("A", 2, 2), ("C", 1, 2), ("C", 0, 0, 3), ("A", 2, 3), ("A", 3, 3),
    ("A", 2, 1), ("F", 1, 2), ("C", 2, 2), ("C", 0, 1), ("C", 1, 1), ("F", 0, 0), ("prep",),
    ("F", 3, 0), ("F", 0, 2), ("C", 5, 0), ("A", 3, 2), ("F", 0, 1), ("F", 1, 3), ("A", 3, 1),
    ("C", 2, 3), ("F", 2, 0), ("C", 2, 1), ("F", 2, 2), ("C", 3, 3), ("A", 4, 2), ("F", 1, 1),
    ("C", 3, 2), ("F", 0, 3), ("vec",), ("F", 2, 3), ("A", 5, 2), ("A", 4, 3), ("C", 3, 1),
    ("F", 5, 0), ("mask",), ("conv", 0, 0), ("F", 2, 1), ("A", 4, 1), ("turn", 0), ("F", 3, 3),
    ("A", 5, 3), ("widen", 0, 0), ("Z", 6), ("F", 3, 1), ("C", 4, 2), ("F", 3, 2), ("C", 4, 3),
    ("conv", 0, 1), ("C", 4, 1, 0), ("widen", 0, 1), ("F", 4, 2), ("A", 5, 1), ("C", 5, 2, 3),
    ("narrow", 0, 0), ("A", 6, 2), ("C", 6, 0), ("narrow", 0, 1), ("F", 4, 3, 0), ("A", 6, 1),
    ("F", 4, 1), ("C", 5, 1), ("A", 6, 3), ("conv", 1, 0), ("F", 5, 3, 2), ("C", 6, 2),
    ("conv", 1, 1), ("F", 5, 1), ("C", 6, 1), ("turn", 1), ("F", 6, 0), ("C", 6, 3),
    ("widen", 1, 0), ("F", 6, 2, 3, 1), ("widen", 1, 1), ("narrow", 1, 0), ("narrow", 1, 1),
)

KEPT = (
    ((ROWS, D), BF),
    ((ROWS, D), BF),
    ((D, ROWS), BF),
    ((D, ROWS), BF),
    ((4 * ROWS, D), BF),
    ((FF, ROWS), BF),
    ((ROWS, D), BF),
    ((ROWS, 128), F32),
)
NORM_C, SCALE_C, MIXED_T, LOW_T, SLOPE, HIDDEN_T, NORM_B, SCALE_B = range(8)
NK = len(KEPT)


def forward_kernel(schedule, *refs):
    count = len(SHAPES)
    vec_in, cot_ref, mask_in, refs = refs[0], refs[1], refs[2], refs[3:]
    weight_in, emb_ref, refs = refs[:3], refs[3], refs[4:]
    weight_out, refs = refs[:6], refs[6:]
    out_ref, vec_out, cot_out, refs = refs[0], refs[1], refs[2], refs[3:]
    kept_out, refs = (refs[:NK], refs[NK : 2 * NK]), refs[2 * NK :]
    full, refs = refs[:count], refs[count:]
    (stream, cols, hidden, mixed_low, emb, vec_f, vec, cot, out, turned, vec_own), refs = (
        refs[:11],
        refs[11:],
    )
    own_refs = [vec_own] + [ref.at[b] for b in range(2) for ref in weight_in]
    kept, refs = refs[:NK], refs[NK:]
    own_sem, send_sem, recv_sem, half_sem, local_sem, save_sem = refs
    g = Gather(SHAPES, PIECES, own_refs, full, own_sem, send_sem, recv_sem, half_sem)

    loads = [
        pltpu.make_async_copy(src, dst, local_sem.at[i])
        for i, (src, dst) in enumerate(((emb_ref, emb), (cot_ref, cot)))
    ]
    saves = {}

    def save(name, src, dst):
        move = pltpu.make_async_copy(src, dst, save_sem.at[len(saves)])
        move.start()
        saves[name] = move

    waited = set()

    def saved(name):
        if name in saves and name not in waited:
            saves[name].wait()
            waited.add(name)

    settled = set()

    def settle(t):
        if t in settled:
            return
        settled.add(t)
        for p, (tensor, _, _) in enumerate(PIECES):
            if tensor == t:
                g.settle(p)

    def keep(b, *members):
        for i in members:
            save((b, i), kept[i], kept_out[b][i])

    def free(b, *members):
        if b == 1:
            for i in members:
                saved((0, i))

    def prepare():
        loads[0].wait()
        edge = jnp.zeros((EDGE, D), F32)
        for w in range(WINDOWS):
            stream[w, 0:EDGE] = edge
            stream[w, EDGE + L : EDGE + L + EDGE] = edge
            stream[w, EDGE : EDGE + L] = emb[w * L : (w + 1) * L].astype(F32)
        kept[LOW_T][...] = emb[...].T
        keep(0, LOW_T)

    def vectors():
        settle(VEC)
        spread, pick = selectors()
        vec_f[...] = full[VEC][...].astype(F32)
        for b in range(2):
            rows = vec_f[pl.ds(b, NDEV, stride=16)].astype(BF)
            vec[b : b + 1] = jnp.sum(dot(rows, spread) * pick, axis=0, keepdims=True)
        save("vec", vec, vec_out)

    def masked():
        loads[1].wait()
        for i in range(ROWS // 128):
            line = jnp.broadcast_to(mask_in[i : i + 1].astype(F32), (128, 128)).T
            for j in range(D // 128):
                spot = (slice(i * 128, (i + 1) * 128), slice(j * 128, (j + 1) * 128))
                cot[spot] = (cot[spot].astype(F32) * line).astype(BF)
        save("cot", cot, cot_out)

    def turn(b):
        settle(CONV[b])
        if b == 1:
            saved((0, "kernel"))
        for k in range(KS):
            turned[k * D : (k + 1) * D] = full[CONV[b]][k * D : (k + 1) * D].T
        save((b, "kernel"), turned, weight_out[3 * b])

    def conv(b, w):
        at = slice(w * L, (w + 1) * L)
        if w == 0:
            settle(CONV[b])
            free(b, NORM_C, SCALE_C, MIXED_T)
        for k in range(KS):
            first = EDGE + (k - KS // 2) * DILATIONS[b]
            cols[:, k * D : (k + 1) * D] = stream[w, first : first + L].astype(BF)
        pre = dot(cols[...], full[CONV[b]][...]) + vec[b : b + 1, 0:D]
        value, slope = gelu_both(pre)
        n, r = norm_parts(value)
        kept[NORM_C][at] = n.astype(BF)
        kept[SCALE_C][at] = (slope * r).astype(BF)
        mixed = stream[w, EDGE : EDGE + L] + vec[b : b + 1, D : 2 * D] * n
        stream[w, EDGE : EDGE + L] = mixed
        low = mixed.astype(BF)
        mixed_low[at] = low
        kept[MIXED_T][:, at] = low.T
        if w == WINDOWS - 1:
            keep(b, NORM_C, SCALE_C, MIXED_T)

    def widen(b, w):
        at = slice(w * L, (w + 1) * L)
        if w == 0:
            settle(INNER[b])
            free(b, SLOPE, HIDDEN_T)
            save((b, "inner"), full[INNER[b]], weight_out[3 * b + 1])
        values = mixed_low[at]
        for n in range(FF // D):
            part = slice(n * D, (n + 1) * D)
            pre = dot(values, full[INNER[b]][:, part])
            pre = pre + vec[b : b + 1, 3 * D + n * D : 3 * D + (n + 1) * D]
            value, slope = gelu_both(pre)
            kept[SLOPE][n * ROWS + w * L : n * ROWS + (w + 1) * L] = slope.astype(BF)
            low = value.astype(BF)
            hidden[at, part] = low
            kept[HIDDEN_T][part, at] = low.T
        if w == WINDOWS - 1:
            keep(b, SLOPE, HIDDEN_T)

    def narrow(b, w):
        at = slice(w * L, (w + 1) * L)
        if w == 0:
            settle(OUTER[b])
            free(b, NORM_B, SCALE_B)
            save((b, "outer"), full[OUTER[b]], weight_out[3 * b + 2])
        n, r = norm_parts(dot(hidden[at], full[OUTER[b]][...]))
        kept[NORM_B][at] = n.astype(BF)
        kept[SCALE_B][at] = jnp.broadcast_to(r, (L, 128))
        result = stream[w, EDGE : EDGE + L] + vec[b : b + 1, 2 * D : 3 * D] * n
        if b == 0:
            stream[w, EDGE : EDGE + L] = result
            if w == 0:
                saved((0, LOW_T))
            kept[LOW_T][:, at] = result.astype(BF).T
        else:
            out[at] = result.astype(BF)
        if w == WINDOWS - 1:
            keep(b, NORM_B, SCALE_B)
            if b == 0:
                keep(1, LOW_T)
            else:
                save("out", out, out_ref)

    actions = {
        "Z": g.Z,
        "A": g.A,
        "C": g.C,
        "F": g.F,
        "E": g.E,
        "prep": prepare,
        "vec": vectors,
        "mask": masked,
        "turn": turn,
        "conv": conv,
        "widen": widen,
        "narrow": narrow,
    }
    vec_f[0:16] = jnp.zeros((16, 128), F32)
    vec_f[0:2, 0:SHARE] = vec_in[...].astype(F32)
    vec_own[...] = vec_f[0:16].astype(BF)
    for t in range(count):
        g.own(t)
    for move in loads:
        move.start()
    g.start()
    for name, *where in schedule:
        if name in "ACFE":
            actions[name](where[0], tuple(where[1:]))
        else:
            actions[name](*where)
    for p in range(len(PIECES)):
        g.sent(p)
    for name in saves:
        saved(name)


def forward(vectors, cotangent, mask, weights, embeddings):
    count, n = len(SHAPES), len(PIECES)
    anywhere = pl.BlockSpec(memory_space=pl.ANY)
    held = pl.BlockSpec(memory_space=pltpu.VMEM)
    out_shape = (
        [jax.ShapeDtypeStruct((NDEV * r, w), BF) for r, w in SHAPES[1:]]
        + [jax.ShapeDtypeStruct((ROWS, D), BF), jax.ShapeDtypeStruct((8, NV), F32)]
        + [jax.ShapeDtypeStruct((ROWS, D), BF)]
        + [jax.ShapeDtypeStruct(shape, dtype) for shape, dtype in KEPT * 2]
    )
    return pl.pallas_call(
        functools.partial(forward_kernel, FORWARD),
        out_shape=out_shape,
        in_specs=[held, anywhere, held] + [anywhere] * 4,
        out_specs=[anywhere] * len(out_shape),
        scratch_shapes=[
            *[pltpu.VMEM((NDEV * r, w), BF) for r, w in SHAPES],
            pltpu.VMEM((WINDOWS, L + 2 * EDGE, D), F32),
            pltpu.VMEM((L, KS * D), BF),
            pltpu.VMEM((ROWS, FF), BF),
            pltpu.VMEM((ROWS, D), BF),
            pltpu.VMEM((ROWS, D), BF),
            pltpu.VMEM((NDEV * 16, 128), F32),
            pltpu.VMEM((8, NV), F32),
            pltpu.VMEM((ROWS, D), BF),
            pltpu.VMEM((ROWS, D), BF),
            pltpu.VMEM((KS * D, D), BF),
            pltpu.VMEM((16, 128), BF),
            *[pltpu.VMEM(shape, dtype) for shape, dtype in KEPT],
            pltpu.SemaphoreType.DMA((count,)),
            pltpu.SemaphoreType.DMA((n, 4)),
            pltpu.SemaphoreType.DMA((n, NDEV)),
            pltpu.SemaphoreType.DMA((n, NZ)),
            pltpu.SemaphoreType.DMA((2,)),
            pltpu.SemaphoreType.DMA((32,)),
        ],
        compiler_params=pltpu.CompilerParams(
            collective_id=0, has_side_effects=True, vmem_limit_bytes=62 * 2**20
        ),
        name="forward",
    )(vectors, cotangent, mask, *weights, embeddings)


REDUCED = (
    ("o", 1, 0, 512),
    ("i", 1, 0, 2048),
    ("c", 1, 0, 128),
    ("c", 1, 128, 128),
    ("c", 1, 256, 128),
    ("c", 1, 384, 128),
    ("o", 0, 0, 512),
    ("i", 0, 0, 2048),
    ("c", 0, 0, 128),
    ("c", 0, 128, 128),
    ("c", 0, 256, 128),
    ("c", 0, 384, 128),
    ("v", 0, 0, 128),
)
HEIGHT = {"o": FF // NDEV, "i": D // NDEV, "c": KS * D // NDEV, "v": 16}
NR = len(REDUCED)
LATER = {p: REDUCED.index((k, 1, left, width)) for p, (k, b, left, width) in enumerate(REDUCED) if b == 0 and k != "v"}


def size_of(p):
    kind, _, _, cols = REDUCED[p]
    return HEIGHT[kind], cols


def halves_in(p):
    rows, cols = size_of(p)
    return halves_of((0, rows, 0, cols))


class Reduce:
    def __init__(self, parts, swap, first_in, second_in, from_x, from_y, total, from_z, result,
                 final, outs, send_sem, recv_sem, out_sem, credit):
        self.parts, self.swap = parts, swap
        self.first_in, self.second_in = first_in, second_in
        self.from_x, self.from_y, self.total, self.from_z = from_x, from_y, total, from_z
        self.result, self.final, self.outs = result, final, outs
        self.ended = set()
        self.send_sem, self.recv_sem, self.out_sem, self.credit = send_sem, recv_sem, out_sem, credit
        self.place = x, z, y, c = place()
        self.to_x = device(1 - x, z, y, c)
        self.to_y = device(x, z, 1 - y, c)
        self.to_c = device(x, z, y, 1 - c)
        self.moves, self.live = [], {}

    def start(self):
        meet(neighbours(*self.place))

    def send(self, p, kind, src, dst, target):
        move = pltpu.make_async_remote_copy(
            src_ref=src, dst_ref=dst, send_sem=self.send_sem.at[p, kind],
            recv_sem=self.recv_sem.at[p, kind], device_id=target, device_id_type=MESH)
        move.start()
        self.moves.append(move)
        self.live[p, kind] = move

    def half_of(self, ref, half):
        at, height, left, width = half
        return ref.at[:, pl.ds(at, height), pl.ds(left, width)]

    def column(self, p, ax, ay, half):
        kind, b, left, width = REDUCED[p]
        part = self.parts[kind, b]
        at, height, off, wide = half
        return part.reshape(NX, NZ, NY, 2, *part.shape[2:]).at[
            ax, :, ay, self.place[3], pl.ds(at, height), pl.ds(left + off, wide)
        ]

    def spot(self, p, j, half=None):
        kind, b, left, width = REDUCED[p]
        at, height, off, wide = (0, *size_of(p)[:1], 0, width) if half is None else half
        return self.parts[kind, b], (j, self.place[3], pl.ds(at, height), pl.ds(left + off, wide))

    def begin(self, p):
        kind, b, left, width = REDUCED[p]
        if p in LATER:
            pl.semaphore_wait(self.credit.at[LATER[p]], 1)
        other = self.parts[kind, b].at[:, 1 - self.place[3], :, pl.ds(left, width)]
        self.send(p, 0, other, self.swap[p], self.to_c)

    def pair(self, p):
        x, z, y, c = self.place
        swap = self.swap[p]
        self.live[p, 0].wait_recv()

        @pl.loop(0, 16)
        def _(i):
            part, at = self.spot(p, i)
            part[at] = (part[at].astype(F32) + swap[i].astype(F32)).astype(BF)

        if p in LATER.values():
            pl.semaphore_signal(self.credit.at[p], inc=1, device_id=self.to_c, device_id_type=MESH)
        first, second = halves_in(p)
        half_of = self.half_of
        self.send(p, 1, self.column(p, 1 - x, 1 - y, first), self.first_in[p], self.to_x)
        if second is not None:
            self.send(p, 2, self.column(p, 1 - x, 1 - y, second), self.second_in[p], self.to_y)
            self.send(p, 4, self.column(p, x, 1 - y, second), half_of(self.from_y[p], second), self.to_y)
        self.send(p, 3, self.column(p, 1 - x, y, first), half_of(self.from_x[p], first), self.to_x)

    def add_half(self, p, ax, ay, half, extra):
        @pl.loop(0, NZ)
        def _(i):
            part, at = self.spot(p, (ax * NZ + i) * NY + ay, half)
            part[at] = (part[at].astype(F32) + extra[i].astype(F32)).astype(BF)

    def corner_x(self, p):
        x, z, y, c = self.place
        first, _ = halves_in(p)
        self.live[p, 1].wait_recv()
        self.add_half(p, x, 1 - y, first, self.first_in[p])
        self.send(p, 5, self.column(p, x, 1 - y, first), self.half_of(self.from_y[p], first), self.to_y)

    def corner_y(self, p):
        x, z, y, c = self.place
        _, second = halves_in(p)
        if second is not None:
            self.live[p, 2].wait_recv()
            self.add_half(p, 1 - x, y, second, self.second_in[p])
            self.send(p, 6, self.column(p, 1 - x, y, second), self.half_of(self.from_x[p], second), self.to_x)

    def line(self, p):
        x, z, y, c = self.place
        for kind in (3, 4, 5, 6):
            if (p, kind) in self.live:
                self.live[p, kind].wait_recv()

        def summed(i):
            part, at = self.spot(p, (x * NZ + i) * NY + y)
            return (
                part[at].astype(F32)
                + self.from_x[p][i].astype(F32)
                + self.from_y[p][i].astype(F32)
            )

        for step in (1, 2, 3):
            level = (z + step) % NZ
            self.total[p][step - 1] = summed(level).astype(BF)
            self.send(p, 6 + step, self.total[p].at[step - 1], self.from_z[p].at[step - 1], device(x, level, y, c))
        self.result[p][...] = summed(z)

    def end(self, p):
        for step in (1, 2, 3):
            self.live[p, 6 + step].wait_recv()
        acc = self.result[p][...]
        for step in range(3):
            acc = acc + self.from_z[p][step].astype(F32)
        kind, b, left, width = REDUCED[p]
        if kind == "v":
            self.final["v"][...] = acc[0:2, 0:SHARE]
        else:
            self.final[kind][:, b, left : left + width] = acc
        self.ended.add(p)
        if all(q in self.ended for q in range(NR) if REDUCED[q][0] == kind):
            move = pltpu.make_async_copy(self.final[kind], self.outs[kind], self.out_sem.at[p])
            move.start()
            self.live[p, "out"] = move

    def close(self):
        for move in self.moves:
            move.wait_send()
        for p in range(NR):
            if (p, "out") in self.live:
                self.live[p, "out"].wait()


def contract_cols(left, right):
    return lax.dot_general(left, right, (((1,), (1,)), ((), ())), preferred_element_type=F32)


def norm_back(n, e):
    return e - jnp.mean(e, axis=-1, keepdims=True) - n * jnp.mean(e * n, axis=-1, keepdims=True)


TAPS = 3

BACKWARD = (
    ("prep",), ("b1", 1, 1), ("b1", 1, 0), ("do", 1, 0), ("do", 1, 1), ("begin", 0), ("b2", 1, 1),
    ("b2", 1, 3), ("b2", 1, 0), ("b2", 1, 2), ("pair", 0), ("di", 1), ("b3", 1, 1), ("begin", 1),
    ("cor2", 0), ("cor1", 0), ("b3", 1, 0), ("b5", 1, 0), ("b5", 1, 1), ("pair", 1), ("dk", 1, 0),
    ("begin", 3), ("dk", 1, 1), ("cor1", 1), ("begin", 5), ("cor2", 1), ("pair", 3), ("line", 0),
    ("b6", 1, 0), ("pair", 5), ("begin", 2), ("b6", 1, 1), ("b1", 0, 0), ("pair", 2), ("b1", 0, 1),
    ("begin", 4), ("slope",), ("do", 0, 1), ("cor2", 3), ("cor1", 3), ("do", 0, 0), ("b2", 0, 1),
    ("pair", 4), ("begin", 6), ("b2", 0, 2), ("cor1", 2), ("b2", 0, 3), ("cor2", 5), ("b2", 0, 0),
    ("cor1", 5), ("cor2", 2), ("line", 1), ("b3", 0, 1), ("pair", 6), ("b5", 0, 1), ("di", 0),
    ("begin", 7), ("b3", 0, 0), ("line", 3), ("cor1", 6), ("cor1", 4), ("cor2", 6), ("b5", 0, 0),
    ("vg",), ("cor2", 4), ("line", 5), ("pair", 7), ("line", 2), ("dk", 0, 0), ("begin", 9),
    ("dk", 0, 1), ("pair", 9), ("line", 6), ("end", 5), ("begin", 12), ("pair", 12), ("begin", 10),
    ("cor1", 9), ("cor2", 9), ("begin", 8), ("end", 2), ("begin", 11), ("cor2", 7), ("line", 4),
    ("cor1", 7), ("pair", 10), ("line", 9), ("pair", 8), ("end", 3), ("end", 0), ("line", 7),
    ("cor2", 10), ("cor1", 10), ("end", 6), ("b6", 0, 0), ("end", 9), ("cor1", 8), ("end", 4),
    ("cor2", 8), ("cor2", 12), ("cor1", 12), ("pair", 11), ("line", 10), ("line", 8), ("line", 12),
    ("end", 1), ("end", 7), ("cor2", 11), ("cor1", 11), ("b6", 0, 1), ("line", 11), ("end", 10),
    ("end", 12), ("end", 8), ("end", 11),
)


def backward_kernel(schedule, *refs):
    weights_hbm, refs = refs[:6], refs[6:]
    (vec_hbm, cot_hbm), refs = refs[:2], refs[2:]
    kept_hbm, refs = (refs[:NK], refs[NK : 2 * NK]), refs[2 * NK :]
    outs, refs = dict(zip("cio", refs[:3])), refs[3:]
    outs["v"], emb_grad_out, refs = refs[0], refs[1], refs[2:]
    part_o1, part_i1, part_c1, part_o0, part_i0, vec_part, refs = *refs[:6], refs[6:]
    swaps, refs = refs[: NR - len(LATER)], refs[NR - len(LATER) :]
    lists = []
    for _ in range(7):
        lists.append(refs[:NR])
        refs = refs[NR:]
    first_in, second_in, from_x, from_y, total, from_z, result = lists
    final, refs = dict(zip("ciov", refs[:4])), refs[4:]
    (conv_w, inner_w, outer_w, big, hidden_t, norm_b, scale_b, mixed_t, norm_c, scale_c, low_t,
     grad, frame, temp, cols, vec, vec_grad, tile), refs = refs[:18], refs[18:]
    send_sem, recv_sem, out_sem, credit, load_sem = refs
    view = big.reshape(16, 2, KS * D // NDEV, D)
    parts = {
        ("o", 1): part_o1, ("i", 1): part_i1, ("c", 1): part_c1,
        ("o", 0): part_o0, ("i", 0): part_i0, ("c", 0): view, ("v", 0): vec_part,
    }
    conv_flat = {1: part_c1.reshape(KS * D, D), 0: big}
    own = [p for p in range(NR) if p not in LATER]
    swap = {p: swaps[own.index(LATER.get(p, p))] for p in range(NR)}
    r = Reduce(parts, swap, first_in, second_in, from_x, from_y, total, from_z, result, final, outs,
               send_sem, recv_sem, out_sem, credit)
    loading = {}
    met = set()

    def load(name, src, dst):
        move = pltpu.make_async_copy(src, dst, load_sem.at[len(loading)])
        move.start()
        loading[name] = move

    def need(*names):
        for name in names:
            if name not in met:
                met.add(name)
                loading[name].wait()

    def load_block(b, *names):
        table = {
            "norm_b": (kept_hbm[b][NORM_B], norm_b),
            "scale_b": (kept_hbm[b][SCALE_B], scale_b),
            "outer": (weights_hbm[3 * b + 2], outer_w),
            "slope": (kept_hbm[b][SLOPE], big.at[pl.ds(0, 4 * ROWS)]),
            "hidden": (kept_hbm[b][HIDDEN_T], hidden_t),
            "mixed": (kept_hbm[b][MIXED_T], mixed_t),
            "inner": (weights_hbm[3 * b + 1], inner_w),
            "norm_c": (kept_hbm[b][NORM_C], norm_c),
            "scale_c": (kept_hbm[b][SCALE_C], scale_c),
            "low": (kept_hbm[b][LOW_T], low_t),
            "kernel": (weights_hbm[3 * b], conv_w),
        }
        for name in names:
            load((b, name), *table[name])

    counts = {}

    def next_block(b, pieces, *names):
        counts[b, names] = counts.get((b, names), 0) + 1
        if b and counts[b, names] == pieces:
            load_block(0, *names)
        return counts[b, names] == pieces

    def rows_at(w):
        return slice(w * L, (w + 1) * L)

    def prepare():
        vec_grad[...] = jnp.zeros_like(vec_grad)
        edge = jnp.zeros((EDGE, D), F32)
        for w in range(WINDOWS):
            frame[w, 0:EDGE] = edge
            frame[w, EDGE + L : EDGE + L + EDGE] = edge
        need("cot")
        grad[...] = temp[...].astype(F32)
        need("vec")

    def add_vec(b, at, values):
        width = values.shape[-1]
        vec_grad[b : b + 1, at : at + width] += jnp.sum(values, axis=0, keepdims=True)

    def branch_back(b, w):
        need((b, "norm_b"), (b, "scale_b"))
        at = rows_at(w)
        n = norm_b[at].astype(F32)
        incoming = grad[at]
        add_vec(b, 2 * D, incoming * n)
        scale = jnp.concatenate([scale_b[at]] * (D // 128), axis=1)
        temp[at] = (scale * norm_back(n, vec[b : b + 1, 2 * D : 3 * D] * incoming)).astype(BF)
        next_block(b, WINDOWS, "norm_b", "scale_b")

    def hidden_back(b, n):
        need((b, "outer"), (b, "slope"))
        at = slice(n * ROWS, (n + 1) * ROWS)
        grad_hidden = contract_cols(temp[...], outer_w[n * D : (n + 1) * D])
        grad_pre = (big[at].astype(F32) * grad_hidden).astype(BF)
        big[at] = grad_pre
        add_vec(b, 3 * D + n * D, grad_pre.astype(F32))
        next_block(b, FF // D, "outer")

    def outer_grad(b, h):
        need((b, "hidden"))
        at = slice(h * 256, (h + 1) * 256)
        out = dot(hidden_t[...], temp[:, at]).astype(BF)
        parts["o", b][:, :, :, at] = out.reshape(16, 2, FF // NDEV, 256)
        next_block(b, 2, "hidden")

    def inner_grad(b):
        need((b, "mixed"))
        for n in range(FF // D):
            out = dot(mixed_t[...], big[n * ROWS : (n + 1) * ROWS]).astype(BF)
            parts["i", b][:, :, :, n * D : (n + 1) * D] = out.reshape(16, 2, D // NDEV, D)
        next_block(b, 1, "mixed")

    def mixed_back(b, w):
        need((b, "inner"))
        acc = grad[rows_at(w)]
        for n in range(FF // D):
            at = slice(n * ROWS + w * L, n * ROWS + (w + 1) * L)
            acc = acc + contract_cols(big[at], inner_w[:, n * D : (n + 1) * D])
        grad[rows_at(w)] = acc
        next_block(b, WINDOWS, "inner")

    def conv_back(b, w):
        need((b, "norm_c"), (b, "scale_c"))
        at = rows_at(w)
        n = norm_c[at].astype(F32)
        incoming = grad[at]
        add_vec(b, D, incoming * n)
        out = scale_c[at].astype(F32) * norm_back(n, vec[b : b + 1, D : 2 * D] * incoming)
        out = out.astype(BF).astype(F32)
        add_vec(b, 0, out)
        frame[w, EDGE : EDGE + L] = out
        next_block(b, WINDOWS, "norm_c", "scale_c")

    def kernel_grad(b, h):
        need((b, "low"))
        at = slice(h * 256, (h + 1) * 256)
        for k in range(KS):
            first = EDGE - (k - KS // 2) * DILATIONS[b]
            for w in range(WINDOWS):
                temp[rows_at(w), 0:256] = frame[w, first : first + L, at].astype(BF)
            conv_flat[b][k * D : (k + 1) * D, at] = dot(low_t[...], temp[:, 0:256]).astype(BF)
        next_block(b, 2, "low")

    def stream_back(b, w):
        need((b, "kernel"))
        acc = grad[rows_at(w)]
        for group in range(KS // TAPS):
            for i in range(TAPS):
                first = EDGE - (group * TAPS + i - KS // 2) * DILATIONS[b]
                cols[:, i * D : (i + 1) * D] = frame[w, first : first + L].astype(BF)
            acc = acc + dot(cols[...], conv_w[group * TAPS * D : (group + 1) * TAPS * D])
        if b:
            grad[rows_at(w)] = acc
        else:
            norm_b[rows_at(w)] = acc.astype(BF)
        if next_block(b, WINDOWS, "kernel") and b == 0:
            load("out", norm_b, emb_grad_out)

    def vector_grads():
        spread, pick = selectors()
        tile[...] = jnp.zeros_like(tile)
        for b in range(2):
            rows = (pick * vec_grad[b : b + 1]).astype(BF)
            tile[pl.ds(b, NDEV, stride=16)] = contract_cols(rows, spread)
        vec_part[...] = tile[...].astype(BF).reshape(16, 2, 16, 128)

    actions = {
        "begin": r.begin,
        "pair": r.pair,
        "cor1": r.corner_x,
        "cor2": r.corner_y,
        "line": r.line,
        "end": r.end,
        "prep": prepare,
        "b1": branch_back,
        "b2": hidden_back,
        "do": outer_grad,
        "di": inner_grad,
        "b3": mixed_back,
        "b5": conv_back,
        "dk": kernel_grad,
        "b6": stream_back,
        "vg": vector_grads,
        "slope": lambda: load_block(0, "slope"),
    }
    load("cot", cot_hbm, temp)
    load("vec", vec_hbm, vec)
    load_block(1, "norm_b", "scale_b", "outer", "slope", "hidden", "mixed", "inner", "norm_c", "scale_c", "low", "kernel")
    r.start()
    for name, *where in schedule:
        actions[name](*where)
    r.close()
    need("out")


def backward(weights, vec, cotangent, kept):
    anywhere = pl.BlockSpec(memory_space=pl.ANY)
    finals = [(rows, 2, cols) for rows, cols in SHAPES[1:4]] + [(2, SHARE)]
    out_shape = [jax.ShapeDtypeStruct(shape, F32) for shape in finals]
    out_shape += [jax.ShapeDtypeStruct((ROWS, D), BF)]

    def halves(which):
        spaces = []
        for p in range(NR):
            half = halves_in(p)[which]
            half = (0, 16, 0, 128) if half is None else half
            spaces.append(pltpu.VMEM((NZ, half[1], half[3]), BF))
        return spaces

    def space(lead, dtype=BF, members=range(NR)):
        return [pltpu.VMEM((*lead, *size_of(p)), dtype) for p in members]

    def whole_part(t):
        return pltpu.VMEM((16, 2, *SHAPES[t]), BF)

    args = (*weights, vec, cotangent, *kept)
    return pl.pallas_call(
        functools.partial(backward_kernel, BACKWARD),
        out_shape=out_shape,
        in_specs=[anywhere] * len(args),
        out_specs=[anywhere] * len(out_shape),
        scratch_shapes=[
            whole_part(3), whole_part(2), whole_part(1), whole_part(3), whole_part(2), whole_part(0),
            *space((16,), members=[p for p in range(NR) if p not in LATER]),
            *halves(0),
            *halves(1),
            *space((NZ,)),
            *space((NZ,)),
            *space((3,)),
            *space((3,)),
            *space((), F32),
            *[pltpu.VMEM(shape, F32) for shape in finals],
            pltpu.VMEM((KS * D, D), BF),
            pltpu.VMEM((D, FF), BF),
            pltpu.VMEM((FF, D), BF),
            pltpu.VMEM((KS * D, D), BF),
            pltpu.VMEM((FF, ROWS), BF),
            pltpu.VMEM((ROWS, D), BF),
            pltpu.VMEM((ROWS, 128), F32),
            pltpu.VMEM((D, ROWS), BF),
            pltpu.VMEM((ROWS, D), BF),
            pltpu.VMEM((ROWS, D), BF),
            pltpu.VMEM((D, ROWS), BF),
            pltpu.VMEM((ROWS, D), F32),
            pltpu.VMEM((WINDOWS, L + 2 * EDGE, D), F32),
            pltpu.VMEM((ROWS, D), BF),
            pltpu.VMEM((L, TAPS * D), BF),
            pltpu.VMEM((8, NV), F32),
            pltpu.VMEM((8, NV), F32),
            pltpu.VMEM((NDEV * 16, 128), F32),
            pltpu.SemaphoreType.DMA((NR, 10)),
            pltpu.SemaphoreType.DMA((NR, 10)),
            pltpu.SemaphoreType.DMA((NR,)),
            pltpu.SemaphoreType.REGULAR((NR,)),
            pltpu.SemaphoreType.DMA((32,)),
        ],
        compiler_params=pltpu.CompilerParams(
            collective_id=1, has_side_effects=True, vmem_limit_bytes=63 * 2**20
        ),
        name="backward",
    )(*args)


def finish_kernel(count, *refs):
    for source, target in zip(refs[:count], refs[count:]):
        target[...] = source[...]


def finish(members):
    steps = 4

    def block(member):
        if member.shape[0] < 16:
            return pl.BlockSpec(member.shape, lambda i: (0,) * member.ndim)
        shape = (member.shape[0] // steps, *member.shape[1:])
        return pl.BlockSpec(shape, lambda i: (i,) + (0,) * (member.ndim - 1))

    blocks = [block(member) for member in members]
    return pl.pallas_call(
        functools.partial(finish_kernel, len(members)),
        grid=(steps,),
        out_shape=[jax.ShapeDtypeStruct(v.shape, v.dtype) for v in members],
        in_specs=blocks,
        out_specs=blocks,
        name="finish",
    )(*members)


def normalize(values):
    centered = values - jnp.mean(values, axis=-1, keepdims=True)
    return centered * lax.rsqrt(jnp.mean(centered * centered, axis=-1, keepdims=True) + 1e-05)


def conv_branch(values):
    return normalize(jax.nn.gelu(values))


def contract_rows(left, right):
    return lax.dot_general(left, right, (((0,), (0,)), ((), ())), preferred_element_type=F32)


def columns(stream_low, dilation):
    windows = stream_low.shape[0] // L
    framed = stream_low.reshape(windows, L, D)
    margin = KS // 2 * dilation
    padded = jnp.pad(framed, ((0, 0), (margin, margin), (0, 0)))
    stacked = jnp.concatenate(
        [padded[:, tap_id * dilation : tap_id * dilation + L] for tap_id in range(KS)], axis=2
    )
    return stacked.reshape(windows * L, KS * D)


def fold_back(grad_cols, dilation):
    windows = grad_cols.shape[0] // L
    framed = grad_cols.reshape(windows, L, KS, D)
    margin = KS // 2 * dilation
    total = jnp.zeros((windows, L + 2 * margin, D), F32)
    for tap_id in range(KS):
        before = tap_id * dilation
        total = total + jnp.pad(
            framed[:, :, tap_id], ((0, 0), (before, 2 * margin - before), (0, 0))
        )
    return total[:, margin : margin + L].reshape(windows * L, D)


def block_forward(stream, weights, dilation):
    conv_mat, inner_mat, outer_mat, vector = weights
    conv_bias = vector[:D]
    gain_conv = vector[D : 2 * D]
    gain_ffn = vector[2 * D : 3 * D]
    bias_ffn = vector[3 * D :]
    stream_low = stream.astype(BF)
    pre_conv = (
        jnp.dot(columns(stream_low, dilation), conv_mat, preferred_element_type=F32) + conv_bias
    )
    mixed = stream + gain_conv * conv_branch(pre_conv)
    mixed_low = mixed.astype(BF)
    pre_ffn = jnp.dot(mixed_low, inner_mat, preferred_element_type=F32) + bias_ffn
    hidden_low = jax.nn.gelu(pre_ffn).astype(BF)
    branch = jnp.dot(hidden_low, outer_mat, preferred_element_type=F32)
    result = mixed + gain_ffn * normalize(branch)
    return (result, (stream_low, pre_conv, mixed_low, pre_ffn, hidden_low, branch))


def block_backward(grad_out, saved, weights, dilation):
    conv_mat, inner_mat, outer_mat, vector = weights
    gain_conv = vector[D : 2 * D]
    gain_ffn = vector[2 * D : 3 * D]
    stream_low, pre_conv, mixed_low, pre_ffn, hidden_low, branch = saved
    normed_branch, branch_back = jax.vjp(normalize, branch)
    grad_gain_ffn = jnp.sum(grad_out * normed_branch, axis=0)
    grad_branch = branch_back(grad_out * gain_ffn)[0].astype(BF)
    grad_outer = contract_rows(hidden_low, grad_branch)
    grad_hidden = contract_cols(grad_branch, outer_mat)
    _, gelu_back = jax.vjp(jax.nn.gelu, pre_ffn)
    grad_pre_ffn = gelu_back(grad_hidden)[0].astype(BF)
    grad_bias_ffn = jnp.sum(grad_pre_ffn.astype(F32), axis=0)
    grad_inner = contract_rows(mixed_low, grad_pre_ffn)
    grad_mixed = grad_out + contract_cols(grad_pre_ffn, inner_mat)
    normed_conv, conv_back = jax.vjp(conv_branch, pre_conv)
    grad_gain_conv = jnp.sum(grad_mixed * normed_conv, axis=0)
    grad_pre_conv = conv_back(grad_mixed * gain_conv)[0].astype(BF)
    grad_conv_bias = jnp.sum(grad_pre_conv.astype(F32), axis=0)
    grad_kernel = contract_rows(columns(stream_low, dilation), grad_pre_conv)
    grad_stream = grad_mixed + fold_back(contract_cols(grad_pre_conv, conv_mat), dilation)
    vector_grad = jnp.concatenate([grad_conv_bias, grad_gain_conv, grad_gain_ffn, grad_bias_ffn])
    return (grad_stream, (grad_kernel, grad_inner, grad_outer, vector_grad))


def gather_any(conv_weight, inner_weight, outer_weight, vectors):
    def whole(member):
        return lax.all_gather(member, ("dp", "fsdp"), axis=1, tiled=True)

    conv, inner, outer, vector = (
        whole(member) for member in (conv_weight, inner_weight, outer_weight, vectors)
    )
    return [
        (
            conv[b].reshape(KS * D, D),
            inner[b].reshape(D, FF),
            outer[b].reshape(FF, D),
            vector[b].astype(F32),
        )
        for b in range(2)
    ]


def reduce_any(grads, width):
    count_dp = lax.axis_size("dp")
    count_fsdp = lax.axis_size("fsdp")

    def settle(first, second):
        member = jnp.stack([first.reshape(-1), second.reshape(-1)]).astype(BF)
        member = member.reshape(2, count_dp, count_fsdp, -1)
        spread = lax.all_to_all(member, "fsdp", split_axis=2, concat_axis=2, tiled=True)
        partial = jnp.sum(spread.astype(F32), axis=2, keepdims=True).astype(BF)
        settled = lax.all_to_all(partial, "dp", split_axis=1, concat_axis=1, tiled=True)
        return jnp.sum(settled.astype(F32), axis=(1, 2))

    return tuple(settle(first, second) for first, second in zip(*grads))


def body_here(embeddings, conv_weight, inner_weight, outer_weight, vectors, cotangent, row_mask):
    weights = (
        conv_weight.reshape(2, -1, D),
        inner_weight.reshape(2, -1, FF),
        outer_weight.reshape(2, -1, D),
    )
    mask = row_mask.reshape(ROWS // 128, 128)
    result = forward(vectors, cotangent, mask, weights, embeddings)
    weights, output, vec, incoming, kept = result[:6], result[6], result[7], result[8], result[9:]
    *grads, vec_grad, emb_grad = finish((output, *backward(weights, vec, incoming, kept)))
    output, *grads = grads
    conv, inner, outer = (member.transpose(1, 0, 2).reshape(2, -1) for member in grads)
    return output, emb_grad, conv, inner, outer, vec_grad


def body_any(embeddings, conv_weight, inner_weight, outer_weight, vectors, cotangent, row_mask):
    weights = gather_any(conv_weight, inner_weight, outer_weight, vectors)
    stream = embeddings.astype(F32)
    saved = []
    for b in range(2):
        stream, kept = block_forward(stream, weights[b], DILATIONS[b])
        saved.append(kept)
    output = stream.astype(BF)
    grad_stream = cotangent.astype(F32) * row_mask.astype(F32)[:, None]
    grads = [None, None]
    for b in (1, 0):
        grad_stream, grads[b] = block_backward(grad_stream, saved[b], weights[b], DILATIONS[b])
    return (output, grad_stream.astype(BF), *reduce_any(grads, vectors.shape[1]))


def solution(mesh):
    rows = P(("dp", "fsdp"), None)
    flat = P(None, ("dp", "fsdp"))
    here = mesh.shape["dp"] == NX and mesh.shape["fsdp"] == NZ * NY * 2
    return jax.shard_map(
        body_here if here else body_any,
        mesh=mesh,
        in_specs=(rows, flat, flat, flat, flat, rows, P(("dp", "fsdp"))),
        out_specs=(rows, rows, flat, flat, flat, flat),
        check_vma=False,
    )
```

```python
import functools

import jax
import jax.numpy as jnp
import numpy as np
from jax import lax
from jax.experimental import pallas as pl
from jax.experimental.pallas import tpu as pltpu
from jax.sharding import PartitionSpec as P

MESH = pl.DeviceIdType.MESH
BF = jnp.bfloat16
NX, NZ, NY = 2, 4, 2
NDEV = 32


def place():
    across = lax.axis_index("dp")
    index = lax.axis_index("fsdp")
    return across, index // (2 * NY), (index // 2) % NY, index % 2


def device(x, z, y, c):
    return (x, (z * NY + y) * 2 + c)


def shard(x, z, y, c):
    return x * (NZ * NY * 2) + (z * NY + y) * 2 + c


def meet(peers):
    barrier = pltpu.get_barrier_semaphore()
    for peer in peers:
        pl.semaphore_signal(barrier, inc=1, device_id=peer, device_id_type=MESH)
    pl.semaphore_wait(barrier, len(peers))


def neighbours(x, z, y, c):
    return [
        device(1 - x, z, y, c),
        device(x, z, 1 - y, c),
        device(x, z, y, 1 - c),
        device(x, (z + 1) % NZ, y, c),
        device(x, (z + 2) % NZ, y, c),
        device(x, (z + 3) % NZ, y, c),
    ]

def halves_of(rect):
    at, rows, left, cols = rect
    if rows >= 32:
        first = (rows // 2 + 15) // 16 * 16
        return (at, first, left, cols), (at + first, rows - first, left, cols)
    if cols >= 256:
        return (at, rows, left, cols // 2), (at, rows, left + cols // 2, cols // 2)
    return rect, None


class Gather:
    def __init__(self, shapes, pieces, own_refs, full_refs, own_sem, send_sem, recv_sem):
        self.shapes, self.pieces = shapes, pieces
        self.own_refs, self.full_refs = own_refs, full_refs
        self.own_sem, self.send_sem, self.recv_sem = own_sem, send_sem, recv_sem
        self.place = x, z, y, c = place()
        self.to_x = device(1 - x, z, y, c)
        self.to_y = device(x, z, 1 - y, c)
        self.to_c = device(x, z, y, 1 - c)
        self.near = z + 1 - 2 * (z % 2)
        self.away = 2 - 2 * (z // 2)
        self.moves, self.totals = {}, {}

    def start(self):
        meet(neighbours(*self.place))

    def levels(self, which):
        z = self.place[1]
        return {
            "own": (z, 1),
            "near": (self.near, 1),
            "away": (self.away, 2),
            "pair": (2 * (z // 2), 2),
            "all": (0, NZ),
        }[which]

    def part(self, p, ax, level, ay, c, half=None):
        t, rect = self.pieces[p]
        at, height, left, width = rect if half is None else half
        rows, cols = self.shapes[t]
        low, count = level
        view = self.full_refs[t].reshape(NX, NZ, NY, 2, rows, cols)
        return view.at[ax, pl.ds(low, count), ay, c, pl.ds(at, height), pl.ds(left, width)]

    def send(self, p, part, kind, slot, target, amount):
        self.totals[p, kind] = self.totals.get((p, kind), 0) + amount
        pltpu.make_async_remote_copy(
            src_ref=part, dst_ref=part, send_sem=self.send_sem.at[p, kind],
            recv_sem=self.recv_sem.at[p, slot], device_id=target, device_id_type=MESH).start()

    def arrive(self, p, part, slot):
        pltpu.make_async_copy(part, part, self.recv_sem.at[p, slot]).wait()

    def amount(self, p, half=None):
        rect = self.pieces[p][1] if half is None else half
        return rect[1] * rect[3]

    def own(self, t):
        x, z, y, c = self.place
        rows, cols = self.shapes[t]
        view = self.full_refs[t].reshape(NX, NZ, NY, 2, rows, cols)
        self.moves[t] = pltpu.make_async_copy(self.own_refs[t], view.at[x, z, y, c], self.own_sem.at[t])
        self.moves[t].start()

    def over(self, p, which, slot, count):
        x, z, y, c = self.place
        part = self.part(p, x, self.levels(which), y, c)
        self.send(p, part, 1, 4 + slot, self.to_x, count * self.amount(p))
        self.send(p, part, 2, 7 + slot, self.to_y, count * self.amount(p))

    def column(self, p, ax, ay, slot):
        part = self.part(p, ax, self.levels("all"), ay, self.place[3])
        self.send(p, part, 3, 14 + slot, self.to_c, NZ * self.amount(p))

    def Z(self, p):
        x, z, y, c = self.place
        t = self.pieces[p][0]
        if t in self.moves:
            self.moves.pop(t).wait()
        part = self.part(p, x, self.levels("own"), y, c)
        for step in (1, 2, 3):
            self.send(p, part, 0, z, device(x, (z + step) % NZ, y, c), self.amount(p))
        self.over(p, "own", 0, 1)

    def A(self, p, k):
        x, z, y, c = self.place
        if k == 0:
            self.arrive(p, self.part(p, x, self.levels("near"), y, c), self.near)
            self.over(p, "near", 1, 1)
        else:
            for i in range(2):
                self.arrive(p, self.part(p, x, (self.away + i, 1), y, c), self.away + i)
            self.over(p, "away", 2, 2)
            self.column(p, x, y, 0)

    def C(self, p, k):
        x, z, y, c = self.place
        first, second = halves_of(self.pieces[p][1])
        which = "away" if k else "pair"
        for slot, part_levels in (((2, "away"),) if k else ((0, "own"), (1, "near"))):
            self.arrive(p, self.part(p, 1 - x, self.levels(part_levels), y, c), 4 + slot)
        half = self.part(p, 1 - x, self.levels(which), y, c, first)
        self.send(p, half, 2, 10 + k, self.to_y, 2 * self.amount(p, first))
        for slot, part_levels in (((2, "away"),) if k else ((0, "own"), (1, "near"))):
            self.arrive(p, self.part(p, x, self.levels(part_levels), 1 - y, c), 7 + slot)
        if second is not None:
            half = self.part(p, x, self.levels(which), 1 - y, c, second)
            self.send(p, half, 1, 12 + k, self.to_x, 2 * self.amount(p, second))
        if k:
            self.column(p, 1 - x, y, 1)
            self.column(p, x, 1 - y, 2)

    def F(self, p):
        x, z, y, c = self.place
        first, second = halves_of(self.pieces[p][1])
        for k, which in enumerate(("pair", "away")):
            self.arrive(p, self.part(p, 1 - x, self.levels(which), 1 - y, c, first), 10 + k)
            if second is not None:
                self.arrive(p, self.part(p, 1 - x, self.levels(which), 1 - y, c, second), 12 + k)
        self.column(p, 1 - x, 1 - y, 3)

    def settle(self, p):
        x, z, y, c = self.place
        for slot, (ax, ay) in enumerate(((x, y), (1 - x, y), (x, 1 - y), (1 - x, 1 - y))):
            self.arrive(p, self.part(p, ax, self.levels("all"), ay, 1 - c), 14 + slot)

    def sent(self, p):
        t, (at, rows, left, cols) = self.pieces[p]
        for kind in range(4):
            total = self.totals[p, kind]
            part = self.full_refs[t].at[pl.ds(0, total // cols), pl.ds(left, cols)]
            pltpu.make_async_copy(part, part, self.send_sem.at[p, kind]).wait()


D = 512
FF = 2048
KS = 9
L = 512
NV = 3 * D + FF
DILATIONS = (2, 16)
F32 = jnp.float32
EDGE = 64
WINDOWS = 2
ROWS = WINDOWS * L
SHARE = NV // NDEV
SHAPES = ((16, 128),) + ((KS * D // NDEV, D), (D // NDEV, FF), (FF // NDEV, D)) * 2
VEC, CONV, INNER, OUTER = 0, (1, 4), (2, 5), (3, 6)


def selectors():
    column = lax.broadcasted_iota(jnp.int32, (NDEV, NV), 1)
    first = lax.broadcasted_iota(jnp.int32, (NDEV, NV), 0) * SHARE
    inside = (column >= first) & (column < first + SHARE)
    pick = jnp.where(inside, 1.0, 0.0).astype(F32)
    offset = jnp.sum(jnp.where(inside, column - first, 0), axis=0, keepdims=True)
    lane = lax.broadcasted_iota(jnp.int32, (128, NV), 0)
    return jnp.where(lane == offset, 1.0, 0.0).astype(BF), pick


def dot(left, right):
    return jnp.dot(left, right, preferred_element_type=F32)


def gelu_both(v):
    square = v * v
    t = jnp.tanh(0.7978845608028654 * (v + 0.044715 * (square * v)))
    half = 0.5 * (1.0 + t)
    slope = half + (0.5 * v) * ((1.0 - t * t) * (0.7978845608028654 + 0.10703222440890037 * square))
    return v * half, slope


def norm_parts(v):
    centered = v - jnp.mean(v, axis=-1, keepdims=True)
    r = lax.rsqrt(jnp.mean(centered * centered, axis=-1, keepdims=True) + 1e-05)
    return centered * r, r


def whole(t):
    rows, cols = SHAPES[t]
    return (0, rows, 0, cols)


PIECES = (
    (VEC, whole(VEC)),
    (CONV[0], (0, 80, 0, D)),
    (CONV[0], (80, 64, 0, D)),
    (INNER[0], whole(INNER[0])),
    (OUTER[0], whole(OUTER[0])),
    (CONV[1], (0, 80, 0, D)),
    (CONV[1], (80, 64, 0, D)),
    (INNER[1], whole(INNER[1])),
    (OUTER[1], whole(OUTER[1])),
)


FORWARD = (
    ("Z", 0), ("Z", 1), ("Z", 6), ("A", 0, 0), ("Z", 2), ("C", 0, 0), ("Z", 3), ("A", 1, 0),
    ("Z", 5), ("prep",), ("A", 6, 0), ("C", 1, 0), ("A", 0, 1), ("Z", 4), ("A", 2, 0), ("C", 6, 0),
    ("A", 1, 1), ("C", 2, 0), ("A", 3, 0), ("C", 0, 1), ("C", 1, 1), ("A", 5, 0), ("A", 6, 1),
    ("A", 2, 1), ("C", 6, 1), ("F", 0), ("A", 3, 1), ("C", 2, 1), ("C", 3, 0), ("A", 4, 0),
    ("F", 1), ("C", 3, 1), ("F", 2), ("F", 6), ("A", 4, 1), ("C", 5, 0), ("A", 5, 1), ("vec",),
    ("Z", 7), ("mask",), ("conv", 0, 0), ("F", 3), ("conv", 0, 1), ("C", 4, 0), ("C", 4, 1),
    ("widen", 0, 0), ("C", 5, 1), ("A", 7, 0), ("turn", 0), ("A", 7, 1), ("Z", 8), ("widen", 0, 1),
    ("F", 4), ("F", 5), ("narrow", 0, 0), ("A", 8, 0), ("C", 7, 0), ("turn", 1), ("narrow", 0, 1),
    ("C", 7, 1), ("A", 8, 1), ("conv", 1, 0), ("conv", 1, 1), ("F", 7), ("C", 8, 0), ("C", 8, 1),
    ("widen", 1, 0), ("F", 8), ("widen", 1, 1), ("narrow", 1, 0), ("narrow", 1, 1),
)

KEPT = (
    ((ROWS, D), BF),
    ((ROWS, D), BF),
    ((D, ROWS), BF),
    ((D, ROWS), BF),
    ((4 * ROWS, D), BF),
    ((FF, ROWS), BF),
    ((ROWS, D), BF),
    ((ROWS, 128), F32),
)
NORM_C, SCALE_C, MIXED_T, LOW_T, SLOPE, HIDDEN_T, NORM_B, SCALE_B = range(8)
NK = len(KEPT)


def forward_kernel(schedule, *refs):
    count = len(SHAPES)
    vec_in, cot_ref, mask_in, refs = refs[0], refs[1], refs[2], refs[3:]
    weight_in, emb_ref, refs = refs[:3], refs[3], refs[4:]
    weight_out, refs = refs[:6], refs[6:]
    out_ref, vec_out, cot_out, refs = refs[0], refs[1], refs[2], refs[3:]
    kept_out, refs = (refs[:NK], refs[NK : 2 * NK]), refs[2 * NK :]
    full, refs = refs[:count], refs[count:]
    (stream, cols, hidden, mixed_low, emb, vec_f, vec, cot, out, turned, vec_own), refs = (
        refs[:11],
        refs[11:],
    )
    own_refs = [vec_own] + [ref.at[b] for b in range(2) for ref in weight_in]
    kept, refs = refs[:NK], refs[NK:]
    own_sem, send_sem, recv_sem, local_sem, save_sem = refs
    g = Gather(SHAPES, PIECES, own_refs, full, own_sem, send_sem, recv_sem)

    loads = [
        pltpu.make_async_copy(src, dst, local_sem.at[i])
        for i, (src, dst) in enumerate(((emb_ref, emb), (cot_ref, cot)))
    ]
    saves = {}

    def save(name, src, dst):
        move = pltpu.make_async_copy(src, dst, save_sem.at[len(saves)])
        move.start()
        saves[name] = move

    waited = set()

    def saved(name):
        if name in saves and name not in waited:
            saves[name].wait()
            waited.add(name)

    settled = set()

    def settle(t):
        if t in settled:
            return
        settled.add(t)
        for p, (tensor, _) in enumerate(PIECES):
            if tensor == t:
                g.settle(p)

    def keep(b, *members):
        for i in members:
            save((b, i), kept[i], kept_out[b][i])

    def free(b, *members):
        if b == 1:
            for i in members:
                saved((0, i))

    def prepare():
        loads[0].wait()
        edge = jnp.zeros((EDGE, D), F32)
        for w in range(WINDOWS):
            stream[w, 0:EDGE] = edge
            stream[w, EDGE + L : EDGE + L + EDGE] = edge
            stream[w, EDGE : EDGE + L] = emb[w * L : (w + 1) * L].astype(F32)
        kept[LOW_T][...] = emb[...].T
        keep(0, LOW_T)

    def vectors():
        settle(VEC)
        spread, pick = selectors()
        vec_f[...] = full[VEC][...].astype(F32)
        for b in range(2):
            rows = vec_f[pl.ds(b, NDEV, stride=16)].astype(BF)
            vec[b : b + 1] = jnp.sum(dot(rows, spread) * pick, axis=0, keepdims=True)
        save("vec", vec, vec_out)

    def masked():
        loads[1].wait()
        for i in range(ROWS // 128):
            line = jnp.broadcast_to(mask_in[i : i + 1].astype(F32), (128, 128)).T
            for j in range(D // 128):
                spot = (slice(i * 128, (i + 1) * 128), slice(j * 128, (j + 1) * 128))
                cot[spot] = (cot[spot].astype(F32) * line).astype(BF)
        save("cot", cot, cot_out)

    def turn(b):
        settle(CONV[b])
        if b == 1:
            saved((0, "kernel"))
        for k in range(KS):
            turned[k * D : (k + 1) * D] = full[CONV[b]][k * D : (k + 1) * D].T
        save((b, "kernel"), turned, weight_out[3 * b])

    def conv(b, w):
        at = slice(w * L, (w + 1) * L)
        if w == 0:
            settle(CONV[b])
            free(b, NORM_C, SCALE_C, MIXED_T)
        for k in range(KS):
            first = EDGE + (k - KS // 2) * DILATIONS[b]
            cols[:, k * D : (k + 1) * D] = stream[w, first : first + L].astype(BF)
        pre = dot(cols[...], full[CONV[b]][...]) + vec[b : b + 1, 0:D]
        value, slope = gelu_both(pre)
        n, r = norm_parts(value)
        kept[NORM_C][at] = n.astype(BF)
        kept[SCALE_C][at] = (slope * r).astype(BF)
        mixed = stream[w, EDGE : EDGE + L] + vec[b : b + 1, D : 2 * D] * n
        stream[w, EDGE : EDGE + L] = mixed
        low = mixed.astype(BF)
        mixed_low[at] = low
        kept[MIXED_T][:, at] = low.T
        if w == WINDOWS - 1:
            keep(b, NORM_C, SCALE_C, MIXED_T)

    def widen(b, w):
        at = slice(w * L, (w + 1) * L)
        if w == 0:
            settle(INNER[b])
            free(b, SLOPE, HIDDEN_T)
            save((b, "inner"), full[INNER[b]], weight_out[3 * b + 1])
        values = mixed_low[at]
        for n in range(FF // D):
            part = slice(n * D, (n + 1) * D)
            pre = dot(values, full[INNER[b]][:, part])
            pre = pre + vec[b : b + 1, 3 * D + n * D : 3 * D + (n + 1) * D]
            value, slope = gelu_both(pre)
            kept[SLOPE][n * ROWS + w * L : n * ROWS + (w + 1) * L] = slope.astype(BF)
            low = value.astype(BF)
            hidden[at, part] = low
            kept[HIDDEN_T][part, at] = low.T
        if w == WINDOWS - 1:
            keep(b, SLOPE, HIDDEN_T)

    def narrow(b, w):
        at = slice(w * L, (w + 1) * L)
        if w == 0:
            settle(OUTER[b])
            free(b, NORM_B, SCALE_B)
            save((b, "outer"), full[OUTER[b]], weight_out[3 * b + 2])
        n, r = norm_parts(dot(hidden[at], full[OUTER[b]][...]))
        kept[NORM_B][at] = n.astype(BF)
        kept[SCALE_B][at] = jnp.broadcast_to(r, (L, 128))
        result = stream[w, EDGE : EDGE + L] + vec[b : b + 1, 2 * D : 3 * D] * n
        if b == 0:
            stream[w, EDGE : EDGE + L] = result
            if w == 0:
                saved((0, LOW_T))
            kept[LOW_T][:, at] = result.astype(BF).T
        else:
            out[at] = result.astype(BF)
        if w == WINDOWS - 1:
            keep(b, NORM_B, SCALE_B)
            if b == 0:
                keep(1, LOW_T)
            else:
                save("out", out, out_ref)

    actions = {
        "Z": g.Z,
        "A": g.A,
        "C": g.C,
        "F": g.F,
        "prep": prepare,
        "vec": vectors,
        "mask": masked,
        "turn": turn,
        "conv": conv,
        "widen": widen,
        "narrow": narrow,
    }
    vec_f[0:16] = jnp.zeros((16, 128), F32)
    vec_f[0:2, 0:SHARE] = vec_in[...].astype(F32)
    vec_own[...] = vec_f[0:16].astype(BF)
    for t in range(count):
        g.own(t)
    for move in loads:
        move.start()
    g.start()
    for name, *where in schedule:
        actions[name](*where)
    for p in range(len(PIECES)):
        g.sent(p)
    for name in saves:
        saved(name)


def forward(vectors, cotangent, mask, weights, embeddings):
    count, n = len(SHAPES), len(PIECES)
    anywhere = pl.BlockSpec(memory_space=pl.ANY)
    held = pl.BlockSpec(memory_space=pltpu.VMEM)
    out_shape = (
        [jax.ShapeDtypeStruct((NDEV * r, w), BF) for r, w in SHAPES[1:]]
        + [jax.ShapeDtypeStruct((ROWS, D), BF), jax.ShapeDtypeStruct((8, NV), F32)]
        + [jax.ShapeDtypeStruct((ROWS, D), BF)]
        + [jax.ShapeDtypeStruct(shape, dtype) for shape, dtype in KEPT * 2]
    )
    return pl.pallas_call(
        functools.partial(forward_kernel, FORWARD),
        out_shape=out_shape,
        in_specs=[held, anywhere, held] + [anywhere] * 4,
        out_specs=[anywhere] * len(out_shape),
        scratch_shapes=[
            *[pltpu.VMEM((NDEV * r, w), BF) for r, w in SHAPES],
            pltpu.VMEM((WINDOWS, L + 2 * EDGE, D), F32),
            pltpu.VMEM((L, KS * D), BF),
            pltpu.VMEM((ROWS, FF), BF),
            pltpu.VMEM((ROWS, D), BF),
            pltpu.VMEM((ROWS, D), BF),
            pltpu.VMEM((NDEV * 16, 128), F32),
            pltpu.VMEM((8, NV), F32),
            pltpu.VMEM((ROWS, D), BF),
            pltpu.VMEM((ROWS, D), BF),
            pltpu.VMEM((KS * D, D), BF),
            pltpu.VMEM((16, 128), BF),
            *[pltpu.VMEM(shape, dtype) for shape, dtype in KEPT],
            pltpu.SemaphoreType.DMA((count,)),
            pltpu.SemaphoreType.DMA((n, 4)),
            pltpu.SemaphoreType.DMA((n, 18)),
            pltpu.SemaphoreType.DMA((2,)),
            pltpu.SemaphoreType.DMA((32,)),
        ],
        compiler_params=pltpu.CompilerParams(
            collective_id=0, has_side_effects=True, vmem_limit_bytes=62 * 2**20
        ),
        name="forward",
    )(vectors, cotangent, mask, *weights, embeddings)


REDUCED = (
    ("o", 1, 0, 512),
    ("i", 1, 0, 2048),
    ("c", 1, 0, 128),
    ("c", 1, 128, 128),
    ("c", 1, 256, 128),
    ("c", 1, 384, 128),
    ("o", 0, 0, 512),
    ("i", 0, 0, 2048),
    ("c", 0, 0, 128),
    ("c", 0, 128, 128),
    ("c", 0, 256, 128),
    ("c", 0, 384, 128),
    ("v", 0, 0, 128),
)
Z_FIRST = (2,)
HEIGHT = {"o": FF // NDEV, "i": D // NDEV, "c": KS * D // NDEV, "v": 16}
NR = len(REDUCED)
LATER = {p: REDUCED.index((k, 1, left, width)) for p, (k, b, left, width) in enumerate(REDUCED) if b == 0 and k != "v"}


def size_of(p):
    kind, _, _, cols = REDUCED[p]
    return HEIGHT[kind], cols


def halves_in(p):
    rows, cols = size_of(p)
    return halves_of((0, rows, 0, cols))


class Reduce:
    def __init__(self, parts, swap, first_in, second_in, from_x, from_y, total, from_z, result,
                 final, outs, send_sem, recv_sem, out_sem, credit):
        self.parts, self.swap = parts, swap
        self.first_in, self.second_in = first_in, second_in
        self.from_x, self.from_y, self.total, self.from_z = from_x, from_y, total, from_z
        self.result, self.final, self.outs = result, final, outs
        self.ended = set()
        self.send_sem, self.recv_sem, self.out_sem, self.credit = send_sem, recv_sem, out_sem, credit
        self.place = x, z, y, c = place()
        self.to_x = device(1 - x, z, y, c)
        self.to_y = device(x, z, 1 - y, c)
        self.to_c = device(x, z, y, 1 - c)
        self.moves, self.live = [], {}

    def start(self):
        meet(neighbours(*self.place))

    def send(self, p, kind, src, dst, target):
        move = pltpu.make_async_remote_copy(
            src_ref=src, dst_ref=dst, send_sem=self.send_sem.at[p, kind],
            recv_sem=self.recv_sem.at[p, kind], device_id=target, device_id_type=MESH)
        move.start()
        self.moves.append(move)
        self.live[p, kind] = move

    def half_of(self, ref, half):
        at, height, left, width = half
        return ref.at[:, pl.ds(at, height), pl.ds(left, width)]

    def column(self, p, ax, ay, half):
        kind, b, left, width = REDUCED[p]
        part = self.parts[kind, b]
        at, height, off, wide = half
        return part.reshape(NX, NZ, NY, 2, *part.shape[2:]).at[
            ax, :, ay, self.place[3], pl.ds(at, height), pl.ds(left + off, wide)
        ]

    def plane(self, p, level):
        kind, b, left, width = REDUCED[p]
        part = self.parts[kind, b]
        return part.reshape(NX, NZ, NY, 2, *part.shape[2:]).at[
            :, level, :, self.place[3], :, pl.ds(left, width)
        ]

    def single(self, p, ax, ay, half):
        kind, b, left, width = REDUCED[p]
        at, height, off, wide = half
        j = (ax * NZ + self.place[1]) * NY + ay
        return self.parts[kind, b].at[j, self.place[3], pl.ds(at, height), pl.ds(left + off, wide)]

    def exchange(self, p):
        x, z, y, c = self.place
        for step in (1, 2, 3):
            self.live[p, 6 + step].wait_recv()
        for ax in range(NX):
            for ay in range(NY):
                part, at = self.spot(p, (ax * NZ + z) * NY + ay)
                acc = part[at].astype(F32)
                for step in range(3):
                    acc = acc + self.from_z[p][step, ax, ay].astype(F32)
                part[at] = acc.astype(BF)
        first, second = halves_in(p)

        def side(ref, half):
            at, height, left, width = half
            return ref.at[0, pl.ds(at, height), pl.ds(left, width)]

        self.send(p, 1, self.single(p, 1 - x, 1 - y, first), self.first_in[p].at[0], self.to_x)
        self.send(p, 2, self.single(p, 1 - x, 1 - y, second), self.second_in[p].at[0], self.to_y)
        self.send(p, 4, self.single(p, x, 1 - y, second), side(self.from_y[p], second), self.to_y)
        self.send(p, 3, self.single(p, 1 - x, y, first), side(self.from_x[p], first), self.to_x)

    def turn_corner(self, p, ax, ay, half, extra, to, kind, target):
        part, at = self.spot(p, (ax * NZ + self.place[1]) * NY + ay, half)
        part[at] = (part[at].astype(F32) + extra[0].astype(F32)).astype(BF)
        row, height, left, width = half
        self.send(p, kind, self.single(p, ax, ay, half), to.at[0, pl.ds(row, height), pl.ds(left, width)], target)

    def finish_level(self, p):
        x, z, y, c = self.place
        for kind in (3, 4, 5, 6):
            self.live[p, kind].wait_recv()
        part, at = self.spot(p, (x * NZ + z) * NY + y)
        return part[at].astype(F32) + self.from_x[p][0].astype(F32) + self.from_y[p][0].astype(F32)

    def spot(self, p, j, half=None):
        kind, b, left, width = REDUCED[p]
        at, height, off, wide = (0, *size_of(p)[:1], 0, width) if half is None else half
        return self.parts[kind, b], (j, self.place[3], pl.ds(at, height), pl.ds(left + off, wide))

    def begin(self, p):
        kind, b, left, width = REDUCED[p]
        if p in LATER:
            pl.semaphore_wait(self.credit.at[LATER[p]], 1)
        other = self.parts[kind, b].at[:, 1 - self.place[3], :, pl.ds(left, width)]
        self.send(p, 0, other, self.swap[p], self.to_c)

    def pair(self, p):
        x, z, y, c = self.place
        swap = self.swap[p]
        self.live[p, 0].wait_recv()

        @pl.loop(0, 16)
        def _(i):
            part, at = self.spot(p, i)
            part[at] = (part[at].astype(F32) + swap[i].astype(F32)).astype(BF)

        if p in LATER.values():
            pl.semaphore_signal(self.credit.at[p], inc=1, device_id=self.to_c, device_id_type=MESH)
        if p in Z_FIRST:
            for step in (1, 2, 3):
                level = (z + step) % NZ
                self.send(p, 6 + step, self.plane(p, level), self.from_z[p].at[step - 1], device(x, level, y, c))
            return
        first, second = halves_in(p)
        half_of = self.half_of
        self.send(p, 1, self.column(p, 1 - x, 1 - y, first), self.first_in[p], self.to_x)
        if second is not None:
            self.send(p, 2, self.column(p, 1 - x, 1 - y, second), self.second_in[p], self.to_y)
            self.send(p, 4, self.column(p, x, 1 - y, second), half_of(self.from_y[p], second), self.to_y)
        self.send(p, 3, self.column(p, 1 - x, y, first), half_of(self.from_x[p], first), self.to_x)

    def add_half(self, p, ax, ay, half, extra):
        @pl.loop(0, NZ)
        def _(i):
            part, at = self.spot(p, (ax * NZ + i) * NY + ay, half)
            part[at] = (part[at].astype(F32) + extra[i].astype(F32)).astype(BF)

    def corner_x(self, p):
        x, z, y, c = self.place
        first, _ = halves_in(p)
        self.live[p, 1].wait_recv()
        if p in Z_FIRST:
            self.turn_corner(p, x, 1 - y, first, self.first_in[p], self.from_y[p], 5, self.to_y)
            return
        self.add_half(p, x, 1 - y, first, self.first_in[p])
        self.send(p, 5, self.column(p, x, 1 - y, first), self.half_of(self.from_y[p], first), self.to_y)

    def corner_y(self, p):
        x, z, y, c = self.place
        _, second = halves_in(p)
        if p in Z_FIRST:
            self.live[p, 2].wait_recv()
            self.turn_corner(p, 1 - x, y, second, self.second_in[p], self.from_x[p], 6, self.to_x)
        elif second is not None:
            self.live[p, 2].wait_recv()
            self.add_half(p, 1 - x, y, second, self.second_in[p])
            self.send(p, 6, self.column(p, 1 - x, y, second), self.half_of(self.from_x[p], second), self.to_x)

    def line(self, p):
        x, z, y, c = self.place
        if p in Z_FIRST:
            self.exchange(p)
            return
        for kind in (3, 4, 5, 6):
            if (p, kind) in self.live:
                self.live[p, kind].wait_recv()

        def summed(i):
            part, at = self.spot(p, (x * NZ + i) * NY + y)
            return (
                part[at].astype(F32)
                + self.from_x[p][i].astype(F32)
                + self.from_y[p][i].astype(F32)
            )

        for step in (1, 2, 3):
            level = (z + step) % NZ
            self.total[p][step - 1] = summed(level).astype(BF)
            self.send(p, 6 + step, self.total[p].at[step - 1], self.from_z[p].at[step - 1], device(x, level, y, c))
        self.result[p][...] = summed(z)

    def end(self, p):
        if p in Z_FIRST:
            acc = self.finish_level(p)
        else:
            for step in (1, 2, 3):
                self.live[p, 6 + step].wait_recv()
            acc = self.result[p][...]
            for step in range(3):
                acc = acc + self.from_z[p][step].astype(F32)
        kind, b, left, width = REDUCED[p]
        if kind == "v":
            self.final["v"][...] = acc[0:2, 0:SHARE]
        else:
            self.final[kind][:, b, left : left + width] = acc
        self.ended.add(p)
        if all(q in self.ended for q in range(NR) if REDUCED[q][0] == kind):
            move = pltpu.make_async_copy(self.final[kind], self.outs[kind], self.out_sem.at[p])
            move.start()
            self.live[p, "out"] = move

    def close(self):
        for move in self.moves:
            move.wait_send()
        for p in range(NR):
            if (p, "out") in self.live:
                self.live[p, "out"].wait()


def contract_cols(left, right):
    return lax.dot_general(left, right, (((1,), (1,)), ((), ())), preferred_element_type=F32)


def norm_back(n, e):
    return e - jnp.mean(e, axis=-1, keepdims=True) - n * jnp.mean(e * n, axis=-1, keepdims=True)


TAPS = 3

BACKWARD = (
    ("prep",), ("b1", 1, 1), ("b1", 1, 0), ("do", 1, 1), ("do", 1, 0), ("begin", 0), ("b2", 1, 1),
    ("b2", 1, 0), ("b2", 1, 2), ("b2", 1, 3), ("pair", 0), ("di", 1), ("begin", 1), ("b3", 1, 1),
    ("b3", 1, 0), ("b5", 1, 1), ("cor1", 0), ("pair", 1), ("b5", 1, 0), ("cor2", 0), ("dk", 1, 1),
    ("begin", 4), ("begin", 5), ("dk", 1, 0), ("pair", 4), ("begin", 2), ("b6", 1, 1), ("pair", 5),
    ("pair", 2), ("begin", 3), ("b6", 1, 0), ("b1", 0, 1), ("cor2", 1), ("cor1", 1), ("b1", 0, 0),
    ("cor2", 4), ("pair", 3), ("slope",), ("line", 0), ("b2", 0, 1), ("b2", 0, 0), ("cor1", 4),
    ("b2", 0, 3), ("cor2", 5), ("cor1", 5), ("do", 0, 1), ("do", 0, 0), ("begin", 6), ("b2", 0, 2),
    ("di", 0), ("begin", 7), ("pair", 6), ("pair", 7), ("line", 1), ("b3", 0, 1), ("b3", 0, 0),
    ("line", 5), ("b5", 0, 1), ("cor2", 6), ("b5", 0, 0), ("dk", 0, 0), ("cor1", 6), ("dk", 0, 1),
    ("cor1", 3), ("cor2", 3), ("begin", 10), ("line", 4), ("cor2", 7), ("vg",), ("cor1", 7),
    ("pair", 10), ("begin", 8), ("line", 6), ("begin", 12), ("line", 3), ("pair", 8), ("b6", 0, 1),
    ("line", 7), ("cor1", 10), ("end", 0), ("begin", 9), ("cor2", 10), ("pair", 12), ("begin", 11),
    ("end", 5), ("pair", 9), ("b6", 0, 0), ("cor2", 12), ("cor1", 8), ("cor2", 8), ("cor1", 12),
    ("line", 10), ("cor2", 9), ("cor1", 9), ("pair", 11), ("line", 8), ("line", 12), ("end", 3),
    ("end", 7), ("end", 4), ("cor2", 11), ("cor1", 11), ("line", 9), ("end", 1), ("end", 6),
    ("end", 10), ("line", 2), ("line", 11), ("end", 8), ("end", 12), ("cor2", 2), ("cor1", 2),
    ("end", 2), ("end", 9), ("end", 11),
)


def backward_kernel(schedule, *refs):
    weights_hbm, refs = refs[:6], refs[6:]
    (vec_hbm, cot_hbm), refs = refs[:2], refs[2:]
    kept_hbm, refs = (refs[:NK], refs[NK : 2 * NK]), refs[2 * NK :]
    outs, refs = dict(zip("cio", refs[:3])), refs[3:]
    outs["v"], emb_grad_out, refs = refs[0], refs[1], refs[2:]
    part_o1, part_i1, part_c1, part_o0, part_i0, vec_part, refs = *refs[:6], refs[6:]
    swaps, refs = refs[: NR - len(LATER)], refs[NR - len(LATER) :]
    lists = []
    for _ in range(7):
        lists.append(refs[:NR])
        refs = refs[NR:]
    first_in, second_in, from_x, from_y, total, from_z, result = lists
    final, refs = dict(zip("ciov", refs[:4])), refs[4:]
    (conv_w, inner_w, outer_w, big, hidden_t, norm_b, scale_b, mixed_t, norm_c, scale_c, low_t,
     grad, frame, temp, cols, vec, vec_grad, tile), refs = refs[:18], refs[18:]
    send_sem, recv_sem, out_sem, credit, load_sem = refs
    view = big.reshape(16, 2, KS * D // NDEV, D)
    parts = {
        ("o", 1): part_o1, ("i", 1): part_i1, ("c", 1): part_c1,
        ("o", 0): part_o0, ("i", 0): part_i0, ("c", 0): view, ("v", 0): vec_part,
    }
    conv_flat = {1: part_c1.reshape(KS * D, D), 0: big}
    own = [p for p in range(NR) if p not in LATER]
    swap = {p: swaps[own.index(LATER.get(p, p))] for p in range(NR)}
    r = Reduce(parts, swap, first_in, second_in, from_x, from_y, total, from_z, result, final, outs,
               send_sem, recv_sem, out_sem, credit)
    loading = {}
    met = set()

    def load(name, src, dst):
        move = pltpu.make_async_copy(src, dst, load_sem.at[len(loading)])
        move.start()
        loading[name] = move

    def need(*names):
        for name in names:
            if name not in met:
                met.add(name)
                loading[name].wait()

    def load_block(b, *names):
        table = {
            "norm_b": (kept_hbm[b][NORM_B], norm_b),
            "scale_b": (kept_hbm[b][SCALE_B], scale_b),
            "outer": (weights_hbm[3 * b + 2], outer_w),
            "slope": (kept_hbm[b][SLOPE], big.at[pl.ds(0, 4 * ROWS)]),
            "hidden": (kept_hbm[b][HIDDEN_T], hidden_t),
            "mixed": (kept_hbm[b][MIXED_T], mixed_t),
            "inner": (weights_hbm[3 * b + 1], inner_w),
            "norm_c": (kept_hbm[b][NORM_C], norm_c),
            "scale_c": (kept_hbm[b][SCALE_C], scale_c),
            "low": (kept_hbm[b][LOW_T], low_t),
            "kernel": (weights_hbm[3 * b], conv_w),
        }
        for name in names:
            load((b, name), *table[name])

    counts = {}

    def next_block(b, pieces, *names):
        counts[b, names] = counts.get((b, names), 0) + 1
        if b and counts[b, names] == pieces:
            load_block(0, *names)
        return counts[b, names] == pieces

    def rows_at(w):
        return slice(w * L, (w + 1) * L)

    def prepare():
        vec_grad[...] = jnp.zeros_like(vec_grad)
        edge = jnp.zeros((EDGE, D), F32)
        for w in range(WINDOWS):
            frame[w, 0:EDGE] = edge
            frame[w, EDGE + L : EDGE + L + EDGE] = edge
        need("cot")
        grad[...] = temp[...].astype(F32)
        need("vec")

    def add_vec(b, at, values):
        width = values.shape[-1]
        vec_grad[b : b + 1, at : at + width] += jnp.sum(values, axis=0, keepdims=True)

    def branch_back(b, w):
        need((b, "norm_b"), (b, "scale_b"))
        at = rows_at(w)
        n = norm_b[at].astype(F32)
        incoming = grad[at]
        add_vec(b, 2 * D, incoming * n)
        scale = jnp.concatenate([scale_b[at]] * (D // 128), axis=1)
        temp[at] = (scale * norm_back(n, vec[b : b + 1, 2 * D : 3 * D] * incoming)).astype(BF)
        next_block(b, WINDOWS, "norm_b", "scale_b")

    def hidden_back(b, n):
        need((b, "outer"), (b, "slope"))
        at = slice(n * ROWS, (n + 1) * ROWS)
        grad_hidden = contract_cols(temp[...], outer_w[n * D : (n + 1) * D])
        grad_pre = (big[at].astype(F32) * grad_hidden).astype(BF)
        big[at] = grad_pre
        add_vec(b, 3 * D + n * D, grad_pre.astype(F32))
        next_block(b, FF // D, "outer")

    def outer_grad(b, h):
        need((b, "hidden"))
        at = slice(h * 256, (h + 1) * 256)
        out = dot(hidden_t[...], temp[:, at]).astype(BF)
        parts["o", b][:, :, :, at] = out.reshape(16, 2, FF // NDEV, 256)
        next_block(b, 2, "hidden")

    def inner_grad(b):
        need((b, "mixed"))
        for n in range(FF // D):
            out = dot(mixed_t[...], big[n * ROWS : (n + 1) * ROWS]).astype(BF)
            parts["i", b][:, :, :, n * D : (n + 1) * D] = out.reshape(16, 2, D // NDEV, D)
        next_block(b, 1, "mixed")

    def mixed_back(b, w):
        need((b, "inner"))
        acc = grad[rows_at(w)]
        for n in range(FF // D):
            at = slice(n * ROWS + w * L, n * ROWS + (w + 1) * L)
            acc = acc + contract_cols(big[at], inner_w[:, n * D : (n + 1) * D])
        grad[rows_at(w)] = acc
        next_block(b, WINDOWS, "inner")

    def conv_back(b, w):
        need((b, "norm_c"), (b, "scale_c"))
        at = rows_at(w)
        n = norm_c[at].astype(F32)
        incoming = grad[at]
        add_vec(b, D, incoming * n)
        out = scale_c[at].astype(F32) * norm_back(n, vec[b : b + 1, D : 2 * D] * incoming)
        out = out.astype(BF).astype(F32)
        add_vec(b, 0, out)
        frame[w, EDGE : EDGE + L] = out
        next_block(b, WINDOWS, "norm_c", "scale_c")

    def kernel_grad(b, h):
        need((b, "low"))
        at = slice(h * 256, (h + 1) * 256)
        for k in range(KS):
            first = EDGE - (k - KS // 2) * DILATIONS[b]
            for w in range(WINDOWS):
                temp[rows_at(w), 0:256] = frame[w, first : first + L, at].astype(BF)
            conv_flat[b][k * D : (k + 1) * D, at] = dot(low_t[...], temp[:, 0:256]).astype(BF)
        next_block(b, 2, "low")

    def stream_back(b, w):
        need((b, "kernel"))
        acc = grad[rows_at(w)]
        for group in range(KS // TAPS):
            for i in range(TAPS):
                first = EDGE - (group * TAPS + i - KS // 2) * DILATIONS[b]
                cols[:, i * D : (i + 1) * D] = frame[w, first : first + L].astype(BF)
            acc = acc + dot(cols[...], conv_w[group * TAPS * D : (group + 1) * TAPS * D])
        if b:
            grad[rows_at(w)] = acc
        else:
            norm_b[rows_at(w)] = acc.astype(BF)
        if next_block(b, WINDOWS, "kernel") and b == 0:
            load("out", norm_b, emb_grad_out)

    def vector_grads():
        spread, pick = selectors()
        tile[...] = jnp.zeros_like(tile)
        for b in range(2):
            rows = (pick * vec_grad[b : b + 1]).astype(BF)
            tile[pl.ds(b, NDEV, stride=16)] = contract_cols(rows, spread)
        vec_part[...] = tile[...].astype(BF).reshape(16, 2, 16, 128)

    actions = {
        "begin": r.begin,
        "pair": r.pair,
        "cor1": r.corner_x,
        "cor2": r.corner_y,
        "line": r.line,
        "end": r.end,
        "prep": prepare,
        "b1": branch_back,
        "b2": hidden_back,
        "do": outer_grad,
        "di": inner_grad,
        "b3": mixed_back,
        "b5": conv_back,
        "dk": kernel_grad,
        "b6": stream_back,
        "vg": vector_grads,
        "slope": lambda: load_block(0, "slope"),
    }
    load("cot", cot_hbm, temp)
    load("vec", vec_hbm, vec)
    load_block(1, "norm_b", "scale_b", "outer", "slope", "hidden", "mixed", "inner", "norm_c", "scale_c", "low", "kernel")
    r.start()
    for name, *where in schedule:
        actions[name](*where)
    r.close()
    need("out")


def backward(weights, vec, cotangent, kept):
    anywhere = pl.BlockSpec(memory_space=pl.ANY)
    finals = [(rows, 2, cols) for rows, cols in SHAPES[1:4]] + [(2, SHARE)]
    out_shape = [jax.ShapeDtypeStruct(shape, F32) for shape in finals]
    out_shape += [jax.ShapeDtypeStruct((ROWS, D), BF)]

    def halves(which):
        spaces = []
        for p in range(NR):
            half = halves_in(p)[which]
            half = (0, 16, 0, 128) if half is None else half
            spaces.append(pltpu.VMEM((1 if p in Z_FIRST else NZ, half[1], half[3]), BF))
        return spaces

    def space(lead, dtype=BF, members=range(NR), early=None):
        leads = [early if p in Z_FIRST and early is not None else lead for p in members]
        return [pltpu.VMEM((*before, *size_of(p)), dtype) for p, before in zip(members, leads)]

    def whole_part(t):
        return pltpu.VMEM((16, 2, *SHAPES[t]), BF)

    args = (*weights, vec, cotangent, *kept)
    return pl.pallas_call(
        functools.partial(backward_kernel, BACKWARD),
        out_shape=out_shape,
        in_specs=[anywhere] * len(args),
        out_specs=[anywhere] * len(out_shape),
        scratch_shapes=[
            whole_part(3), whole_part(2), whole_part(1), whole_part(3), whole_part(2), whole_part(0),
            *space((16,), members=[p for p in range(NR) if p not in LATER]),
            *halves(0),
            *halves(1),
            *space((NZ,), early=(1,)),
            *space((NZ,), early=(1,)),
            *space((3,), early=(1,)),
            *space((3,), early=(3, NX, NY)),
            *space((), F32),
            *[pltpu.VMEM(shape, F32) for shape in finals],
            pltpu.VMEM((KS * D, D), BF),
            pltpu.VMEM((D, FF), BF),
            pltpu.VMEM((FF, D), BF),
            pltpu.VMEM((KS * D, D), BF),
            pltpu.VMEM((FF, ROWS), BF),
            pltpu.VMEM((ROWS, D), BF),
            pltpu.VMEM((ROWS, 128), F32),
            pltpu.VMEM((D, ROWS), BF),
            pltpu.VMEM((ROWS, D), BF),
            pltpu.VMEM((ROWS, D), BF),
            pltpu.VMEM((D, ROWS), BF),
            pltpu.VMEM((ROWS, D), F32),
            pltpu.VMEM((WINDOWS, L + 2 * EDGE, D), F32),
            pltpu.VMEM((ROWS, D), BF),
            pltpu.VMEM((L, TAPS * D), BF),
            pltpu.VMEM((8, NV), F32),
            pltpu.VMEM((8, NV), F32),
            pltpu.VMEM((NDEV * 16, 128), F32),
            pltpu.SemaphoreType.DMA((NR, 10)),
            pltpu.SemaphoreType.DMA((NR, 10)),
            pltpu.SemaphoreType.DMA((NR,)),
            pltpu.SemaphoreType.REGULAR((NR,)),
            pltpu.SemaphoreType.DMA((32,)),
        ],
        compiler_params=pltpu.CompilerParams(
            collective_id=1, has_side_effects=True, vmem_limit_bytes=63 * 2**20
        ),
        name="backward",
    )(*args)


def finish_kernel(count, *refs):
    for source, target in zip(refs[:count], refs[count:]):
        target[...] = source[...]


def finish(members):
    steps = 4

    def block(member):
        if member.shape[0] < 16:
            return pl.BlockSpec(member.shape, lambda i: (0,) * member.ndim)
        shape = (member.shape[0] // steps, *member.shape[1:])
        return pl.BlockSpec(shape, lambda i: (i,) + (0,) * (member.ndim - 1))

    blocks = [block(member) for member in members]
    return pl.pallas_call(
        functools.partial(finish_kernel, len(members)),
        grid=(steps,),
        out_shape=[jax.ShapeDtypeStruct(v.shape, v.dtype) for v in members],
        in_specs=blocks,
        out_specs=blocks,
        name="finish",
    )(*members)


def normalize(values):
    centered = values - jnp.mean(values, axis=-1, keepdims=True)
    return centered * lax.rsqrt(jnp.mean(centered * centered, axis=-1, keepdims=True) + 1e-05)


def conv_branch(values):
    return normalize(jax.nn.gelu(values))


def contract_rows(left, right):
    return lax.dot_general(left, right, (((0,), (0,)), ((), ())), preferred_element_type=F32)


def columns(stream_low, dilation):
    windows = stream_low.shape[0] // L
    framed = stream_low.reshape(windows, L, D)
    margin = KS // 2 * dilation
    padded = jnp.pad(framed, ((0, 0), (margin, margin), (0, 0)))
    stacked = jnp.concatenate(
        [padded[:, tap_id * dilation : tap_id * dilation + L] for tap_id in range(KS)], axis=2
    )
    return stacked.reshape(windows * L, KS * D)


def fold_back(grad_cols, dilation):
    windows = grad_cols.shape[0] // L
    framed = grad_cols.reshape(windows, L, KS, D)
    margin = KS // 2 * dilation
    total = jnp.zeros((windows, L + 2 * margin, D), F32)
    for tap_id in range(KS):
        before = tap_id * dilation
        total = total + jnp.pad(
            framed[:, :, tap_id], ((0, 0), (before, 2 * margin - before), (0, 0))
        )
    return total[:, margin : margin + L].reshape(windows * L, D)


def block_forward(stream, weights, dilation):
    conv_mat, inner_mat, outer_mat, vector = weights
    conv_bias = vector[:D]
    gain_conv = vector[D : 2 * D]
    gain_ffn = vector[2 * D : 3 * D]
    bias_ffn = vector[3 * D :]
    stream_low = stream.astype(BF)
    pre_conv = (
        jnp.dot(columns(stream_low, dilation), conv_mat, preferred_element_type=F32) + conv_bias
    )
    mixed = stream + gain_conv * conv_branch(pre_conv)
    mixed_low = mixed.astype(BF)
    pre_ffn = jnp.dot(mixed_low, inner_mat, preferred_element_type=F32) + bias_ffn
    hidden_low = jax.nn.gelu(pre_ffn).astype(BF)
    branch = jnp.dot(hidden_low, outer_mat, preferred_element_type=F32)
    result = mixed + gain_ffn * normalize(branch)
    return (result, (stream_low, pre_conv, mixed_low, pre_ffn, hidden_low, branch))


def block_backward(grad_out, saved, weights, dilation):
    conv_mat, inner_mat, outer_mat, vector = weights
    gain_conv = vector[D : 2 * D]
    gain_ffn = vector[2 * D : 3 * D]
    stream_low, pre_conv, mixed_low, pre_ffn, hidden_low, branch = saved
    normed_branch, branch_back = jax.vjp(normalize, branch)
    grad_gain_ffn = jnp.sum(grad_out * normed_branch, axis=0)
    grad_branch = branch_back(grad_out * gain_ffn)[0].astype(BF)
    grad_outer = contract_rows(hidden_low, grad_branch)
    grad_hidden = contract_cols(grad_branch, outer_mat)
    _, gelu_back = jax.vjp(jax.nn.gelu, pre_ffn)
    grad_pre_ffn = gelu_back(grad_hidden)[0].astype(BF)
    grad_bias_ffn = jnp.sum(grad_pre_ffn.astype(F32), axis=0)
    grad_inner = contract_rows(mixed_low, grad_pre_ffn)
    grad_mixed = grad_out + contract_cols(grad_pre_ffn, inner_mat)
    normed_conv, conv_back = jax.vjp(conv_branch, pre_conv)
    grad_gain_conv = jnp.sum(grad_mixed * normed_conv, axis=0)
    grad_pre_conv = conv_back(grad_mixed * gain_conv)[0].astype(BF)
    grad_conv_bias = jnp.sum(grad_pre_conv.astype(F32), axis=0)
    grad_kernel = contract_rows(columns(stream_low, dilation), grad_pre_conv)
    grad_stream = grad_mixed + fold_back(contract_cols(grad_pre_conv, conv_mat), dilation)
    vector_grad = jnp.concatenate([grad_conv_bias, grad_gain_conv, grad_gain_ffn, grad_bias_ffn])
    return (grad_stream, (grad_kernel, grad_inner, grad_outer, vector_grad))


def gather_any(conv_weight, inner_weight, outer_weight, vectors):
    def whole(member):
        return lax.all_gather(member, ("dp", "fsdp"), axis=1, tiled=True)

    conv, inner, outer, vector = (
        whole(member) for member in (conv_weight, inner_weight, outer_weight, vectors)
    )
    return [
        (
            conv[b].reshape(KS * D, D),
            inner[b].reshape(D, FF),
            outer[b].reshape(FF, D),
            vector[b].astype(F32),
        )
        for b in range(2)
    ]


def reduce_any(grads, width):
    count_dp = lax.axis_size("dp")
    count_fsdp = lax.axis_size("fsdp")

    def settle(first, second):
        member = jnp.stack([first.reshape(-1), second.reshape(-1)]).astype(BF)
        member = member.reshape(2, count_dp, count_fsdp, -1)
        spread = lax.all_to_all(member, "fsdp", split_axis=2, concat_axis=2, tiled=True)
        partial = jnp.sum(spread.astype(F32), axis=2, keepdims=True).astype(BF)
        settled = lax.all_to_all(partial, "dp", split_axis=1, concat_axis=1, tiled=True)
        return jnp.sum(settled.astype(F32), axis=(1, 2))

    return tuple(settle(first, second) for first, second in zip(*grads))


def body_here(embeddings, conv_weight, inner_weight, outer_weight, vectors, cotangent, row_mask):
    weights = (
        conv_weight.reshape(2, -1, D),
        inner_weight.reshape(2, -1, FF),
        outer_weight.reshape(2, -1, D),
    )
    mask = row_mask.reshape(ROWS // 128, 128)
    result = forward(vectors, cotangent, mask, weights, embeddings)
    weights, output, vec, incoming, kept = result[:6], result[6], result[7], result[8], result[9:]
    *grads, vec_grad, emb_grad = finish((output, *backward(weights, vec, incoming, kept)))
    output, *grads = grads
    conv, inner, outer = (member.transpose(1, 0, 2).reshape(2, -1) for member in grads)
    return output, emb_grad, conv, inner, outer, vec_grad


def body_any(embeddings, conv_weight, inner_weight, outer_weight, vectors, cotangent, row_mask):
    weights = gather_any(conv_weight, inner_weight, outer_weight, vectors)
    stream = embeddings.astype(F32)
    saved = []
    for b in range(2):
        stream, kept = block_forward(stream, weights[b], DILATIONS[b])
        saved.append(kept)
    output = stream.astype(BF)
    grad_stream = cotangent.astype(F32) * row_mask.astype(F32)[:, None]
    grads = [None, None]
    for b in (1, 0):
        grad_stream, grads[b] = block_backward(grad_stream, saved[b], weights[b], DILATIONS[b])
    return (output, grad_stream.astype(BF), *reduce_any(grads, vectors.shape[1]))


def solution(mesh):
    rows = P(("dp", "fsdp"), None)
    flat = P(None, ("dp", "fsdp"))
    here = mesh.shape["dp"] == NX and mesh.shape["fsdp"] == NZ * NY * 2
    return jax.shard_map(
        body_here if here else body_any,
        mesh=mesh,
        in_specs=(rows, flat, flat, flat, flat, rows, P(("dp", "fsdp"))),
        out_specs=(rows, rows, flat, flat, flat, flat),
        check_vma=False,
    )
```

```python
import functools

import jax
import jax.numpy as jnp
import numpy as np
from jax import lax
from jax.experimental import pallas as pl
from jax.experimental.pallas import tpu as pltpu
from jax.sharding import PartitionSpec as P

MESH = pl.DeviceIdType.MESH
BF = jnp.bfloat16
NX, NZ, NY = 2, 4, 2
NDEV = 32


def place():
    across = lax.axis_index("dp")
    index = lax.axis_index("fsdp")
    return across, index // (2 * NY), (index // 2) % NY, index % 2


def device(x, z, y, c):
    return (x, (z * NY + y) * 2 + c)


def shard(x, z, y, c):
    return x * (NZ * NY * 2) + (z * NY + y) * 2 + c


def meet(peers):
    barrier = pltpu.get_barrier_semaphore()
    for peer in peers:
        pl.semaphore_signal(barrier, inc=1, device_id=peer, device_id_type=MESH)
    pl.semaphore_wait(barrier, len(peers))


def neighbours(x, z, y, c):
    return [
        device(1 - x, z, y, c),
        device(x, z, 1 - y, c),
        device(x, z, y, 1 - c),
        device(x, (z + 1) % NZ, y, c),
        device(x, (z + 2) % NZ, y, c),
        device(x, (z + 3) % NZ, y, c),
    ]

def halves_of(rect):
    at, rows, left, cols = rect
    if rows >= 32:
        first = (rows // 2 + 15) // 16 * 16
        return (at, first, left, cols), (at + first, rows - first, left, cols)
    if cols >= 256:
        return (at, rows, left, cols // 2), (at, rows, left + cols // 2, cols // 2)
    return rect, None


class Gather:
    def __init__(self, shapes, pieces, own_refs, full_refs, own_sem, send_sem, recv_sem):
        self.shapes, self.pieces = shapes, pieces
        self.own_refs, self.full_refs = own_refs, full_refs
        self.own_sem, self.send_sem, self.recv_sem = own_sem, send_sem, recv_sem
        self.place = x, z, y, c = place()
        self.to_x = device(1 - x, z, y, c)
        self.to_y = device(x, z, 1 - y, c)
        self.to_c = device(x, z, y, 1 - c)
        self.near = z + 1 - 2 * (z % 2)
        self.away = 2 - 2 * (z // 2)
        self.moves, self.totals = {}, {}

    def start(self):
        meet(neighbours(*self.place))

    def levels(self, which):
        z = self.place[1]
        return {
            "own": (z, 1),
            "near": (self.near, 1),
            "away": (self.away, 2),
            "pair": (2 * (z // 2), 2),
            "all": (0, NZ),
        }[which]

    def part(self, p, ax, level, ay, c, half=None):
        t, rect = self.pieces[p]
        at, height, left, width = rect if half is None else half
        rows, cols = self.shapes[t]
        low, count = level
        view = self.full_refs[t].reshape(NX, NZ, NY, 2, rows, cols)
        return view.at[ax, pl.ds(low, count), ay, c, pl.ds(at, height), pl.ds(left, width)]

    def send(self, p, part, kind, slot, target, amount):
        self.totals[p, kind] = self.totals.get((p, kind), 0) + amount
        pltpu.make_async_remote_copy(
            src_ref=part, dst_ref=part, send_sem=self.send_sem.at[p, kind],
            recv_sem=self.recv_sem.at[p, slot], device_id=target, device_id_type=MESH).start()

    def arrive(self, p, part, slot):
        pltpu.make_async_copy(part, part, self.recv_sem.at[p, slot]).wait()

    def amount(self, p, half=None):
        rect = self.pieces[p][1] if half is None else half
        return rect[1] * rect[3]

    def own(self, t):
        x, z, y, c = self.place
        rows, cols = self.shapes[t]
        view = self.full_refs[t].reshape(NX, NZ, NY, 2, rows, cols)
        self.moves[t] = pltpu.make_async_copy(self.own_refs[t], view.at[x, z, y, c], self.own_sem.at[t])
        self.moves[t].start()

    def over(self, p, which, slot, count):
        x, z, y, c = self.place
        part = self.part(p, x, self.levels(which), y, c)
        self.send(p, part, 1, 4 + slot, self.to_x, count * self.amount(p))
        self.send(p, part, 2, 7 + slot, self.to_y, count * self.amount(p))

    def column(self, p, ax, ay, slot):
        part = self.part(p, ax, self.levels("all"), ay, self.place[3])
        self.send(p, part, 3, 14 + slot, self.to_c, NZ * self.amount(p))

    def plane(self, p, level):
        rows, cols = self.shapes[self.pieces[p][0]]
        at, height, left, width = self.pieces[p][1]
        view = self.full_refs[self.pieces[p][0]].reshape(NX, NZ, NY, 2, rows, cols)
        return view.at[:, level, :, self.place[3], pl.ds(at, height), pl.ds(left, width)]

    def other_plane(self, p, level):
        rows, cols = self.shapes[self.pieces[p][0]]
        at, height, left, width = self.pieces[p][1]
        view = self.full_refs[self.pieces[p][0]].reshape(NX, NZ, NY, 2, rows, cols)
        return view.at[:, level, :, 1 - self.place[3], pl.ds(at, height), pl.ds(left, width)]

    def Z(self, p):
        x, z, y, c = self.place
        t = self.pieces[p][0]
        if t in self.moves:
            self.moves.pop(t).wait()
        if p in Z_LAST:
            self.over(p, "own", 0, 1)
            return
        part = self.part(p, x, self.levels("own"), y, c)
        for step in (1, 2, 3):
            self.send(p, part, 0, z, device(x, (z + step) % NZ, y, c), self.amount(p))
        self.over(p, "own", 0, 1)

    def A(self, p, k):
        x, z, y, c = self.place
        if p in Z_LAST:
            for step in (1, 2, 3):
                level = (z + step) % NZ
                self.arrive(p, self.plane(p, level), level)
                self.send(p, self.plane(p, level), 3, 14 + step, self.to_c, 4 * self.amount(p))
        elif k == 0:
            self.arrive(p, self.part(p, x, self.levels("near"), y, c), self.near)
            self.over(p, "near", 1, 1)
        else:
            for i in range(2):
                self.arrive(p, self.part(p, x, (self.away + i, 1), y, c), self.away + i)
            self.over(p, "away", 2, 2)
            self.column(p, x, y, 0)

    def C(self, p, k):
        x, z, y, c = self.place
        first, second = halves_of(self.pieces[p][1])
        if p in Z_LAST:
            self.arrive(p, self.part(p, 1 - x, self.levels("own"), y, c), 4)
            half = self.part(p, 1 - x, self.levels("own"), y, c, first)
            self.send(p, half, 2, 10, self.to_y, self.amount(p, first))
            self.arrive(p, self.part(p, x, self.levels("own"), 1 - y, c), 7)
            half = self.part(p, x, self.levels("own"), 1 - y, c, second)
            self.send(p, half, 1, 12, self.to_x, self.amount(p, second))
            return
        which = "away" if k else "pair"
        for slot, part_levels in (((2, "away"),) if k else ((0, "own"), (1, "near"))):
            self.arrive(p, self.part(p, 1 - x, self.levels(part_levels), y, c), 4 + slot)
        half = self.part(p, 1 - x, self.levels(which), y, c, first)
        self.send(p, half, 2, 10 + k, self.to_y, 2 * self.amount(p, first))
        for slot, part_levels in (((2, "away"),) if k else ((0, "own"), (1, "near"))):
            self.arrive(p, self.part(p, x, self.levels(part_levels), 1 - y, c), 7 + slot)
        if second is not None:
            half = self.part(p, x, self.levels(which), 1 - y, c, second)
            self.send(p, half, 1, 12 + k, self.to_x, 2 * self.amount(p, second))
        if k:
            self.column(p, 1 - x, y, 1)
            self.column(p, x, 1 - y, 2)

    def F(self, p):
        x, z, y, c = self.place
        first, second = halves_of(self.pieces[p][1])
        if p in Z_LAST:
            self.arrive(p, self.part(p, 1 - x, self.levels("own"), 1 - y, c, first), 10)
            self.arrive(p, self.part(p, 1 - x, self.levels("own"), 1 - y, c, second), 12)
            for step in (1, 2, 3):
                self.send(p, self.plane(p, z), 0, z, device(x, (z + step) % NZ, y, c), 4 * self.amount(p))
            self.send(p, self.plane(p, z), 3, 14, self.to_c, 4 * self.amount(p))
            return
        for k, which in enumerate(("pair", "away")):
            self.arrive(p, self.part(p, 1 - x, self.levels(which), 1 - y, c, first), 10 + k)
            if second is not None:
                self.arrive(p, self.part(p, 1 - x, self.levels(which), 1 - y, c, second), 12 + k)
        self.column(p, 1 - x, 1 - y, 3)

    def settle(self, p):
        x, z, y, c = self.place
        if p in Z_LAST:
            for step in range(NZ):
                self.arrive(p, self.other_plane(p, (z + step) % NZ), 14 + step)
            return
        for slot, (ax, ay) in enumerate(((x, y), (1 - x, y), (x, 1 - y), (1 - x, 1 - y))):
            self.arrive(p, self.part(p, ax, self.levels("all"), ay, 1 - c), 14 + slot)

    def sent(self, p):
        t, (at, rows, left, cols) = self.pieces[p]
        for kind in range(4):
            total = self.totals[p, kind]
            part = self.full_refs[t].at[pl.ds(0, total // cols), pl.ds(left, cols)]
            pltpu.make_async_copy(part, part, self.send_sem.at[p, kind]).wait()


D = 512
FF = 2048
KS = 9
L = 512
NV = 3 * D + FF
DILATIONS = (2, 16)
F32 = jnp.float32
EDGE = 64
WINDOWS = 2
ROWS = WINDOWS * L
SHARE = NV // NDEV
SHAPES = ((16, 128),) + ((KS * D // NDEV, D), (D // NDEV, FF), (FF // NDEV, D)) * 2
VEC, CONV, INNER, OUTER = 0, (1, 4), (2, 5), (3, 6)


def selectors():
    column = lax.broadcasted_iota(jnp.int32, (NDEV, NV), 1)
    first = lax.broadcasted_iota(jnp.int32, (NDEV, NV), 0) * SHARE
    inside = (column >= first) & (column < first + SHARE)
    pick = jnp.where(inside, 1.0, 0.0).astype(F32)
    offset = jnp.sum(jnp.where(inside, column - first, 0), axis=0, keepdims=True)
    lane = lax.broadcasted_iota(jnp.int32, (128, NV), 0)
    return jnp.where(lane == offset, 1.0, 0.0).astype(BF), pick


def dot(left, right):
    return jnp.dot(left, right, preferred_element_type=F32)


def gelu_both(v):
    square = v * v
    half = 0.5 + 0.5 * jnp.tanh(v * (0.7978845608028654 + 0.035677408136300125 * square))
    value = v * half
    steep = 1.5957691216057308 + 0.21406444881780075 * square
    return value, half + value * ((1.0 - half) * steep)


def norm_parts(v):
    centered = v - jnp.mean(v, axis=-1, keepdims=True)
    r = lax.rsqrt(jnp.mean(centered * centered, axis=-1, keepdims=True) + 1e-05)
    return centered * r, r


def whole(t):
    rows, cols = SHAPES[t]
    return (0, rows, 0, cols)


PIECES = (
    (VEC, whole(VEC)),
    (CONV[0], (0, 80, 0, D)),
    (CONV[0], (80, 64, 0, D)),
    (INNER[0], whole(INNER[0])),
    (OUTER[0], whole(OUTER[0])),
    (CONV[1], (0, 32, 0, D)),
    (CONV[1], (32, 64, 0, D)),
    (CONV[1], (96, 48, 0, D)),
    (INNER[1], whole(INNER[1])),
    (OUTER[1], whole(OUTER[1])),
)
Z_LAST = (5,)


FORWARD = (
    ("Z", 0), ("Z", 2), ("Z", 5), ("Z", 1), ("Z", 3), ("C", 5, 0), ("A", 0, 0), ("Z", 8),
    ("A", 2, 0), ("Z", 4), ("Z", 7), ("C", 0, 0), ("prep",), ("C", 2, 0), ("A", 1, 0), ("Z", 6),
    ("A", 0, 1), ("A", 3, 0), ("C", 1, 0), ("C", 0, 1), ("A", 2, 1), ("C", 3, 0), ("A", 8, 0),
    ("C", 2, 1), ("F", 0), ("A", 1, 1), ("A", 7, 0), ("A", 4, 0), ("A", 3, 1), ("C", 1, 1),
    ("C", 4, 0), ("C", 3, 1), ("A", 4, 1), ("F", 5), ("F", 2), ("A", 7, 1), ("A", 6, 0), ("vec",),
    ("Z", 9), ("F", 1), ("mask",), ("conv", 0, 0), ("turn", 0), ("A", 6, 1), ("F", 3), ("C", 7, 0),
    ("C", 4, 1), ("conv", 0, 1), ("C", 6, 0), ("C", 7, 1), ("widen", 0, 0), ("C", 6, 1),
    ("A", 8, 1), ("C", 8, 0), ("F", 4), ("widen", 0, 1), ("A", 5, 0), ("F", 7), ("A", 9, 0),
    ("narrow", 0, 0), ("F", 6), ("narrow", 0, 1), ("C", 8, 1), ("A", 9, 1), ("conv", 1, 0),
    ("C", 9, 0), ("turn", 1), ("F", 8), ("conv", 1, 1), ("C", 9, 1), ("widen", 1, 0), ("F", 9),
    ("widen", 1, 1), ("narrow", 1, 0), ("narrow", 1, 1),
)

KEPT = (
    ((ROWS, D), BF),
    ((ROWS, D), BF),
    ((D, ROWS), BF),
    ((D, ROWS), BF),
    ((4 * ROWS, D), BF),
    ((FF, ROWS), BF),
    ((ROWS, D), BF),
    ((ROWS, 128), F32),
)
NORM_C, SCALE_C, MIXED_T, LOW_T, SLOPE, HIDDEN_T, NORM_B, SCALE_B = range(8)
NK = len(KEPT)


def forward_kernel(schedule, *refs):
    count = len(SHAPES)
    vec_in, cot_ref, mask_in, refs = refs[0], refs[1], refs[2], refs[3:]
    weight_in, emb_ref, refs = refs[:3], refs[3], refs[4:]
    weight_out, refs = refs[:6], refs[6:]
    out_ref, vec_out, cot_out, refs = refs[0], refs[1], refs[2], refs[3:]
    kept_out, refs = (refs[:NK], refs[NK : 2 * NK]), refs[2 * NK :]
    full, refs = refs[:count], refs[count:]
    (stream, cols, hidden, mixed_low, emb, vec_f, vec, cot, out, turned, vec_own), refs = (
        refs[:11],
        refs[11:],
    )
    own_refs = [vec_own] + [ref.at[b] for b in range(2) for ref in weight_in]
    kept, refs = refs[:NK], refs[NK:]
    own_sem, send_sem, recv_sem, local_sem, save_sem = refs
    g = Gather(SHAPES, PIECES, own_refs, full, own_sem, send_sem, recv_sem)

    loads = [
        pltpu.make_async_copy(src, dst, local_sem.at[i])
        for i, (src, dst) in enumerate(((emb_ref, emb), (cot_ref, cot)))
    ]
    saves = {}

    def save(name, src, dst):
        move = pltpu.make_async_copy(src, dst, save_sem.at[len(saves)])
        move.start()
        saves[name] = move

    waited = set()

    def saved(name):
        if name in saves and name not in waited:
            saves[name].wait()
            waited.add(name)

    settled = set()

    def settle(t):
        if t in settled:
            return
        settled.add(t)
        for p, (tensor, _) in enumerate(PIECES):
            if tensor == t:
                g.settle(p)

    def keep(b, *members):
        for i in members:
            save((b, i), kept[i], kept_out[b][i])

    def free(b, *members):
        if b == 1:
            for i in members:
                saved((0, i))

    def prepare():
        loads[0].wait()
        edge = jnp.zeros((EDGE, D), F32)
        for w in range(WINDOWS):
            stream[w, 0:EDGE] = edge
            stream[w, EDGE + L : EDGE + L + EDGE] = edge
            stream[w, EDGE : EDGE + L] = emb[w * L : (w + 1) * L].astype(F32)
        kept[LOW_T][...] = emb[...].T
        keep(0, LOW_T)

    def vectors():
        settle(VEC)
        spread, pick = selectors()
        vec_f[...] = full[VEC][...].astype(F32)
        for b in range(2):
            rows = vec_f[pl.ds(b, NDEV, stride=16)].astype(BF)
            vec[b : b + 1] = jnp.sum(dot(rows, spread) * pick, axis=0, keepdims=True)
        save("vec", vec, vec_out)

    def masked():
        loads[1].wait()
        for i in range(ROWS // 128):
            line = jnp.broadcast_to(mask_in[i : i + 1].astype(F32), (128, 128)).T
            for j in range(D // 128):
                spot = (slice(i * 128, (i + 1) * 128), slice(j * 128, (j + 1) * 128))
                cot[spot] = (cot[spot].astype(F32) * line).astype(BF)
        save("cot", cot, cot_out)

    def turn(b):
        settle(CONV[b])
        if b == 1:
            saved((0, "kernel"))
        for k in range(KS):
            turned[k * D : (k + 1) * D] = full[CONV[b]][k * D : (k + 1) * D].T
        save((b, "kernel"), turned, weight_out[3 * b])

    def conv(b, w):
        at = slice(w * L, (w + 1) * L)
        if w == 0:
            settle(CONV[b])
            free(b, NORM_C, SCALE_C, MIXED_T)
        for k in range(KS):
            first = EDGE + (k - KS // 2) * DILATIONS[b]
            cols[:, k * D : (k + 1) * D] = stream[w, first : first + L].astype(BF)
        pre = dot(cols[...], full[CONV[b]][...]) + vec[b : b + 1, 0:D]
        value, slope = gelu_both(pre)
        n, r = norm_parts(value)
        kept[NORM_C][at] = n.astype(BF)
        kept[SCALE_C][at] = (slope * r).astype(BF)
        mixed = stream[w, EDGE : EDGE + L] + vec[b : b + 1, D : 2 * D] * n
        stream[w, EDGE : EDGE + L] = mixed
        low = mixed.astype(BF)
        mixed_low[at] = low
        kept[MIXED_T][:, at] = low.T
        if w == WINDOWS - 1:
            keep(b, NORM_C, SCALE_C, MIXED_T)

    def widen(b, w):
        at = slice(w * L, (w + 1) * L)
        if w == 0:
            settle(INNER[b])
            free(b, SLOPE, HIDDEN_T)
            save((b, "inner"), full[INNER[b]], weight_out[3 * b + 1])
        values = mixed_low[at]
        for n in range(FF // D):
            part = slice(n * D, (n + 1) * D)
            pre = dot(values, full[INNER[b]][:, part])
            pre = pre + vec[b : b + 1, 3 * D + n * D : 3 * D + (n + 1) * D]
            value, slope = gelu_both(pre)
            kept[SLOPE][n * ROWS + w * L : n * ROWS + (w + 1) * L] = slope.astype(BF)
            low = value.astype(BF)
            hidden[at, part] = low
            kept[HIDDEN_T][part, at] = low.T
        if w == WINDOWS - 1:
            keep(b, SLOPE, HIDDEN_T)

    def narrow(b, w):
        at = slice(w * L, (w + 1) * L)
        if w == 0:
            settle(OUTER[b])
            free(b, NORM_B, SCALE_B)
            save((b, "outer"), full[OUTER[b]], weight_out[3 * b + 2])
        n, r = norm_parts(dot(hidden[at], full[OUTER[b]][...]))
        kept[NORM_B][at] = n.astype(BF)
        kept[SCALE_B][at] = jnp.broadcast_to(r, (L, 128))
        result = stream[w, EDGE : EDGE + L] + vec[b : b + 1, 2 * D : 3 * D] * n
        if b == 0:
            stream[w, EDGE : EDGE + L] = result
            if w == 0:
                saved((0, LOW_T))
            kept[LOW_T][:, at] = result.astype(BF).T
        else:
            out[at] = result.astype(BF)
        if w == WINDOWS - 1:
            keep(b, NORM_B, SCALE_B)
            if b == 0:
                keep(1, LOW_T)
            else:
                save("out", out, out_ref)

    actions = {
        "Z": g.Z,
        "A": g.A,
        "C": g.C,
        "F": g.F,
        "prep": prepare,
        "vec": vectors,
        "mask": masked,
        "turn": turn,
        "conv": conv,
        "widen": widen,
        "narrow": narrow,
    }
    vec_f[0:16] = jnp.zeros((16, 128), F32)
    vec_f[0:2, 0:SHARE] = vec_in[...].astype(F32)
    vec_own[...] = vec_f[0:16].astype(BF)
    for t in range(count):
        g.own(t)
    for move in loads:
        move.start()
    g.start()
    for name, *where in schedule:
        actions[name](*where)
    for p in range(len(PIECES)):
        g.sent(p)
    for name in saves:
        saved(name)


def forward(vectors, cotangent, mask, weights, embeddings):
    count, n = len(SHAPES), len(PIECES)
    anywhere = pl.BlockSpec(memory_space=pl.ANY)
    held = pl.BlockSpec(memory_space=pltpu.VMEM)
    out_shape = (
        [jax.ShapeDtypeStruct((NDEV * r, w), BF) for r, w in SHAPES[1:]]
        + [jax.ShapeDtypeStruct((ROWS, D), BF), jax.ShapeDtypeStruct((8, NV), F32)]
        + [jax.ShapeDtypeStruct((ROWS, D), BF)]
        + [jax.ShapeDtypeStruct(shape, dtype) for shape, dtype in KEPT * 2]
    )
    return pl.pallas_call(
        functools.partial(forward_kernel, FORWARD),
        out_shape=out_shape,
        in_specs=[held, anywhere, held] + [anywhere] * 4,
        out_specs=[anywhere] * len(out_shape),
        scratch_shapes=[
            *[pltpu.VMEM((NDEV * r, w), BF) for r, w in SHAPES],
            pltpu.VMEM((WINDOWS, L + 2 * EDGE, D), F32),
            pltpu.VMEM((L, KS * D), BF),
            pltpu.VMEM((ROWS, FF), BF),
            pltpu.VMEM((ROWS, D), BF),
            pltpu.VMEM((ROWS, D), BF),
            pltpu.VMEM((NDEV * 16, 128), F32),
            pltpu.VMEM((8, NV), F32),
            pltpu.VMEM((ROWS, D), BF),
            pltpu.VMEM((ROWS, D), BF),
            pltpu.VMEM((KS * D, D), BF),
            pltpu.VMEM((16, 128), BF),
            *[pltpu.VMEM(shape, dtype) for shape, dtype in KEPT],
            pltpu.SemaphoreType.DMA((count,)),
            pltpu.SemaphoreType.DMA((n, 4)),
            pltpu.SemaphoreType.DMA((n, 18)),
            pltpu.SemaphoreType.DMA((2,)),
            pltpu.SemaphoreType.DMA((32,)),
        ],
        compiler_params=pltpu.CompilerParams(
            collective_id=0, has_side_effects=True, vmem_limit_bytes=62 * 2**20
        ),
        name="forward",
    )(vectors, cotangent, mask, *weights, embeddings)


REDUCED = (
    ("o", 1, 0, 512),
    ("i", 1, 0, 2048),
    ("c", 1, 0, 128),
    ("c", 1, 128, 128),
    ("c", 1, 256, 128),
    ("c", 1, 384, 128),
    ("o", 0, 0, 512),
    ("i", 0, 0, 2048),
    ("c", 0, 0, 128),
    ("c", 0, 128, 128),
    ("c", 0, 256, 128),
    ("c", 0, 384, 128),
    ("v", 0, 0, 128),
)
Z_FIRST = (2,)
HEIGHT = {"o": FF // NDEV, "i": D // NDEV, "c": KS * D // NDEV, "v": 16}
NR = len(REDUCED)
LATER = {p: REDUCED.index((k, 1, left, width)) for p, (k, b, left, width) in enumerate(REDUCED) if b == 0 and k != "v"}


def size_of(p):
    kind, _, _, cols = REDUCED[p]
    return HEIGHT[kind], cols


def halves_in(p):
    rows, cols = size_of(p)
    return halves_of((0, rows, 0, cols))


class Reduce:
    def __init__(self, parts, swap, first_in, second_in, from_x, from_y, total, from_z, result,
                 final, outs, send_sem, recv_sem, out_sem, credit):
        self.parts, self.swap = parts, swap
        self.first_in, self.second_in = first_in, second_in
        self.from_x, self.from_y, self.total, self.from_z = from_x, from_y, total, from_z
        self.result, self.final, self.outs = result, final, outs
        self.ended = set()
        self.send_sem, self.recv_sem, self.out_sem, self.credit = send_sem, recv_sem, out_sem, credit
        self.place = x, z, y, c = place()
        self.to_x = device(1 - x, z, y, c)
        self.to_y = device(x, z, 1 - y, c)
        self.to_c = device(x, z, y, 1 - c)
        self.moves, self.live = [], {}

    def start(self):
        meet(neighbours(*self.place))

    def send(self, p, kind, src, dst, target):
        move = pltpu.make_async_remote_copy(
            src_ref=src, dst_ref=dst, send_sem=self.send_sem.at[p, kind],
            recv_sem=self.recv_sem.at[p, kind], device_id=target, device_id_type=MESH)
        move.start()
        self.moves.append(move)
        self.live[p, kind] = move

    def half_of(self, ref, half):
        at, height, left, width = half
        return ref.at[:, pl.ds(at, height), pl.ds(left, width)]

    def column(self, p, ax, ay, half):
        kind, b, left, width = REDUCED[p]
        part = self.parts[kind, b]
        at, height, off, wide = half
        return part.reshape(NX, NZ, NY, 2, *part.shape[2:]).at[
            ax, :, ay, self.place[3], pl.ds(at, height), pl.ds(left + off, wide)
        ]

    def plane(self, p, level):
        kind, b, left, width = REDUCED[p]
        part = self.parts[kind, b]
        return part.reshape(NX, NZ, NY, 2, *part.shape[2:]).at[
            :, level, :, self.place[3], :, pl.ds(left, width)
        ]

    def single(self, p, ax, ay, half):
        kind, b, left, width = REDUCED[p]
        at, height, off, wide = half
        j = (ax * NZ + self.place[1]) * NY + ay
        return self.parts[kind, b].at[j, self.place[3], pl.ds(at, height), pl.ds(left + off, wide)]

    def exchange(self, p):
        x, z, y, c = self.place
        for step in (1, 2, 3):
            self.live[p, 6 + step].wait_recv()
        for ax in range(NX):
            for ay in range(NY):
                part, at = self.spot(p, (ax * NZ + z) * NY + ay)
                acc = part[at].astype(F32)
                for step in range(3):
                    acc = acc + self.from_z[p][step, ax, ay].astype(F32)
                part[at] = acc.astype(BF)
        first, second = halves_in(p)

        def side(ref, half):
            at, height, left, width = half
            return ref.at[0, pl.ds(at, height), pl.ds(left, width)]

        self.send(p, 1, self.single(p, 1 - x, 1 - y, first), self.first_in[p].at[0], self.to_x)
        self.send(p, 2, self.single(p, 1 - x, 1 - y, second), self.second_in[p].at[0], self.to_y)
        self.send(p, 4, self.single(p, x, 1 - y, second), side(self.from_y[p], second), self.to_y)
        self.send(p, 3, self.single(p, 1 - x, y, first), side(self.from_x[p], first), self.to_x)

    def turn_corner(self, p, ax, ay, half, extra, to, kind, target):
        part, at = self.spot(p, (ax * NZ + self.place[1]) * NY + ay, half)
        part[at] = (part[at].astype(F32) + extra[0].astype(F32)).astype(BF)
        row, height, left, width = half
        self.send(p, kind, self.single(p, ax, ay, half), to.at[0, pl.ds(row, height), pl.ds(left, width)], target)

    def finish_level(self, p):
        x, z, y, c = self.place
        for kind in (3, 4, 5, 6):
            self.live[p, kind].wait_recv()
        part, at = self.spot(p, (x * NZ + z) * NY + y)
        return part[at].astype(F32) + self.from_x[p][0].astype(F32) + self.from_y[p][0].astype(F32)

    def spot(self, p, j, half=None):
        kind, b, left, width = REDUCED[p]
        at, height, off, wide = (0, *size_of(p)[:1], 0, width) if half is None else half
        return self.parts[kind, b], (j, self.place[3], pl.ds(at, height), pl.ds(left + off, wide))

    def begin(self, p):
        kind, b, left, width = REDUCED[p]
        if p in LATER:
            pl.semaphore_wait(self.credit.at[LATER[p]], 1)
        other = self.parts[kind, b].at[:, 1 - self.place[3], :, pl.ds(left, width)]
        self.send(p, 0, other, self.swap[p], self.to_c)

    def pair(self, p):
        x, z, y, c = self.place
        swap = self.swap[p]
        self.live[p, 0].wait_recv()

        @pl.loop(0, 16)
        def _(i):
            part, at = self.spot(p, i)
            part[at] = (part[at].astype(F32) + swap[i].astype(F32)).astype(BF)

        if p in LATER.values():
            pl.semaphore_signal(self.credit.at[p], inc=1, device_id=self.to_c, device_id_type=MESH)
        if p in Z_FIRST:
            for step in (1, 2, 3):
                level = (z + step) % NZ
                self.send(p, 6 + step, self.plane(p, level), self.from_z[p].at[step - 1], device(x, level, y, c))
            return
        first, second = halves_in(p)
        half_of = self.half_of
        self.send(p, 1, self.column(p, 1 - x, 1 - y, first), self.first_in[p], self.to_x)
        if second is not None:
            self.send(p, 2, self.column(p, 1 - x, 1 - y, second), self.second_in[p], self.to_y)
            self.send(p, 4, self.column(p, x, 1 - y, second), half_of(self.from_y[p], second), self.to_y)
        self.send(p, 3, self.column(p, 1 - x, y, first), half_of(self.from_x[p], first), self.to_x)

    def add_half(self, p, ax, ay, half, extra):
        @pl.loop(0, NZ)
        def _(i):
            part, at = self.spot(p, (ax * NZ + i) * NY + ay, half)
            part[at] = (part[at].astype(F32) + extra[i].astype(F32)).astype(BF)

    def corner_x(self, p):
        x, z, y, c = self.place
        first, _ = halves_in(p)
        self.live[p, 1].wait_recv()
        if p in Z_FIRST:
            self.turn_corner(p, x, 1 - y, first, self.first_in[p], self.from_y[p], 5, self.to_y)
            return
        self.add_half(p, x, 1 - y, first, self.first_in[p])
        self.send(p, 5, self.column(p, x, 1 - y, first), self.half_of(self.from_y[p], first), self.to_y)

    def corner_y(self, p):
        x, z, y, c = self.place
        _, second = halves_in(p)
        if p in Z_FIRST:
            self.live[p, 2].wait_recv()
            self.turn_corner(p, 1 - x, y, second, self.second_in[p], self.from_x[p], 6, self.to_x)
        elif second is not None:
            self.live[p, 2].wait_recv()
            self.add_half(p, 1 - x, y, second, self.second_in[p])
            self.send(p, 6, self.column(p, 1 - x, y, second), self.half_of(self.from_x[p], second), self.to_x)

    def line(self, p):
        x, z, y, c = self.place
        if p in Z_FIRST:
            self.exchange(p)
            return
        for kind in (3, 4, 5, 6):
            if (p, kind) in self.live:
                self.live[p, kind].wait_recv()

        def summed(i):
            part, at = self.spot(p, (x * NZ + i) * NY + y)
            return (
                part[at].astype(F32)
                + self.from_x[p][i].astype(F32)
                + self.from_y[p][i].astype(F32)
            )

        for step in (1, 2, 3):
            level = (z + step) % NZ
            self.total[p][step - 1] = summed(level).astype(BF)
            self.send(p, 6 + step, self.total[p].at[step - 1], self.from_z[p].at[step - 1], device(x, level, y, c))
        self.result[p][...] = summed(z)

    def end(self, p):
        if p in Z_FIRST:
            acc = self.finish_level(p)
        else:
            for step in (1, 2, 3):
                self.live[p, 6 + step].wait_recv()
            acc = self.result[p][...]
            for step in range(3):
                acc = acc + self.from_z[p][step].astype(F32)
        kind, b, left, width = REDUCED[p]
        if kind == "v":
            self.final["v"][...] = acc[0:2, 0:SHARE]
        else:
            self.final[kind][:, b, left : left + width] = acc
        self.ended.add(p)
        if all(q in self.ended for q in range(NR) if REDUCED[q][0] == kind):
            move = pltpu.make_async_copy(self.final[kind], self.outs[kind], self.out_sem.at[p])
            move.start()
            self.live[p, "out"] = move

    def close(self):
        for move in self.moves:
            move.wait_send()
        for p in range(NR):
            if (p, "out") in self.live:
                self.live[p, "out"].wait()


def contract_cols(left, right):
    return lax.dot_general(left, right, (((1,), (1,)), ((), ())), preferred_element_type=F32)


def norm_back(n, e):
    return e - jnp.mean(e, axis=-1, keepdims=True) - n * jnp.mean(e * n, axis=-1, keepdims=True)


TAPS = 3

BACKWARD = (
    ("prep",), ("b1", 1, 1), ("b1", 1, 0), ("do", 1, 0), ("do", 1, 1), ("begin", 0), ("b2", 1, 1),
    ("b2", 1, 3), ("b2", 1, 2), ("b2", 1, 0), ("pair", 0), ("di", 1), ("begin", 1), ("b3", 1, 1),
    ("b3", 1, 0), ("cor2", 0), ("cor1", 0), ("b5", 1, 0), ("pair", 1), ("b5", 1, 1), ("dk", 1, 1),
    ("begin", 4), ("dk", 1, 0), ("begin", 3), ("line", 0), ("pair", 4), ("begin", 5), ("b6", 1, 1),
    ("pair", 3), ("begin", 2), ("pair", 5), ("slope",), ("cor2", 1), ("b6", 1, 0), ("cor1", 1),
    ("pair", 2), ("b1", 0, 1), ("b1", 0, 0), ("b2", 0, 1), ("cor2", 4), ("cor1", 4), ("do", 0, 1),
    ("b2", 0, 0), ("cor1", 3), ("do", 0, 0), ("begin", 6), ("b2", 0, 2), ("cor1", 5), ("cor2", 3),
    ("cor2", 5), ("b2", 0, 3), ("di", 0), ("pair", 6), ("begin", 7), ("line", 4), ("line", 1),
    ("b3", 0, 0), ("b5", 0, 0), ("line", 3), ("b3", 0, 1), ("pair", 7), ("end", 0), ("cor2", 6),
    ("b5", 0, 1), ("cor1", 6), ("dk", 0, 1), ("vg",), ("line", 5), ("begin", 10), ("begin", 12),
    ("cor1", 7), ("dk", 0, 0), ("pair", 12), ("begin", 9), ("cor2", 7), ("pair", 10), ("b6", 0, 0),
    ("line", 6), ("pair", 9), ("line", 7), ("cor2", 12), ("cor1", 10), ("begin", 8), ("end", 4),
    ("cor2", 10), ("pair", 8), ("b6", 0, 1), ("cor2", 9), ("end", 1), ("cor1", 9), ("begin", 11),
    ("line", 10), ("cor1", 12), ("cor1", 8), ("cor2", 8), ("pair", 11), ("line", 9), ("line", 8),
    ("cor2", 11), ("cor1", 11), ("end", 3), ("line", 12), ("end", 5), ("line", 2), ("end", 7),
    ("line", 11), ("end", 10), ("cor1", 2), ("cor2", 2), ("end", 6), ("end", 8), ("end", 2),
    ("end", 9), ("end", 12), ("end", 11),
)


def backward_kernel(schedule, *refs):
    weights_hbm, refs = refs[:6], refs[6:]
    (vec_hbm, cot_hbm), refs = refs[:2], refs[2:]
    kept_hbm, refs = (refs[:NK], refs[NK : 2 * NK]), refs[2 * NK :]
    outs, refs = dict(zip("cio", refs[:3])), refs[3:]
    outs["v"], emb_grad_out, refs = refs[0], refs[1], refs[2:]
    part_o1, part_i1, part_c1, part_o0, part_i0, vec_part, refs = *refs[:6], refs[6:]
    swaps, refs = refs[: NR - len(LATER)], refs[NR - len(LATER) :]
    lists = []
    for _ in range(7):
        lists.append(refs[:NR])
        refs = refs[NR:]
    first_in, second_in, from_x, from_y, total, from_z, result = lists
    final, refs = dict(zip("ciov", refs[:4])), refs[4:]
    (conv_w, inner_w, outer_w, big, hidden_t, norm_b, scale_b, mixed_t, norm_c, scale_c, low_t,
     grad, frame, temp, cols, vec, vec_grad, tile), refs = refs[:18], refs[18:]
    send_sem, recv_sem, out_sem, credit, load_sem = refs
    view = big.reshape(16, 2, KS * D // NDEV, D)
    parts = {
        ("o", 1): part_o1, ("i", 1): part_i1, ("c", 1): part_c1,
        ("o", 0): part_o0, ("i", 0): part_i0, ("c", 0): view, ("v", 0): vec_part,
    }
    conv_flat = {1: part_c1.reshape(KS * D, D), 0: big}
    own = [p for p in range(NR) if p not in LATER]
    swap = {p: swaps[own.index(LATER.get(p, p))] for p in range(NR)}
    r = Reduce(parts, swap, first_in, second_in, from_x, from_y, total, from_z, result, final, outs,
               send_sem, recv_sem, out_sem, credit)
    loading = {}
    met = set()

    def load(name, src, dst):
        move = pltpu.make_async_copy(src, dst, load_sem.at[len(loading)])
        move.start()
        loading[name] = move

    def need(*names):
        for name in names:
            if name not in met:
                met.add(name)
                loading[name].wait()

    def load_block(b, *names):
        table = {
            "norm_b": (kept_hbm[b][NORM_B], norm_b),
            "scale_b": (kept_hbm[b][SCALE_B], scale_b),
            "outer": (weights_hbm[3 * b + 2], outer_w),
            "slope": (kept_hbm[b][SLOPE], big.at[pl.ds(0, 4 * ROWS)]),
            "hidden": (kept_hbm[b][HIDDEN_T], hidden_t),
            "mixed": (kept_hbm[b][MIXED_T], mixed_t),
            "inner": (weights_hbm[3 * b + 1], inner_w),
            "norm_c": (kept_hbm[b][NORM_C], norm_c),
            "scale_c": (kept_hbm[b][SCALE_C], scale_c),
            "low": (kept_hbm[b][LOW_T], low_t),
            "kernel": (weights_hbm[3 * b], conv_w),
        }
        for name in names:
            load((b, name), *table[name])

    counts = {}

    def next_block(b, pieces, *names):
        counts[b, names] = counts.get((b, names), 0) + 1
        if b and counts[b, names] == pieces:
            load_block(0, *names)
        return counts[b, names] == pieces

    def rows_at(w):
        return slice(w * L, (w + 1) * L)

    def prepare():
        vec_grad[...] = jnp.zeros_like(vec_grad)
        edge = jnp.zeros((EDGE, D), F32)
        for w in range(WINDOWS):
            frame[w, 0:EDGE] = edge
            frame[w, EDGE + L : EDGE + L + EDGE] = edge
        need("cot")
        grad[...] = temp[...].astype(F32)
        need("vec")

    def add_vec(b, at, values):
        width = values.shape[-1]
        vec_grad[b : b + 1, at : at + width] += jnp.sum(values, axis=0, keepdims=True)

    def branch_back(b, w):
        need((b, "norm_b"), (b, "scale_b"))
        at = rows_at(w)
        n = norm_b[at].astype(F32)
        incoming = grad[at]
        add_vec(b, 2 * D, incoming * n)
        scale = jnp.concatenate([scale_b[at]] * (D // 128), axis=1)
        temp[at] = (scale * norm_back(n, vec[b : b + 1, 2 * D : 3 * D] * incoming)).astype(BF)
        next_block(b, WINDOWS, "norm_b", "scale_b")

    def hidden_back(b, n):
        need((b, "outer"), (b, "slope"))
        at = slice(n * ROWS, (n + 1) * ROWS)
        grad_hidden = contract_cols(temp[...], outer_w[n * D : (n + 1) * D])
        grad_pre = (big[at].astype(F32) * grad_hidden).astype(BF)
        big[at] = grad_pre
        add_vec(b, 3 * D + n * D, grad_pre.astype(F32))
        next_block(b, FF // D, "outer")

    def outer_grad(b, h):
        need((b, "hidden"))
        at = slice(h * 256, (h + 1) * 256)
        out = dot(hidden_t[...], temp[:, at]).astype(BF)
        parts["o", b][:, :, :, at] = out.reshape(16, 2, FF // NDEV, 256)
        next_block(b, 2, "hidden")

    def inner_grad(b):
        need((b, "mixed"))
        for n in range(FF // D):
            out = dot(mixed_t[...], big[n * ROWS : (n + 1) * ROWS]).astype(BF)
            parts["i", b][:, :, :, n * D : (n + 1) * D] = out.reshape(16, 2, D // NDEV, D)
        next_block(b, 1, "mixed")

    def mixed_back(b, w):
        need((b, "inner"))
        acc = grad[rows_at(w)]
        for n in range(FF // D):
            at = slice(n * ROWS + w * L, n * ROWS + (w + 1) * L)
            acc = acc + contract_cols(big[at], inner_w[:, n * D : (n + 1) * D])
        grad[rows_at(w)] = acc
        next_block(b, WINDOWS, "inner")

    def conv_back(b, w):
        need((b, "norm_c"), (b, "scale_c"))
        at = rows_at(w)
        n = norm_c[at].astype(F32)
        incoming = grad[at]
        add_vec(b, D, incoming * n)
        out = scale_c[at].astype(F32) * norm_back(n, vec[b : b + 1, D : 2 * D] * incoming)
        out = out.astype(BF).astype(F32)
        add_vec(b, 0, out)
        frame[w, EDGE : EDGE + L] = out
        next_block(b, WINDOWS, "norm_c", "scale_c")

    def kernel_grad(b, h):
        need((b, "low"))
        at = slice(h * 256, (h + 1) * 256)
        for k in range(KS):
            first = EDGE - (k - KS // 2) * DILATIONS[b]
            for w in range(WINDOWS):
                temp[rows_at(w), 0:256] = frame[w, first : first + L, at].astype(BF)
            conv_flat[b][k * D : (k + 1) * D, at] = dot(low_t[...], temp[:, 0:256]).astype(BF)
        next_block(b, 2, "low")

    def stream_back(b, w):
        need((b, "kernel"))
        acc = grad[rows_at(w)]
        for group in range(KS // TAPS):
            for i in range(TAPS):
                first = EDGE - (group * TAPS + i - KS // 2) * DILATIONS[b]
                cols[:, i * D : (i + 1) * D] = frame[w, first : first + L].astype(BF)
            acc = acc + dot(cols[...], conv_w[group * TAPS * D : (group + 1) * TAPS * D])
        if b:
            grad[rows_at(w)] = acc
        else:
            norm_b[rows_at(w)] = acc.astype(BF)
        if next_block(b, WINDOWS, "kernel") and b == 0:
            load("out", norm_b, emb_grad_out)

    def vector_grads():
        spread, pick = selectors()
        tile[...] = jnp.zeros_like(tile)
        for b in range(2):
            rows = (pick * vec_grad[b : b + 1]).astype(BF)
            tile[pl.ds(b, NDEV, stride=16)] = contract_cols(rows, spread)
        vec_part[...] = tile[...].astype(BF).reshape(16, 2, 16, 128)

    actions = {
        "begin": r.begin,
        "pair": r.pair,
        "cor1": r.corner_x,
        "cor2": r.corner_y,
        "line": r.line,
        "end": r.end,
        "prep": prepare,
        "b1": branch_back,
        "b2": hidden_back,
        "do": outer_grad,
        "di": inner_grad,
        "b3": mixed_back,
        "b5": conv_back,
        "dk": kernel_grad,
        "b6": stream_back,
        "vg": vector_grads,
        "slope": lambda: load_block(0, "slope"),
    }
    load("cot", cot_hbm, temp)
    load("vec", vec_hbm, vec)
    load_block(1, "norm_b", "scale_b", "outer", "slope", "hidden", "mixed", "inner", "norm_c", "scale_c", "low", "kernel")
    r.start()
    for name, *where in schedule:
        actions[name](*where)
    r.close()
    need("out")


def backward(weights, vec, cotangent, kept):
    anywhere = pl.BlockSpec(memory_space=pl.ANY)
    finals = [(rows, 2, cols) for rows, cols in SHAPES[1:4]] + [(2, SHARE)]
    out_shape = [jax.ShapeDtypeStruct(shape, F32) for shape in finals]
    out_shape += [jax.ShapeDtypeStruct((ROWS, D), BF)]

    def halves(which):
        spaces = []
        for p in range(NR):
            half = halves_in(p)[which]
            half = (0, 16, 0, 128) if half is None else half
            spaces.append(pltpu.VMEM((1 if p in Z_FIRST else NZ, half[1], half[3]), BF))
        return spaces

    def space(lead, dtype=BF, members=range(NR), early=None):
        leads = [early if p in Z_FIRST and early is not None else lead for p in members]
        return [pltpu.VMEM((*before, *size_of(p)), dtype) for p, before in zip(members, leads)]

    def whole_part(t):
        return pltpu.VMEM((16, 2, *SHAPES[t]), BF)

    args = (*weights, vec, cotangent, *kept)
    return pl.pallas_call(
        functools.partial(backward_kernel, BACKWARD),
        out_shape=out_shape,
        in_specs=[anywhere] * len(args),
        out_specs=[anywhere] * len(out_shape),
        scratch_shapes=[
            whole_part(3), whole_part(2), whole_part(1), whole_part(3), whole_part(2), whole_part(0),
            *space((16,), members=[p for p in range(NR) if p not in LATER]),
            *halves(0),
            *halves(1),
            *space((NZ,), early=(1,)),
            *space((NZ,), early=(1,)),
            *space((3,), early=(1,)),
            *space((3,), early=(3, NX, NY)),
            *space((), F32),
            *[pltpu.VMEM(shape, F32) for shape in finals],
            pltpu.VMEM((KS * D, D), BF),
            pltpu.VMEM((D, FF), BF),
            pltpu.VMEM((FF, D), BF),
            pltpu.VMEM((KS * D, D), BF),
            pltpu.VMEM((FF, ROWS), BF),
            pltpu.VMEM((ROWS, D), BF),
            pltpu.VMEM((ROWS, 128), F32),
            pltpu.VMEM((D, ROWS), BF),
            pltpu.VMEM((ROWS, D), BF),
            pltpu.VMEM((ROWS, D), BF),
            pltpu.VMEM((D, ROWS), BF),
            pltpu.VMEM((ROWS, D), F32),
            pltpu.VMEM((WINDOWS, L + 2 * EDGE, D), F32),
            pltpu.VMEM((ROWS, D), BF),
            pltpu.VMEM((L, TAPS * D), BF),
            pltpu.VMEM((8, NV), F32),
            pltpu.VMEM((8, NV), F32),
            pltpu.VMEM((NDEV * 16, 128), F32),
            pltpu.SemaphoreType.DMA((NR, 10)),
            pltpu.SemaphoreType.DMA((NR, 10)),
            pltpu.SemaphoreType.DMA((NR,)),
            pltpu.SemaphoreType.REGULAR((NR,)),
            pltpu.SemaphoreType.DMA((32,)),
        ],
        compiler_params=pltpu.CompilerParams(
            collective_id=1, has_side_effects=True, vmem_limit_bytes=63 * 2**20
        ),
        name="backward",
    )(*args)


def finish_kernel(count, *refs):
    for source, target in zip(refs[:count], refs[count:]):
        target[...] = source[...]


def finish(members):
    steps = 2

    def block(member):
        if member.shape[0] < 16:
            return pl.BlockSpec(member.shape, lambda i: (0,) * member.ndim)
        shape = (member.shape[0] // steps, *member.shape[1:])
        return pl.BlockSpec(shape, lambda i: (i,) + (0,) * (member.ndim - 1))

    blocks = [block(member) for member in members]
    return pl.pallas_call(
        functools.partial(finish_kernel, len(members)),
        grid=(steps,),
        out_shape=[jax.ShapeDtypeStruct(v.shape, v.dtype) for v in members],
        in_specs=blocks,
        out_specs=blocks,
        name="finish",
    )(*members)


def normalize(values):
    centered = values - jnp.mean(values, axis=-1, keepdims=True)
    return centered * lax.rsqrt(jnp.mean(centered * centered, axis=-1, keepdims=True) + 1e-05)


def conv_branch(values):
    return normalize(jax.nn.gelu(values))


def contract_rows(left, right):
    return lax.dot_general(left, right, (((0,), (0,)), ((), ())), preferred_element_type=F32)


def columns(stream_low, dilation):
    windows = stream_low.shape[0] // L
    framed = stream_low.reshape(windows, L, D)
    margin = KS // 2 * dilation
    padded = jnp.pad(framed, ((0, 0), (margin, margin), (0, 0)))
    stacked = jnp.concatenate(
        [padded[:, tap_id * dilation : tap_id * dilation + L] for tap_id in range(KS)], axis=2
    )
    return stacked.reshape(windows * L, KS * D)


def fold_back(grad_cols, dilation):
    windows = grad_cols.shape[0] // L
    framed = grad_cols.reshape(windows, L, KS, D)
    margin = KS // 2 * dilation
    total = jnp.zeros((windows, L + 2 * margin, D), F32)
    for tap_id in range(KS):
        before = tap_id * dilation
        total = total + jnp.pad(
            framed[:, :, tap_id], ((0, 0), (before, 2 * margin - before), (0, 0))
        )
    return total[:, margin : margin + L].reshape(windows * L, D)


def block_forward(stream, weights, dilation):
    conv_mat, inner_mat, outer_mat, vector = weights
    conv_bias = vector[:D]
    gain_conv = vector[D : 2 * D]
    gain_ffn = vector[2 * D : 3 * D]
    bias_ffn = vector[3 * D :]
    stream_low = stream.astype(BF)
    pre_conv = (
        jnp.dot(columns(stream_low, dilation), conv_mat, preferred_element_type=F32) + conv_bias
    )
    mixed = stream + gain_conv * conv_branch(pre_conv)
    mixed_low = mixed.astype(BF)
    pre_ffn = jnp.dot(mixed_low, inner_mat, preferred_element_type=F32) + bias_ffn
    hidden_low = jax.nn.gelu(pre_ffn).astype(BF)
    branch = jnp.dot(hidden_low, outer_mat, preferred_element_type=F32)
    result = mixed + gain_ffn * normalize(branch)
    return (result, (stream_low, pre_conv, mixed_low, pre_ffn, hidden_low, branch))


def block_backward(grad_out, saved, weights, dilation):
    conv_mat, inner_mat, outer_mat, vector = weights
    gain_conv = vector[D : 2 * D]
    gain_ffn = vector[2 * D : 3 * D]
    stream_low, pre_conv, mixed_low, pre_ffn, hidden_low, branch = saved
    normed_branch, branch_back = jax.vjp(normalize, branch)
    grad_gain_ffn = jnp.sum(grad_out * normed_branch, axis=0)
    grad_branch = branch_back(grad_out * gain_ffn)[0].astype(BF)
    grad_outer = contract_rows(hidden_low, grad_branch)
    grad_hidden = contract_cols(grad_branch, outer_mat)
    _, gelu_back = jax.vjp(jax.nn.gelu, pre_ffn)
    grad_pre_ffn = gelu_back(grad_hidden)[0].astype(BF)
    grad_bias_ffn = jnp.sum(grad_pre_ffn.astype(F32), axis=0)
    grad_inner = contract_rows(mixed_low, grad_pre_ffn)
    grad_mixed = grad_out + contract_cols(grad_pre_ffn, inner_mat)
    normed_conv, conv_back = jax.vjp(conv_branch, pre_conv)
    grad_gain_conv = jnp.sum(grad_mixed * normed_conv, axis=0)
    grad_pre_conv = conv_back(grad_mixed * gain_conv)[0].astype(BF)
    grad_conv_bias = jnp.sum(grad_pre_conv.astype(F32), axis=0)
    grad_kernel = contract_rows(columns(stream_low, dilation), grad_pre_conv)
    grad_stream = grad_mixed + fold_back(contract_cols(grad_pre_conv, conv_mat), dilation)
    vector_grad = jnp.concatenate([grad_conv_bias, grad_gain_conv, grad_gain_ffn, grad_bias_ffn])
    return (grad_stream, (grad_kernel, grad_inner, grad_outer, vector_grad))


def gather_any(conv_weight, inner_weight, outer_weight, vectors):
    def whole(member):
        return lax.all_gather(member, ("dp", "fsdp"), axis=1, tiled=True)

    conv, inner, outer, vector = (
        whole(member) for member in (conv_weight, inner_weight, outer_weight, vectors)
    )
    return [
        (
            conv[b].reshape(KS * D, D),
            inner[b].reshape(D, FF),
            outer[b].reshape(FF, D),
            vector[b].astype(F32),
        )
        for b in range(2)
    ]


def reduce_any(grads, width):
    count_dp = lax.axis_size("dp")
    count_fsdp = lax.axis_size("fsdp")

    def settle(first, second):
        member = jnp.stack([first.reshape(-1), second.reshape(-1)]).astype(BF)
        member = member.reshape(2, count_dp, count_fsdp, -1)
        spread = lax.all_to_all(member, "fsdp", split_axis=2, concat_axis=2, tiled=True)
        partial = jnp.sum(spread.astype(F32), axis=2, keepdims=True).astype(BF)
        settled = lax.all_to_all(partial, "dp", split_axis=1, concat_axis=1, tiled=True)
        return jnp.sum(settled.astype(F32), axis=(1, 2))

    return tuple(settle(first, second) for first, second in zip(*grads))


def body_here(embeddings, conv_weight, inner_weight, outer_weight, vectors, cotangent, row_mask):
    weights = (
        conv_weight.reshape(2, -1, D),
        inner_weight.reshape(2, -1, FF),
        outer_weight.reshape(2, -1, D),
    )
    mask = row_mask.reshape(ROWS // 128, 128)
    result = forward(vectors, cotangent, mask, weights, embeddings)
    weights, output, vec, incoming, kept = result[:6], result[6], result[7], result[8], result[9:]
    *grads, vec_grad, emb_grad = finish((output, *backward(weights, vec, incoming, kept)))
    output, *grads = grads
    conv, inner, outer = (member.transpose(1, 0, 2).reshape(2, -1) for member in grads)
    return output, emb_grad, conv, inner, outer, vec_grad


def body_any(embeddings, conv_weight, inner_weight, outer_weight, vectors, cotangent, row_mask):
    weights = gather_any(conv_weight, inner_weight, outer_weight, vectors)
    stream = embeddings.astype(F32)
    saved = []
    for b in range(2):
        stream, kept = block_forward(stream, weights[b], DILATIONS[b])
        saved.append(kept)
    output = stream.astype(BF)
    grad_stream = cotangent.astype(F32) * row_mask.astype(F32)[:, None]
    grads = [None, None]
    for b in (1, 0):
        grad_stream, grads[b] = block_backward(grad_stream, saved[b], weights[b], DILATIONS[b])
    return (output, grad_stream.astype(BF), *reduce_any(grads, vectors.shape[1]))


def solution(mesh):
    rows = P(("dp", "fsdp"), None)
    flat = P(None, ("dp", "fsdp"))
    here = mesh.shape["dp"] == NX and mesh.shape["fsdp"] == NZ * NY * 2
    return jax.shard_map(
        body_here if here else body_any,
        mesh=mesh,
        in_specs=(rows, flat, flat, flat, flat, rows, P(("dp", "fsdp"))),
        out_specs=(rows, rows, flat, flat, flat, flat),
        check_vma=False,
    )
```

```python
import functools

import jax
import jax.numpy as jnp
import numpy as np
from jax import lax
from jax.experimental import pallas as pl
from jax.experimental.pallas import tpu as pltpu
from jax.sharding import PartitionSpec as P

MESH = pl.DeviceIdType.MESH
BF = jnp.bfloat16
NX, NZ, NY = 2, 4, 2
NDEV = 32


def place():
    across = lax.axis_index("dp")
    index = lax.axis_index("fsdp")
    return across, index // (2 * NY), (index // 2) % NY, index % 2


def device(x, z, y, c):
    return (x, (z * NY + y) * 2 + c)


def shard(x, z, y, c):
    return x * (NZ * NY * 2) + (z * NY + y) * 2 + c


def meet(peers):
    barrier = pltpu.get_barrier_semaphore()
    for peer in peers:
        pl.semaphore_signal(barrier, inc=1, device_id=peer, device_id_type=MESH)
    pl.semaphore_wait(barrier, len(peers))


def neighbours(x, z, y, c):
    return [
        device(1 - x, z, y, c),
        device(x, z, 1 - y, c),
        device(x, z, y, 1 - c),
        device(x, (z + 1) % NZ, y, c),
        device(x, (z + 2) % NZ, y, c),
        device(x, (z + 3) % NZ, y, c),
    ]

def halves_of(rect):
    at, rows, left, cols = rect
    if rows >= 32:
        first = (rows // 2 + 15) // 16 * 16
        return (at, first, left, cols), (at + first, rows - first, left, cols)
    if cols >= 256:
        return (at, rows, left, cols // 2), (at, rows, left + cols // 2, cols // 2)
    return rect, None


class Gather:
    def __init__(self, shapes, pieces, own_refs, full_refs, own_sem, send_sem, recv_sem):
        self.shapes, self.pieces = shapes, pieces
        self.own_refs, self.full_refs = own_refs, full_refs
        self.own_sem, self.send_sem, self.recv_sem = own_sem, send_sem, recv_sem
        self.place = x, z, y, c = place()
        self.to_x = device(1 - x, z, y, c)
        self.to_y = device(x, z, 1 - y, c)
        self.to_c = device(x, z, y, 1 - c)
        self.near = z + 1 - 2 * (z % 2)
        self.away = 2 - 2 * (z // 2)
        self.moves, self.totals = {}, {}

    def start(self):
        meet(neighbours(*self.place))

    def levels(self, which):
        z = self.place[1]
        return {
            "own": (z, 1),
            "near": (self.near, 1),
            "away": (self.away, 2),
            "pair": (2 * (z // 2), 2),
            "all": (0, NZ),
        }[which]

    def part(self, p, ax, level, ay, c, half=None):
        t, rect = self.pieces[p]
        at, height, left, width = rect if half is None else half
        rows, cols = self.shapes[t]
        low, count = level
        view = self.full_refs[t].reshape(NX, NZ, NY, 2, rows, cols)
        return view.at[ax, pl.ds(low, count), ay, c, pl.ds(at, height), pl.ds(left, width)]

    def send(self, p, part, kind, slot, target, amount):
        self.totals[p, kind] = self.totals.get((p, kind), 0) + amount
        pltpu.make_async_remote_copy(
            src_ref=part, dst_ref=part, send_sem=self.send_sem.at[p, kind],
            recv_sem=self.recv_sem.at[p, slot], device_id=target, device_id_type=MESH).start()

    def arrive(self, p, part, slot):
        pltpu.make_async_copy(part, part, self.recv_sem.at[p, slot]).wait()

    def amount(self, p, half=None):
        rect = self.pieces[p][1] if half is None else half
        return rect[1] * rect[3]

    def own(self, t):
        x, z, y, c = self.place
        rows, cols = self.shapes[t]
        view = self.full_refs[t].reshape(NX, NZ, NY, 2, rows, cols)
        self.moves[t] = pltpu.make_async_copy(self.own_refs[t], view.at[x, z, y, c], self.own_sem.at[t])
        self.moves[t].start()

    def over(self, p, which, slot, count):
        x, z, y, c = self.place
        part = self.part(p, x, self.levels(which), y, c)
        self.send(p, part, 1, 4 + slot, self.to_x, count * self.amount(p))
        self.send(p, part, 2, 7 + slot, self.to_y, count * self.amount(p))

    def column(self, p, ax, ay, slot):
        part = self.part(p, ax, self.levels("all"), ay, self.place[3])
        self.send(p, part, 3, 14 + slot, self.to_c, NZ * self.amount(p))

    def plane(self, p, level):
        rows, cols = self.shapes[self.pieces[p][0]]
        at, height, left, width = self.pieces[p][1]
        view = self.full_refs[self.pieces[p][0]].reshape(NX, NZ, NY, 2, rows, cols)
        return view.at[:, level, :, self.place[3], pl.ds(at, height), pl.ds(left, width)]

    def other_plane(self, p, level):
        rows, cols = self.shapes[self.pieces[p][0]]
        at, height, left, width = self.pieces[p][1]
        view = self.full_refs[self.pieces[p][0]].reshape(NX, NZ, NY, 2, rows, cols)
        return view.at[:, level, :, 1 - self.place[3], pl.ds(at, height), pl.ds(left, width)]

    def Z(self, p):
        x, z, y, c = self.place
        t = self.pieces[p][0]
        if t in self.moves:
            self.moves.pop(t).wait()
        if p in Z_LAST:
            self.over(p, "own", 0, 1)
            return
        part = self.part(p, x, self.levels("own"), y, c)
        for step in (1, 2, 3):
            self.send(p, part, 0, z, device(x, (z + step) % NZ, y, c), self.amount(p))
        self.over(p, "own", 0, 1)

    def A(self, p, k):
        x, z, y, c = self.place
        if p in Z_LAST:
            for step in (1, 2, 3):
                level = (z + step) % NZ
                self.arrive(p, self.plane(p, level), level)
                self.send(p, self.plane(p, level), 3, 14 + step, self.to_c, 4 * self.amount(p))
        elif k == 0:
            self.arrive(p, self.part(p, x, self.levels("near"), y, c), self.near)
            self.over(p, "near", 1, 1)
        else:
            for i in range(2):
                self.arrive(p, self.part(p, x, (self.away + i, 1), y, c), self.away + i)
            self.over(p, "away", 2, 2)
            self.column(p, x, y, 0)

    def C(self, p, k):
        x, z, y, c = self.place
        first, second = halves_of(self.pieces[p][1])
        if p in Z_LAST:
            self.arrive(p, self.part(p, 1 - x, self.levels("own"), y, c), 4)
            half = self.part(p, 1 - x, self.levels("own"), y, c, first)
            self.send(p, half, 2, 10, self.to_y, self.amount(p, first))
            self.arrive(p, self.part(p, x, self.levels("own"), 1 - y, c), 7)
            half = self.part(p, x, self.levels("own"), 1 - y, c, second)
            self.send(p, half, 1, 12, self.to_x, self.amount(p, second))
            return
        which = "away" if k else "pair"
        for slot, part_levels in (((2, "away"),) if k else ((0, "own"), (1, "near"))):
            self.arrive(p, self.part(p, 1 - x, self.levels(part_levels), y, c), 4 + slot)
        half = self.part(p, 1 - x, self.levels(which), y, c, first)
        self.send(p, half, 2, 10 + k, self.to_y, 2 * self.amount(p, first))
        for slot, part_levels in (((2, "away"),) if k else ((0, "own"), (1, "near"))):
            self.arrive(p, self.part(p, x, self.levels(part_levels), 1 - y, c), 7 + slot)
        if second is not None:
            half = self.part(p, x, self.levels(which), 1 - y, c, second)
            self.send(p, half, 1, 12 + k, self.to_x, 2 * self.amount(p, second))
        if k:
            self.column(p, 1 - x, y, 1)
            self.column(p, x, 1 - y, 2)

    def F(self, p):
        x, z, y, c = self.place
        first, second = halves_of(self.pieces[p][1])
        if p in Z_LAST:
            self.arrive(p, self.part(p, 1 - x, self.levels("own"), 1 - y, c, first), 10)
            self.arrive(p, self.part(p, 1 - x, self.levels("own"), 1 - y, c, second), 12)
            for step in (1, 2, 3):
                self.send(p, self.plane(p, z), 0, z, device(x, (z + step) % NZ, y, c), 4 * self.amount(p))
            self.send(p, self.plane(p, z), 3, 14, self.to_c, 4 * self.amount(p))
            return
        for k, which in enumerate(("pair", "away")):
            self.arrive(p, self.part(p, 1 - x, self.levels(which), 1 - y, c, first), 10 + k)
            if second is not None:
                self.arrive(p, self.part(p, 1 - x, self.levels(which), 1 - y, c, second), 12 + k)
        self.column(p, 1 - x, 1 - y, 3)

    def settle(self, p):
        x, z, y, c = self.place
        if p in Z_LAST:
            for step in range(NZ):
                self.arrive(p, self.other_plane(p, (z + step) % NZ), 14 + step)
            return
        for slot, (ax, ay) in enumerate(((x, y), (1 - x, y), (x, 1 - y), (1 - x, 1 - y))):
            self.arrive(p, self.part(p, ax, self.levels("all"), ay, 1 - c), 14 + slot)

    def sent(self, p):
        t, (at, rows, left, cols) = self.pieces[p]
        for kind in range(4):
            total = self.totals[p, kind]
            part = self.full_refs[t].at[pl.ds(0, total // cols), pl.ds(left, cols)]
            pltpu.make_async_copy(part, part, self.send_sem.at[p, kind]).wait()


D = 512
FF = 2048
KS = 9
L = 512
NV = 3 * D + FF
DILATIONS = (2, 16)
F32 = jnp.float32
EDGE = 64
WINDOWS = 2
ROWS = WINDOWS * L
SHARE = NV // NDEV
SHAPES = ((16, 128),) + ((KS * D // NDEV, D), (D // NDEV, FF), (FF // NDEV, D)) * 2
VEC, CONV, INNER, OUTER = 0, (1, 4), (2, 5), (3, 6)


def selectors():
    column = lax.broadcasted_iota(jnp.int32, (NDEV, NV), 1)
    first = lax.broadcasted_iota(jnp.int32, (NDEV, NV), 0) * SHARE
    inside = (column >= first) & (column < first + SHARE)
    pick = jnp.where(inside, 1.0, 0.0).astype(F32)
    offset = jnp.sum(jnp.where(inside, column - first, 0), axis=0, keepdims=True)
    lane = lax.broadcasted_iota(jnp.int32, (128, NV), 0)
    return jnp.where(lane == offset, 1.0, 0.0).astype(BF), pick


def dot(left, right):
    return jnp.dot(left, right, preferred_element_type=F32)


def gelu_both(v):
    square = v * v
    half = 0.5 + 0.5 * jnp.tanh(v * (0.7978845608028654 + 0.035677408136300125 * square))
    value = v * half
    steep = 1.5957691216057308 + 0.21406444881780075 * square
    return value, half + value * ((1.0 - half) * steep)


def norm_parts(v):
    centered = v - jnp.mean(v, axis=-1, keepdims=True)
    r = lax.rsqrt(jnp.mean(centered * centered, axis=-1, keepdims=True) + 1e-05)
    return centered * r, r


def whole(t):
    rows, cols = SHAPES[t]
    return (0, rows, 0, cols)


PIECES = (
    (VEC, whole(VEC)),
    (CONV[0], (0, 80, 0, D)),
    (CONV[0], (80, 64, 0, D)),
    (INNER[0], whole(INNER[0])),
    (OUTER[0], whole(OUTER[0])),
    (CONV[1], (0, 32, 0, D)),
    (CONV[1], (32, 64, 0, D)),
    (CONV[1], (96, 48, 0, D)),
    (INNER[1], whole(INNER[1])),
    (OUTER[1], whole(OUTER[1])),
)
Z_LAST = (5,)


FORWARD = (
    ("Z", 5), ("Z", 0), ("Z", 1), ("Z", 3), ("A", 0, 0), ("Z", 2), ("Z", 6), ("C", 0, 0), ("Z", 4),
    ("A", 1, 0), ("C", 5, 0), ("Z", 7), ("A", 3, 0), ("A", 0, 1), ("C", 1, 0), ("prep",), ("Z", 8),
    ("C", 3, 0), ("A", 2, 0), ("C", 0, 1), ("A", 1, 1), ("C", 2, 0), ("A", 6, 0), ("A", 4, 0),
    ("F", 0), ("C", 1, 1), ("A", 3, 1), ("A", 2, 1), ("C", 4, 0), ("C", 3, 1), ("F", 1),
    ("C", 2, 1), ("A", 7, 0), ("vec",), ("A", 4, 1), ("F", 5), ("F", 3), ("A", 6, 1), ("A", 7, 1),
    ("F", 2), ("mask",), ("conv", 0, 0), ("C", 4, 1), ("A", 8, 0), ("turn", 0), ("C", 6, 0),
    ("C", 7, 0), ("widen", 0, 0), ("C", 7, 1), ("C", 6, 1), ("A", 8, 1), ("Z", 9), ("conv", 0, 1),
    ("F", 4), ("widen", 0, 1), ("A", 9, 0), ("F", 7), ("C", 8, 0), ("A", 5, 0), ("narrow", 0, 0),
    ("F", 6), ("narrow", 0, 1), ("C", 8, 1), ("A", 9, 1), ("conv", 1, 0), ("C", 9, 0),
    ("conv", 1, 1), ("F", 8), ("turn", 1), ("C", 9, 1), ("widen", 1, 0), ("F", 9), ("widen", 1, 1),
    ("narrow", 1, 0), ("narrow", 1, 1),
)

KEPT = (
    ((ROWS, D), BF),
    ((ROWS, D), BF),
    ((D, ROWS), BF),
    ((D, ROWS), BF),
    ((4 * ROWS, D), BF),
    ((FF, ROWS), BF),
    ((ROWS, D), BF),
    ((ROWS, 128), F32),
)
NORM_C, SCALE_C, MIXED_T, LOW_T, SLOPE, HIDDEN_T, NORM_B, SCALE_B = range(8)
NK = len(KEPT)


def forward_kernel(schedule, *refs):
    count = len(SHAPES)
    vec_in, cot_ref, mask_in, refs = refs[0], refs[1], refs[2], refs[3:]
    weight_in, emb_ref, refs = refs[:3], refs[3], refs[4:]
    weight_out, refs = refs[:6], refs[6:]
    out_ref, vec_out, cot_out, refs = refs[0], refs[1], refs[2], refs[3:]
    kept_out, refs = (refs[:NK], refs[NK : 2 * NK]), refs[2 * NK :]
    full, refs = refs[:count], refs[count:]
    (stream, cols, hidden, mixed_low, emb, vec_f, vec, cot, out, turned, vec_own), refs = (
        refs[:11],
        refs[11:],
    )
    own_refs = [vec_own] + [ref.at[b] for b in range(2) for ref in weight_in]
    kept, refs = refs[:NK], refs[NK:]
    own_sem, send_sem, recv_sem, local_sem, save_sem = refs
    g = Gather(SHAPES, PIECES, own_refs, full, own_sem, send_sem, recv_sem)

    loads = [
        pltpu.make_async_copy(src, dst, local_sem.at[i])
        for i, (src, dst) in enumerate(((emb_ref, emb), (cot_ref, cot)))
    ]
    saves = {}

    def save(name, src, dst):
        move = pltpu.make_async_copy(src, dst, save_sem.at[len(saves)])
        move.start()
        saves[name] = move

    waited = set()

    def saved(name):
        if name in saves and name not in waited:
            saves[name].wait()
            waited.add(name)

    settled = set()

    def settle(t):
        if t in settled:
            return
        settled.add(t)
        for p, (tensor, _) in enumerate(PIECES):
            if tensor == t:
                g.settle(p)

    def keep(b, *members):
        for i in members:
            save((b, i), kept[i], kept_out[b][i])

    def free(b, *members):
        if b == 1:
            for i in members:
                saved((0, i))

    def prepare():
        loads[0].wait()
        edge = jnp.zeros((EDGE, D), F32)
        for w in range(WINDOWS):
            stream[w, 0:EDGE] = edge
            stream[w, EDGE + L : EDGE + L + EDGE] = edge
            stream[w, EDGE : EDGE + L] = emb[w * L : (w + 1) * L].astype(F32)
        kept[LOW_T][...] = emb[...].T
        keep(0, LOW_T)

    def vectors():
        settle(VEC)
        spread, pick = selectors()
        vec_f[...] = full[VEC][...].astype(F32)
        for b in range(2):
            rows = vec_f[pl.ds(b, NDEV, stride=16)].astype(BF)
            vec[b : b + 1] = jnp.sum(dot(rows, spread) * pick, axis=0, keepdims=True)
        save("vec", vec, vec_out)

    def masked():
        loads[1].wait()
        for i in range(ROWS // 128):
            line = jnp.broadcast_to(mask_in[i : i + 1].astype(F32), (128, 128)).T
            for j in range(D // 128):
                spot = (slice(i * 128, (i + 1) * 128), slice(j * 128, (j + 1) * 128))
                cot[spot] = (cot[spot].astype(F32) * line).astype(BF)
        save("cot", cot, cot_out)

    def turn(b):
        settle(CONV[b])
        if b == 1:
            saved((0, "kernel"))
        for k in range(KS):
            turned[k * D : (k + 1) * D] = full[CONV[b]][k * D : (k + 1) * D].T
        save((b, "kernel"), turned, weight_out[3 * b])

    def conv(b, w):
        at = slice(w * L, (w + 1) * L)
        if w == 0:
            settle(CONV[b])
            free(b, NORM_C, SCALE_C, MIXED_T)
        for k in range(KS):
            first = EDGE + (k - KS // 2) * DILATIONS[b]
            cols[:, k * D : (k + 1) * D] = stream[w, first : first + L].astype(BF)
        pre = dot(cols[...], full[CONV[b]][...]) + vec[b : b + 1, 0:D]
        value, slope = gelu_both(pre)
        n, r = norm_parts(value)
        kept[NORM_C][at] = n.astype(BF)
        kept[SCALE_C][at] = (slope * r).astype(BF)
        mixed = stream[w, EDGE : EDGE + L] + vec[b : b + 1, D : 2 * D] * n
        stream[w, EDGE : EDGE + L] = mixed
        low = mixed.astype(BF)
        mixed_low[at] = low
        kept[MIXED_T][:, at] = low.T
        if w == WINDOWS - 1:
            keep(b, NORM_C, SCALE_C, MIXED_T)

    def widen(b, w):
        at = slice(w * L, (w + 1) * L)
        if w == 0:
            settle(INNER[b])
            free(b, SLOPE, HIDDEN_T)
            save((b, "inner"), full[INNER[b]], weight_out[3 * b + 1])
        values = mixed_low[at]
        for n in range(FF // D):
            part = slice(n * D, (n + 1) * D)
            pre = dot(values, full[INNER[b]][:, part])
            pre = pre + vec[b : b + 1, 3 * D + n * D : 3 * D + (n + 1) * D]
            value, slope = gelu_both(pre)
            kept[SLOPE][n * ROWS + w * L : n * ROWS + (w + 1) * L] = slope.astype(BF)
            low = value.astype(BF)
            hidden[at, part] = low
            kept[HIDDEN_T][part, at] = low.T
        if w == WINDOWS - 1:
            keep(b, SLOPE, HIDDEN_T)

    def narrow(b, w):
        at = slice(w * L, (w + 1) * L)
        if w == 0:
            settle(OUTER[b])
            free(b, NORM_B, SCALE_B)
            save((b, "outer"), full[OUTER[b]], weight_out[3 * b + 2])
        n, r = norm_parts(dot(hidden[at], full[OUTER[b]][...]))
        kept[NORM_B][at] = n.astype(BF)
        kept[SCALE_B][at] = jnp.broadcast_to(r, (L, 128))
        result = stream[w, EDGE : EDGE + L] + vec[b : b + 1, 2 * D : 3 * D] * n
        if b == 0:
            stream[w, EDGE : EDGE + L] = result
            if w == 0:
                saved((0, LOW_T))
            kept[LOW_T][:, at] = result.astype(BF).T
        else:
            out[at] = result.astype(BF)
        if w == WINDOWS - 1:
            keep(b, NORM_B, SCALE_B)
            if b == 0:
                keep(1, LOW_T)
            else:
                save("out", out, out_ref)

    actions = {
        "Z": g.Z,
        "A": g.A,
        "C": g.C,
        "F": g.F,
        "prep": prepare,
        "vec": vectors,
        "mask": masked,
        "turn": turn,
        "conv": conv,
        "widen": widen,
        "narrow": narrow,
    }
    vec_f[0:16] = jnp.zeros((16, 128), F32)
    vec_f[0:2, 0:SHARE] = vec_in[...].astype(F32)
    vec_own[...] = vec_f[0:16].astype(BF)
    for t in range(count):
        g.own(t)
    for move in loads:
        move.start()
    g.start()
    for name, *where in schedule:
        actions[name](*where)
    for p in range(len(PIECES)):
        g.sent(p)
    for name in saves:
        saved(name)


def forward(vectors, cotangent, mask, weights, embeddings):
    count, n = len(SHAPES), len(PIECES)
    anywhere = pl.BlockSpec(memory_space=pl.ANY)
    held = pl.BlockSpec(memory_space=pltpu.VMEM)
    out_shape = (
        [jax.ShapeDtypeStruct((NDEV * r, w), BF) for r, w in SHAPES[1:]]
        + [jax.ShapeDtypeStruct((ROWS, D), BF), jax.ShapeDtypeStruct((8, NV), F32)]
        + [jax.ShapeDtypeStruct((ROWS, D), BF)]
        + [jax.ShapeDtypeStruct(shape, dtype) for shape, dtype in KEPT * 2]
    )
    return pl.pallas_call(
        functools.partial(forward_kernel, FORWARD),
        out_shape=out_shape,
        in_specs=[held, anywhere, held] + [anywhere] * 4,
        out_specs=[anywhere] * len(out_shape),
        scratch_shapes=[
            *[pltpu.VMEM((NDEV * r, w), BF) for r, w in SHAPES],
            pltpu.VMEM((WINDOWS, L + 2 * EDGE, D), F32),
            pltpu.VMEM((L, KS * D), BF),
            pltpu.VMEM((ROWS, FF), BF),
            pltpu.VMEM((ROWS, D), BF),
            pltpu.VMEM((ROWS, D), BF),
            pltpu.VMEM((NDEV * 16, 128), F32),
            pltpu.VMEM((8, NV), F32),
            pltpu.VMEM((ROWS, D), BF),
            pltpu.VMEM((ROWS, D), BF),
            pltpu.VMEM((KS * D, D), BF),
            pltpu.VMEM((16, 128), BF),
            *[pltpu.VMEM(shape, dtype) for shape, dtype in KEPT],
            pltpu.SemaphoreType.DMA((count,)),
            pltpu.SemaphoreType.DMA((n, 4)),
            pltpu.SemaphoreType.DMA((n, 18)),
            pltpu.SemaphoreType.DMA((2,)),
            pltpu.SemaphoreType.DMA((32,)),
        ],
        compiler_params=pltpu.CompilerParams(
            collective_id=0, has_side_effects=True, vmem_limit_bytes=62 * 2**20
        ),
        name="forward",
    )(vectors, cotangent, mask, *weights, embeddings)


REDUCED = (
    ("o", 1, 0, 512),
    ("i", 1, 0, 2048),
    ("c", 1, 0, 128),
    ("c", 1, 128, 128),
    ("c", 1, 256, 128),
    ("c", 1, 384, 128),
    ("o", 0, 0, 512),
    ("i", 0, 0, 2048),
    ("c", 0, 0, 128),
    ("c", 0, 128, 128),
    ("c", 0, 256, 128),
    ("c", 0, 384, 128),
    ("v", 0, 0, 128),
)
Z_FIRST = (2,)
HEIGHT = {"o": FF // NDEV, "i": D // NDEV, "c": KS * D // NDEV, "v": 16}
NR = len(REDUCED)
LATER = {p: REDUCED.index((k, 1, left, width)) for p, (k, b, left, width) in enumerate(REDUCED) if b == 0 and k != "v"}


def size_of(p):
    kind, _, _, cols = REDUCED[p]
    return HEIGHT[kind], cols


def halves_in(p):
    rows, cols = size_of(p)
    return halves_of((0, rows, 0, cols))


class Reduce:
    def __init__(self, parts, swap, first_in, second_in, from_x, from_y, total, from_z, result,
                 final, outs, send_sem, recv_sem, out_sem, credit):
        self.parts, self.swap = parts, swap
        self.first_in, self.second_in = first_in, second_in
        self.from_x, self.from_y, self.total, self.from_z = from_x, from_y, total, from_z
        self.result, self.final, self.outs = result, final, outs
        self.ended = set()
        self.send_sem, self.recv_sem, self.out_sem, self.credit = send_sem, recv_sem, out_sem, credit
        self.place = x, z, y, c = place()
        self.to_x = device(1 - x, z, y, c)
        self.to_y = device(x, z, 1 - y, c)
        self.to_c = device(x, z, y, 1 - c)
        self.moves, self.live = [], {}

    def start(self):
        meet(neighbours(*self.place))

    def send(self, p, kind, src, dst, target):
        move = pltpu.make_async_remote_copy(
            src_ref=src, dst_ref=dst, send_sem=self.send_sem.at[p, kind],
            recv_sem=self.recv_sem.at[p, kind], device_id=target, device_id_type=MESH)
        move.start()
        self.moves.append(move)
        self.live[p, kind] = move

    def half_of(self, ref, half):
        at, height, left, width = half
        return ref.at[:, pl.ds(at, height), pl.ds(left, width)]

    def column(self, p, ax, ay, half):
        kind, b, left, width = REDUCED[p]
        part = self.parts[kind, b]
        at, height, off, wide = half
        return part.reshape(NX, NZ, NY, 2, *part.shape[2:]).at[
            ax, :, ay, self.place[3], pl.ds(at, height), pl.ds(left + off, wide)
        ]

    def plane(self, p, level):
        kind, b, left, width = REDUCED[p]
        part = self.parts[kind, b]
        return part.reshape(NX, NZ, NY, 2, *part.shape[2:]).at[
            :, level, :, self.place[3], :, pl.ds(left, width)
        ]

    def single(self, p, ax, ay, half):
        kind, b, left, width = REDUCED[p]
        at, height, off, wide = half
        j = (ax * NZ + self.place[1]) * NY + ay
        return self.parts[kind, b].at[j, self.place[3], pl.ds(at, height), pl.ds(left + off, wide)]

    def exchange(self, p):
        x, z, y, c = self.place
        for step in (1, 2, 3):
            self.live[p, 6 + step].wait_recv()
        for ax in range(NX):
            for ay in range(NY):
                part, at = self.spot(p, (ax * NZ + z) * NY + ay)
                acc = part[at].astype(F32)
                for step in range(3):
                    acc = acc + self.from_z[p][step, ax, ay].astype(F32)
                part[at] = acc.astype(BF)
        first, second = halves_in(p)

        def side(ref, half):
            at, height, left, width = half
            return ref.at[0, pl.ds(at, height), pl.ds(left, width)]

        self.send(p, 1, self.single(p, 1 - x, 1 - y, first), self.first_in[p].at[0], self.to_x)
        self.send(p, 2, self.single(p, 1 - x, 1 - y, second), self.second_in[p].at[0], self.to_y)
        self.send(p, 4, self.single(p, x, 1 - y, second), side(self.from_y[p], second), self.to_y)
        self.send(p, 3, self.single(p, 1 - x, y, first), side(self.from_x[p], first), self.to_x)

    def turn_corner(self, p, ax, ay, half, extra, to, kind, target):
        part, at = self.spot(p, (ax * NZ + self.place[1]) * NY + ay, half)
        part[at] = (part[at].astype(F32) + extra[0].astype(F32)).astype(BF)
        row, height, left, width = half
        self.send(p, kind, self.single(p, ax, ay, half), to.at[0, pl.ds(row, height), pl.ds(left, width)], target)

    def finish_level(self, p):
        x, z, y, c = self.place
        for kind in (3, 4, 5, 6):
            self.live[p, kind].wait_recv()
        part, at = self.spot(p, (x * NZ + z) * NY + y)
        return part[at].astype(F32) + self.from_x[p][0].astype(F32) + self.from_y[p][0].astype(F32)

    def spot(self, p, j, half=None):
        kind, b, left, width = REDUCED[p]
        at, height, off, wide = (0, *size_of(p)[:1], 0, width) if half is None else half
        return self.parts[kind, b], (j, self.place[3], pl.ds(at, height), pl.ds(left + off, wide))

    def begin(self, p):
        kind, b, left, width = REDUCED[p]
        if p in LATER:
            pl.semaphore_wait(self.credit.at[LATER[p]], 1)
        other = self.parts[kind, b].at[:, 1 - self.place[3], :, pl.ds(left, width)]
        self.send(p, 0, other, self.swap[p], self.to_c)

    def pair(self, p):
        x, z, y, c = self.place
        swap = self.swap[p]
        self.live[p, 0].wait_recv()

        @pl.loop(0, 16)
        def _(i):
            part, at = self.spot(p, i)
            part[at] = (part[at].astype(F32) + swap[i].astype(F32)).astype(BF)

        if p in LATER.values():
            pl.semaphore_signal(self.credit.at[p], inc=1, device_id=self.to_c, device_id_type=MESH)
        if p in Z_FIRST:
            for step in (1, 2, 3):
                level = (z + step) % NZ
                self.send(p, 6 + step, self.plane(p, level), self.from_z[p].at[step - 1], device(x, level, y, c))
            return
        first, second = halves_in(p)
        half_of = self.half_of
        self.send(p, 1, self.column(p, 1 - x, 1 - y, first), self.first_in[p], self.to_x)
        if second is not None:
            self.send(p, 2, self.column(p, 1 - x, 1 - y, second), self.second_in[p], self.to_y)
            self.send(p, 4, self.column(p, x, 1 - y, second), half_of(self.from_y[p], second), self.to_y)
        self.send(p, 3, self.column(p, 1 - x, y, first), half_of(self.from_x[p], first), self.to_x)

    def add_half(self, p, ax, ay, half, extra):
        @pl.loop(0, NZ)
        def _(i):
            part, at = self.spot(p, (ax * NZ + i) * NY + ay, half)
            part[at] = (part[at].astype(F32) + extra[i].astype(F32)).astype(BF)

    def corner_x(self, p):
        x, z, y, c = self.place
        first, _ = halves_in(p)
        self.live[p, 1].wait_recv()
        if p in Z_FIRST:
            self.turn_corner(p, x, 1 - y, first, self.first_in[p], self.from_y[p], 5, self.to_y)
            return
        self.add_half(p, x, 1 - y, first, self.first_in[p])
        self.send(p, 5, self.column(p, x, 1 - y, first), self.half_of(self.from_y[p], first), self.to_y)

    def corner_y(self, p):
        x, z, y, c = self.place
        _, second = halves_in(p)
        if p in Z_FIRST:
            self.live[p, 2].wait_recv()
            self.turn_corner(p, 1 - x, y, second, self.second_in[p], self.from_x[p], 6, self.to_x)
        elif second is not None:
            self.live[p, 2].wait_recv()
            self.add_half(p, 1 - x, y, second, self.second_in[p])
            self.send(p, 6, self.column(p, 1 - x, y, second), self.half_of(self.from_x[p], second), self.to_x)

    def line(self, p):
        x, z, y, c = self.place
        if p in Z_FIRST:
            self.exchange(p)
            return
        for kind in (3, 4, 5, 6):
            if (p, kind) in self.live:
                self.live[p, kind].wait_recv()

        def summed(i):
            part, at = self.spot(p, (x * NZ + i) * NY + y)
            return (
                part[at].astype(F32)
                + self.from_x[p][i].astype(F32)
                + self.from_y[p][i].astype(F32)
            )

        for step in (1, 2, 3):
            level = (z + step) % NZ
            self.total[p][step - 1] = summed(level).astype(BF)
            self.send(p, 6 + step, self.total[p].at[step - 1], self.from_z[p].at[step - 1], device(x, level, y, c))
        self.result[p][...] = summed(z)

    def end(self, p):
        if p in Z_FIRST:
            acc = self.finish_level(p)
        else:
            for step in (1, 2, 3):
                self.live[p, 6 + step].wait_recv()
            acc = self.result[p][...]
            for step in range(3):
                acc = acc + self.from_z[p][step].astype(F32)
        kind, b, left, width = REDUCED[p]
        if kind == "v":
            self.final["v"][...] = acc[0:2, 0:SHARE]
        else:
            self.final[kind][:, b, left : left + width] = acc
        self.ended.add(p)
        if all(q in self.ended for q in range(NR) if REDUCED[q][0] == kind):
            move = pltpu.make_async_copy(self.final[kind], self.outs[kind], self.out_sem.at[p])
            move.start()
            self.live[p, "out"] = move

    def close(self):
        for move in self.moves:
            move.wait_send()
        for p in range(NR):
            if (p, "out") in self.live:
                self.live[p, "out"].wait()


def contract_cols(left, right):
    return lax.dot_general(left, right, (((1,), (1,)), ((), ())), preferred_element_type=F32)


def norm_back(n, e):
    return e - jnp.mean(e, axis=-1, keepdims=True) - n * jnp.mean(e * n, axis=-1, keepdims=True)


TAPS = 3

BACKWARD = (
    ("prep",), ("b1", 1, 1), ("b1", 1, 0), ("do", 1, 0), ("do", 1, 1), ("begin", 0), ("b2", 1, 1),
    ("b2", 1, 3), ("b2", 1, 2), ("b2", 1, 0), ("pair", 0), ("di", 1), ("begin", 1), ("b3", 1, 1),
    ("b3", 1, 0), ("cor2", 0), ("cor1", 0), ("b5", 1, 0), ("pair", 1), ("b5", 1, 1), ("dk", 1, 1),
    ("begin", 4), ("dk", 1, 0), ("begin", 3), ("line", 0), ("pair", 4), ("begin", 5), ("b6", 1, 1),
    ("pair", 3), ("begin", 2), ("pair", 5), ("slope",), ("cor2", 1), ("b6", 1, 0), ("cor1", 1),
    ("pair", 2), ("b1", 0, 1), ("b1", 0, 0), ("b2", 0, 1), ("cor2", 4), ("cor1", 4), ("do", 0, 1),
    ("b2", 0, 0), ("cor1", 3), ("do", 0, 0), ("begin", 6), ("b2", 0, 2), ("cor1", 5), ("cor2", 3),
    ("cor2", 5), ("b2", 0, 3), ("di", 0), ("pair", 6), ("begin", 7), ("line", 4), ("line", 1),
    ("b3", 0, 0), ("b5", 0, 0), ("line", 3), ("b3", 0, 1), ("pair", 7), ("end", 0), ("cor2", 6),
    ("b5", 0, 1), ("cor1", 6), ("dk", 0, 1), ("vg",), ("line", 5), ("begin", 10), ("begin", 12),
    ("cor1", 7), ("dk", 0, 0), ("pair", 12), ("begin", 9), ("cor2", 7), ("pair", 10), ("b6", 0, 0),
    ("line", 6), ("pair", 9), ("line", 7), ("cor2", 12), ("cor1", 10), ("begin", 8), ("end", 4),
    ("cor2", 10), ("pair", 8), ("b6", 0, 1), ("cor2", 9), ("end", 1), ("cor1", 9), ("begin", 11),
    ("line", 10), ("cor1", 12), ("cor1", 8), ("cor2", 8), ("pair", 11), ("line", 9), ("line", 8),
    ("cor2", 11), ("cor1", 11), ("end", 3), ("line", 12), ("end", 5), ("line", 2), ("end", 7),
    ("line", 11), ("end", 10), ("cor1", 2), ("cor2", 2), ("end", 6), ("end", 8), ("end", 2),
    ("end", 9), ("end", 12), ("end", 11),
)


def backward_kernel(schedule, *refs):
    weights_hbm, refs = refs[:6], refs[6:]
    (vec_hbm, cot_hbm), refs = refs[:2], refs[2:]
    kept_hbm, refs = (refs[:NK], refs[NK : 2 * NK]), refs[2 * NK :]
    outs, refs = dict(zip("cio", refs[:3])), refs[3:]
    outs["v"], emb_grad_out, refs = refs[0], refs[1], refs[2:]
    part_o1, part_i1, part_c1, part_o0, part_i0, vec_part, refs = *refs[:6], refs[6:]
    swaps, refs = refs[: NR - len(LATER)], refs[NR - len(LATER) :]
    lists = []
    for _ in range(7):
        lists.append(refs[:NR])
        refs = refs[NR:]
    first_in, second_in, from_x, from_y, total, from_z, result = lists
    final, refs = dict(zip("ciov", refs[:4])), refs[4:]
    (conv_w, inner_w, outer_w, big, hidden_t, norm_b, scale_b, mixed_t, norm_c, scale_c, low_t,
     grad, frame, temp, cols, vec, vec_grad, tile), refs = refs[:18], refs[18:]
    send_sem, recv_sem, out_sem, credit, load_sem = refs
    view = big.reshape(16, 2, KS * D // NDEV, D)
    parts = {
        ("o", 1): part_o1, ("i", 1): part_i1, ("c", 1): part_c1,
        ("o", 0): part_o0, ("i", 0): part_i0, ("c", 0): view, ("v", 0): vec_part,
    }
    conv_flat = {1: part_c1.reshape(KS * D, D), 0: big}
    own = [p for p in range(NR) if p not in LATER]
    swap = {p: swaps[own.index(LATER.get(p, p))] for p in range(NR)}
    r = Reduce(parts, swap, first_in, second_in, from_x, from_y, total, from_z, result, final, outs,
               send_sem, recv_sem, out_sem, credit)
    loading = {}
    met = set()

    def load(name, src, dst):
        move = pltpu.make_async_copy(src, dst, load_sem.at[len(loading)])
        move.start()
        loading[name] = move

    def need(*names):
        for name in names:
            if name not in met:
                met.add(name)
                loading[name].wait()

    def load_block(b, *names):
        table = {
            "norm_b": (kept_hbm[b][NORM_B], norm_b),
            "scale_b": (kept_hbm[b][SCALE_B], scale_b),
            "outer": (weights_hbm[3 * b + 2], outer_w),
            "slope": (kept_hbm[b][SLOPE], big.at[pl.ds(0, 4 * ROWS)]),
            "hidden": (kept_hbm[b][HIDDEN_T], hidden_t),
            "mixed": (kept_hbm[b][MIXED_T], mixed_t),
            "inner": (weights_hbm[3 * b + 1], inner_w),
            "norm_c": (kept_hbm[b][NORM_C], norm_c),
            "scale_c": (kept_hbm[b][SCALE_C], scale_c),
            "low": (kept_hbm[b][LOW_T], low_t),
            "kernel": (weights_hbm[3 * b], conv_w),
        }
        for name in names:
            load((b, name), *table[name])

    counts = {}

    def next_block(b, pieces, *names):
        counts[b, names] = counts.get((b, names), 0) + 1
        if b and counts[b, names] == pieces:
            load_block(0, *names)
        return counts[b, names] == pieces

    def rows_at(w):
        return slice(w * L, (w + 1) * L)

    def prepare():
        vec_grad[...] = jnp.zeros_like(vec_grad)
        edge = jnp.zeros((EDGE, D), F32)
        for w in range(WINDOWS):
            frame[w, 0:EDGE] = edge
            frame[w, EDGE + L : EDGE + L + EDGE] = edge
        need("cot")
        grad[...] = temp[...].astype(F32)
        need("vec")

    def add_vec(b, at, values):
        width = values.shape[-1]
        vec_grad[b : b + 1, at : at + width] += jnp.sum(values, axis=0, keepdims=True)

    def branch_back(b, w):
        need((b, "norm_b"), (b, "scale_b"))
        at = rows_at(w)
        n = norm_b[at].astype(F32)
        incoming = grad[at]
        add_vec(b, 2 * D, incoming * n)
        scale = jnp.concatenate([scale_b[at]] * (D // 128), axis=1)
        temp[at] = (scale * norm_back(n, vec[b : b + 1, 2 * D : 3 * D] * incoming)).astype(BF)
        next_block(b, WINDOWS, "norm_b", "scale_b")

    def hidden_back(b, n):
        need((b, "outer"), (b, "slope"))
        at = slice(n * ROWS, (n + 1) * ROWS)
        grad_hidden = contract_cols(temp[...], outer_w[n * D : (n + 1) * D])
        grad_pre = (big[at].astype(F32) * grad_hidden).astype(BF)
        big[at] = grad_pre
        add_vec(b, 3 * D + n * D, grad_pre.astype(F32))
        next_block(b, FF // D, "outer")

    def outer_grad(b, h):
        need((b, "hidden"))
        at = slice(h * 256, (h + 1) * 256)
        out = dot(hidden_t[...], temp[:, at]).astype(BF)
        parts["o", b][:, :, :, at] = out.reshape(16, 2, FF // NDEV, 256)
        next_block(b, 2, "hidden")

    def inner_grad(b):
        need((b, "mixed"))
        for n in range(FF // D):
            out = dot(mixed_t[...], big[n * ROWS : (n + 1) * ROWS]).astype(BF)
            parts["i", b][:, :, :, n * D : (n + 1) * D] = out.reshape(16, 2, D // NDEV, D)
        next_block(b, 1, "mixed")

    def mixed_back(b, w):
        need((b, "inner"))
        acc = grad[rows_at(w)]
        for n in range(FF // D):
            at = slice(n * ROWS + w * L, n * ROWS + (w + 1) * L)
            acc = acc + contract_cols(big[at], inner_w[:, n * D : (n + 1) * D])
        grad[rows_at(w)] = acc
        next_block(b, WINDOWS, "inner")

    def conv_back(b, w):
        need((b, "norm_c"), (b, "scale_c"))
        at = rows_at(w)
        n = norm_c[at].astype(F32)
        incoming = grad[at]
        add_vec(b, D, incoming * n)
        out = scale_c[at].astype(F32) * norm_back(n, vec[b : b + 1, D : 2 * D] * incoming)
        out = out.astype(BF).astype(F32)
        add_vec(b, 0, out)
        frame[w, EDGE : EDGE + L] = out
        next_block(b, WINDOWS, "norm_c", "scale_c")

    def kernel_grad(b, h):
        need((b, "low"))
        at = slice(h * 256, (h + 1) * 256)
        for k in range(KS):
            first = EDGE - (k - KS // 2) * DILATIONS[b]
            for w in range(WINDOWS):
                temp[rows_at(w), 0:256] = frame[w, first : first + L, at].astype(BF)
            conv_flat[b][k * D : (k + 1) * D, at] = dot(low_t[...], temp[:, 0:256]).astype(BF)
        next_block(b, 2, "low")

    def stream_back(b, w):
        need((b, "kernel"))
        acc = grad[rows_at(w)]
        for group in range(KS // TAPS):
            for i in range(TAPS):
                first = EDGE - (group * TAPS + i - KS // 2) * DILATIONS[b]
                cols[:, i * D : (i + 1) * D] = frame[w, first : first + L].astype(BF)
            acc = acc + dot(cols[...], conv_w[group * TAPS * D : (group + 1) * TAPS * D])
        if b:
            grad[rows_at(w)] = acc
        else:
            norm_b[rows_at(w)] = acc.astype(BF)
        if next_block(b, WINDOWS, "kernel") and b == 0:
            load("out", norm_b, emb_grad_out)

    def vector_grads():
        spread, pick = selectors()
        tile[...] = jnp.zeros_like(tile)
        for b in range(2):
            rows = (pick * vec_grad[b : b + 1]).astype(BF)
            tile[pl.ds(b, NDEV, stride=16)] = contract_cols(rows, spread)
        vec_part[...] = tile[...].astype(BF).reshape(16, 2, 16, 128)

    actions = {
        "begin": r.begin,
        "pair": r.pair,
        "cor1": r.corner_x,
        "cor2": r.corner_y,
        "line": r.line,
        "end": r.end,
        "prep": prepare,
        "b1": branch_back,
        "b2": hidden_back,
        "do": outer_grad,
        "di": inner_grad,
        "b3": mixed_back,
        "b5": conv_back,
        "dk": kernel_grad,
        "b6": stream_back,
        "vg": vector_grads,
        "slope": lambda: load_block(0, "slope"),
    }
    load("cot", cot_hbm, temp)
    load("vec", vec_hbm, vec)
    load_block(1, "norm_b", "scale_b", "outer", "slope", "hidden", "mixed", "inner", "norm_c", "scale_c", "low", "kernel")
    r.start()
    for name, *where in schedule:
        actions[name](*where)
    r.close()
    need("out")


def backward(weights, vec, cotangent, kept):
    anywhere = pl.BlockSpec(memory_space=pl.ANY)
    finals = [(rows, 2, cols) for rows, cols in SHAPES[1:4]] + [(2, SHARE)]
    out_shape = [jax.ShapeDtypeStruct(shape, F32) for shape in finals]
    out_shape += [jax.ShapeDtypeStruct((ROWS, D), BF)]

    def halves(which):
        spaces = []
        for p in range(NR):
            half = halves_in(p)[which]
            half = (0, 16, 0, 128) if half is None else half
            spaces.append(pltpu.VMEM((1 if p in Z_FIRST else NZ, half[1], half[3]), BF))
        return spaces

    def space(lead, dtype=BF, members=range(NR), early=None):
        leads = [early if p in Z_FIRST and early is not None else lead for p in members]
        return [pltpu.VMEM((*before, *size_of(p)), dtype) for p, before in zip(members, leads)]

    def whole_part(t):
        return pltpu.VMEM((16, 2, *SHAPES[t]), BF)

    args = (*weights, vec, cotangent, *kept)
    return pl.pallas_call(
        functools.partial(backward_kernel, BACKWARD),
        out_shape=out_shape,
        in_specs=[anywhere] * len(args),
        out_specs=[anywhere] * len(out_shape),
        scratch_shapes=[
            whole_part(3), whole_part(2), whole_part(1), whole_part(3), whole_part(2), whole_part(0),
            *space((16,), members=[p for p in range(NR) if p not in LATER]),
            *halves(0),
            *halves(1),
            *space((NZ,), early=(1,)),
            *space((NZ,), early=(1,)),
            *space((3,), early=(1,)),
            *space((3,), early=(3, NX, NY)),
            *space((), F32),
            *[pltpu.VMEM(shape, F32) for shape in finals],
            pltpu.VMEM((KS * D, D), BF),
            pltpu.VMEM((D, FF), BF),
            pltpu.VMEM((FF, D), BF),
            pltpu.VMEM((KS * D, D), BF),
            pltpu.VMEM((FF, ROWS), BF),
            pltpu.VMEM((ROWS, D), BF),
            pltpu.VMEM((ROWS, 128), F32),
            pltpu.VMEM((D, ROWS), BF),
            pltpu.VMEM((ROWS, D), BF),
            pltpu.VMEM((ROWS, D), BF),
            pltpu.VMEM((D, ROWS), BF),
            pltpu.VMEM((ROWS, D), F32),
            pltpu.VMEM((WINDOWS, L + 2 * EDGE, D), F32),
            pltpu.VMEM((ROWS, D), BF),
            pltpu.VMEM((L, TAPS * D), BF),
            pltpu.VMEM((8, NV), F32),
            pltpu.VMEM((8, NV), F32),
            pltpu.VMEM((NDEV * 16, 128), F32),
            pltpu.SemaphoreType.DMA((NR, 10)),
            pltpu.SemaphoreType.DMA((NR, 10)),
            pltpu.SemaphoreType.DMA((NR,)),
            pltpu.SemaphoreType.REGULAR((NR,)),
            pltpu.SemaphoreType.DMA((32,)),
        ],
        compiler_params=pltpu.CompilerParams(
            collective_id=1, has_side_effects=True, vmem_limit_bytes=63 * 2**20
        ),
        name="backward",
    )(*args)


def finish_kernel(count, *refs):
    for source, target in zip(refs[:count], refs[count:]):
        target[...] = source[...]


def finish(members):
    steps = 2

    def block(member):
        if member.shape[0] < 16:
            return pl.BlockSpec(member.shape, lambda i: (0,) * member.ndim)
        shape = (member.shape[0] // steps, *member.shape[1:])
        return pl.BlockSpec(shape, lambda i: (i,) + (0,) * (member.ndim - 1))

    blocks = [block(member) for member in members]
    return pl.pallas_call(
        functools.partial(finish_kernel, len(members)),
        grid=(steps,),
        out_shape=[jax.ShapeDtypeStruct(v.shape, v.dtype) for v in members],
        in_specs=blocks,
        out_specs=blocks,
        name="finish",
    )(*members)


def normalize(values):
    centered = values - jnp.mean(values, axis=-1, keepdims=True)
    return centered * lax.rsqrt(jnp.mean(centered * centered, axis=-1, keepdims=True) + 1e-05)


def conv_branch(values):
    return normalize(jax.nn.gelu(values))


def contract_rows(left, right):
    return lax.dot_general(left, right, (((0,), (0,)), ((), ())), preferred_element_type=F32)


def columns(stream_low, dilation):
    windows = stream_low.shape[0] // L
    framed = stream_low.reshape(windows, L, D)
    margin = KS // 2 * dilation
    padded = jnp.pad(framed, ((0, 0), (margin, margin), (0, 0)))
    stacked = jnp.concatenate(
        [padded[:, tap_id * dilation : tap_id * dilation + L] for tap_id in range(KS)], axis=2
    )
    return stacked.reshape(windows * L, KS * D)


def fold_back(grad_cols, dilation):
    windows = grad_cols.shape[0] // L
    framed = grad_cols.reshape(windows, L, KS, D)
    margin = KS // 2 * dilation
    total = jnp.zeros((windows, L + 2 * margin, D), F32)
    for tap_id in range(KS):
        before = tap_id * dilation
        total = total + jnp.pad(
            framed[:, :, tap_id], ((0, 0), (before, 2 * margin - before), (0, 0))
        )
    return total[:, margin : margin + L].reshape(windows * L, D)


def block_forward(stream, weights, dilation):
    conv_mat, inner_mat, outer_mat, vector = weights
    conv_bias = vector[:D]
    gain_conv = vector[D : 2 * D]
    gain_ffn = vector[2 * D : 3 * D]
    bias_ffn = vector[3 * D :]
    stream_low = stream.astype(BF)
    pre_conv = (
        jnp.dot(columns(stream_low, dilation), conv_mat, preferred_element_type=F32) + conv_bias
    )
    mixed = stream + gain_conv * conv_branch(pre_conv)
    mixed_low = mixed.astype(BF)
    pre_ffn = jnp.dot(mixed_low, inner_mat, preferred_element_type=F32) + bias_ffn
    hidden_low = jax.nn.gelu(pre_ffn).astype(BF)
    branch = jnp.dot(hidden_low, outer_mat, preferred_element_type=F32)
    result = mixed + gain_ffn * normalize(branch)
    return (result, (stream_low, pre_conv, mixed_low, pre_ffn, hidden_low, branch))


def block_backward(grad_out, saved, weights, dilation):
    conv_mat, inner_mat, outer_mat, vector = weights
    gain_conv = vector[D : 2 * D]
    gain_ffn = vector[2 * D : 3 * D]
    stream_low, pre_conv, mixed_low, pre_ffn, hidden_low, branch = saved
    normed_branch, branch_back = jax.vjp(normalize, branch)
    grad_gain_ffn = jnp.sum(grad_out * normed_branch, axis=0)
    grad_branch = branch_back(grad_out * gain_ffn)[0].astype(BF)
    grad_outer = contract_rows(hidden_low, grad_branch)
    grad_hidden = contract_cols(grad_branch, outer_mat)
    _, gelu_back = jax.vjp(jax.nn.gelu, pre_ffn)
    grad_pre_ffn = gelu_back(grad_hidden)[0].astype(BF)
    grad_bias_ffn = jnp.sum(grad_pre_ffn.astype(F32), axis=0)
    grad_inner = contract_rows(mixed_low, grad_pre_ffn)
    grad_mixed = grad_out + contract_cols(grad_pre_ffn, inner_mat)
    normed_conv, conv_back = jax.vjp(conv_branch, pre_conv)
    grad_gain_conv = jnp.sum(grad_mixed * normed_conv, axis=0)
    grad_pre_conv = conv_back(grad_mixed * gain_conv)[0].astype(BF)
    grad_conv_bias = jnp.sum(grad_pre_conv.astype(F32), axis=0)
    grad_kernel = contract_rows(columns(stream_low, dilation), grad_pre_conv)
    grad_stream = grad_mixed + fold_back(contract_cols(grad_pre_conv, conv_mat), dilation)
    vector_grad = jnp.concatenate([grad_conv_bias, grad_gain_conv, grad_gain_ffn, grad_bias_ffn])
    return (grad_stream, (grad_kernel, grad_inner, grad_outer, vector_grad))


def gather_any(conv_weight, inner_weight, outer_weight, vectors):
    def whole(member):
        return lax.all_gather(member, ("dp", "fsdp"), axis=1, tiled=True)

    conv, inner, outer, vector = (
        whole(member) for member in (conv_weight, inner_weight, outer_weight, vectors)
    )
    return [
        (
            conv[b].reshape(KS * D, D),
            inner[b].reshape(D, FF),
            outer[b].reshape(FF, D),
            vector[b].astype(F32),
        )
        for b in range(2)
    ]


def reduce_any(grads, width):
    count_dp = lax.axis_size("dp")
    count_fsdp = lax.axis_size("fsdp")

    def settle(first, second):
        member = jnp.stack([first.reshape(-1), second.reshape(-1)]).astype(BF)
        member = member.reshape(2, count_dp, count_fsdp, -1)
        spread = lax.all_to_all(member, "fsdp", split_axis=2, concat_axis=2, tiled=True)
        partial = jnp.sum(spread.astype(F32), axis=2, keepdims=True).astype(BF)
        settled = lax.all_to_all(partial, "dp", split_axis=1, concat_axis=1, tiled=True)
        return jnp.sum(settled.astype(F32), axis=(1, 2))

    return tuple(settle(first, second) for first, second in zip(*grads))


def body_here(embeddings, conv_weight, inner_weight, outer_weight, vectors, cotangent, row_mask):
    weights = (
        conv_weight.reshape(2, -1, D),
        inner_weight.reshape(2, -1, FF),
        outer_weight.reshape(2, -1, D),
    )
    mask = row_mask.reshape(ROWS // 128, 128)
    result = forward(vectors, cotangent, mask, weights, embeddings)
    weights, output, vec, incoming, kept = result[:6], result[6], result[7], result[8], result[9:]
    *grads, vec_grad, emb_grad = finish((output, *backward(weights, vec, incoming, kept)))
    output, *grads = grads
    conv, inner, outer = (member.transpose(1, 0, 2).reshape(2, -1) for member in grads)
    return output, emb_grad, conv, inner, outer, vec_grad


def body_any(embeddings, conv_weight, inner_weight, outer_weight, vectors, cotangent, row_mask):
    weights = gather_any(conv_weight, inner_weight, outer_weight, vectors)
    stream = embeddings.astype(F32)
    saved = []
    for b in range(2):
        stream, kept = block_forward(stream, weights[b], DILATIONS[b])
        saved.append(kept)
    output = stream.astype(BF)
    grad_stream = cotangent.astype(F32) * row_mask.astype(F32)[:, None]
    grads = [None, None]
    for b in (1, 0):
        grad_stream, grads[b] = block_backward(grad_stream, saved[b], weights[b], DILATIONS[b])
    return (output, grad_stream.astype(BF), *reduce_any(grads, vectors.shape[1]))


def solution(mesh):
    rows = P(("dp", "fsdp"), None)
    flat = P(None, ("dp", "fsdp"))
    here = mesh.shape["dp"] == NX and mesh.shape["fsdp"] == NZ * NY * 2
    return jax.shard_map(
        body_here if here else body_any,
        mesh=mesh,
        in_specs=(rows, flat, flat, flat, flat, rows, P(("dp", "fsdp"))),
        out_specs=(rows, rows, flat, flat, flat, flat),
        check_vma=False,
    )
```
